256 devices in a mesh: cache: 64 (over x, z, core), section: 4 (over y).
Axes of the slice: x: 4, y: 4, z: 8, core: 2. Of those that a mesh axis runs over, the one named last changes fastest.
Arguments:
- hidden: bfloat16 [16384, 4096], P('cache'), may hold values from -24 to 24
- norm_gain: bfloat16 [4, 4096], P('section'), may hold values from 0.5 to 1.5
- own_kv: bfloat16 [4, 16384, 2048], P('section', 'cache'), may hold values from -128 to 128
- passage_kv: bfloat16 [4, 1024, 32, 2048], P('section', 'cache'), may hold values from -6 to 6
- retrieval: int32 [256, 8], P('cache'), may hold values from 0 to 1023, as said below
- passage_slot: int32 [1024], replicated, may hold values from 0 to 1023, as said below
Outputs:
- layers_out: bfloat16 [4, 16384, 4096], P('section', 'cache')
The draws below stay inside these ranges and needn't reach their ends.
Inputs may be any that keep to these rules, and one draw needn't show every extreme that they name: `retrieval`: the 4 requests of index i of cache (requests i * 4 to (i + 1) * 4 - 1) name 32 different passages; at most 2 of them are stored on one index of cache (storage rows o * 16 to (o + 1) * 16 - 1 of passage_kv), exactly 2 on at least one. A permutation: passage p is row passage_slot[p] of passage_kv's second dimension.
All inputs are finite; a program needn't handle non-finite values.
Results may differ from the reference program's by a relative error of at most 0.0059.
Values may be sent and summed in bfloat16 or wider, within the bound.
A program may use at most 128 MiB of HBM per device.

```python
import jax
import jax.numpy as jnp
from jax import lax

D = 4096
HEADS = 32
KV_HEADS = 8
HEAD_DIM = 128
QT = 64
PT = 32
REQ_DEV = 4
PASS_DEV = 16
NRET = 8
LAYERS = 4
CAP = 2
REQUESTS = 256
TOKENS = 16384
PASSAGES = 1024
N_CACHE = 64


def storage_order(key):
    return jax.random.permutation(jax.random.fold_in(key, 101), PASSAGES).astype(jnp.int32)


def rows_base(key):
    return jnp.clip(jax.random.normal(jax.random.fold_in(key, 202), (TOKENS, D), jnp.float32), -6.0, 6.0)


def draw_passage_slot(key, part):
    order = storage_order(key)
    return jnp.argsort(order, stable=True).astype(jnp.int32)


def draw_retrieval(key, part):
    order = storage_order(key)
    key = jax.random.fold_in(key, 7)
    key_hot, key_pick, key_force, key_base, key_mix = jax.random.split(key, 5)
    cells = N_CACHE * CAP
    wanted = REQ_DEV * NRET
    weight = jax.random.randint(key_hot, (N_CACHE,), 0, 4)
    noise = jax.random.randint(key_pick, (N_CACHE, cells), 0, 2 ** 14)
    cell_ids = jnp.arange(cells, dtype=jnp.int32)
    owner_of = cell_ids // CAP
    forced = jax.random.randint(key_force, (N_CACHE,), 0, N_CACHE)
    hot_score = jnp.sum(jnp.where(owner_of[:, None] == jnp.arange(N_CACHE)[None, :], weight[None, :], 0), axis=1)
    score = noise + hot_score[None, :] * 2 ** 14 + jnp.where(owner_of[None, :] == forced[:, None], 2 ** 17, 0)
    score = (score * cells + cell_ids[None, :]).astype(jnp.int32)
    picked_score, picked = lax.top_k(score, wanted)
    owner = picked // CAP
    rank = picked % CAP
    base = jax.random.randint(key_base, (N_CACHE, N_CACHE), 0, PASS_DEV)
    local = (jnp.take_along_axis(base, owner, axis=1) + rank) % PASS_DEV
    stored = owner * PASS_DEV + local
    shuffle = jax.random.randint(key_mix, (N_CACHE, wanted), 0, 2 ** 20) * wanted + jnp.arange(wanted)[None, :]
    shuffle = jnp.argsort(shuffle, axis=1, stable=True)
    stored = jnp.take_along_axis(stored, shuffle, axis=1)
    return order[stored].reshape(N_CACHE * REQ_DEV, NRET).astype(jnp.int32)


def draw_hidden(key, part):
    base = rows_base(key)
    return base.astype(jnp.bfloat16)


def draw_own_kv(key, part):
    key = jax.random.fold_in(key, 5)
    key_kv = jax.random.fold_in(key, 0)
    width = KV_HEADS * HEAD_DIM
    pairs = jnp.clip(jax.random.normal(key_kv, (LAYERS, TOKENS, 2 * width), jnp.float32), -6.0, 6.0)
    return pairs.astype(jnp.bfloat16)


def level_of(own_key, shape, shards, low, top_value):
    level, own = 1.0, jax.random.fold_in(own_key, 6)
    for dim, shards_of in shards:
        steps = jnp.exp(jax.random.uniform(jax.random.fold_in(own, dim), (shards_of,), jnp.float32, low / len(shards), top_value / len(shards)))
        level = level * jnp.repeat(steps, shape[dim] // shards_of).reshape([-1 if axis == dim else 1 for axis in range(len(shape))])
    return level


def bell_draw(rng, extent, scale, bound, cuts=(), kind=jnp.bfloat16):
    result = scale * jax.random.normal(rng, extent, jnp.float32)
    if cuts:
        result = result * level_of(rng, extent, cuts, -0.22, 0.18)
    return jnp.clip(result, -bound, bound).astype(kind)


def setup_inputs(seed: int = 0) -> dict:
    key_of = jax.random.split(jax.random.key(seed), 7)
    return {
        "hidden": draw_hidden(jax.random.fold_in(key_of[6], 71), 0),
        "norm_gain": jnp.clip(1.0 + 0.1 * jax.random.normal(key_of[1], (LAYERS, D), jnp.float32), 0.5, 1.5).astype(jnp.bfloat16),
        "own_kv": draw_own_kv(jax.random.fold_in(key_of[6], 71), 0),
        "passage_kv": bell_draw(key_of[3], (LAYERS, PASSAGES, PT, 2 * KV_HEADS * HEAD_DIM), 1.0, 6.0, ((0, 4), (1, 64))),
        "retrieval": draw_retrieval(jax.random.fold_in(key_of[6], 71), 0),
        "passage_slot": draw_passage_slot(jax.random.fold_in(key_of[6], 71), 0),
    }


def attend_layer(rows_in, gain, passages, own, count):
    kv_width = KV_HEADS * HEAD_DIM
    group = HEADS // KV_HEADS
    wide = rows_in.astype(jnp.float32)
    mean_sq = lax.optimization_barrier(jnp.mean(wide * wide, axis=-1, keepdims=True))
    query = (wide * lax.rsqrt(mean_sq + 1e-05) * gain.astype(jnp.float32)).astype(jnp.bfloat16)
    query = query.reshape(count, QT, KV_HEADS, group, HEAD_DIM).astype(jnp.float32)
    far_keys = passages[..., :kv_width].reshape(count, NRET * PT, KV_HEADS, HEAD_DIM).astype(jnp.float32)
    far_vals = passages[..., kv_width:].reshape(count, NRET * PT, KV_HEADS, HEAD_DIM).astype(jnp.float32)
    own = own.reshape(count, QT, 2 * kv_width)
    near_keys = own[..., :kv_width].reshape(count, QT, KV_HEADS, HEAD_DIM).astype(jnp.float32)
    near_vals = own[..., kv_width:].reshape(count, QT, KV_HEADS, HEAD_DIM).astype(jnp.float32)
    scale = 1.0 / HEAD_DIM ** 0.5
    far = jnp.einsum('rqkgd,rpkd->rkgqp', query, far_keys) * scale
    near = jnp.einsum('rqkgd,rskd->rkgqs', query, near_keys) * scale
    causal = jnp.arange(QT)[:, None] >= jnp.arange(QT)[None, :]
    near = jnp.where(causal, near, -jnp.inf)
    top = jnp.maximum(lax.optimization_barrier(jnp.max(far, axis=-1)), lax.optimization_barrier(jnp.max(near, axis=-1)))[..., None]
    far_exp = jnp.exp(far - top)
    near_exp = jnp.exp(near - top)
    total = lax.optimization_barrier(jnp.sum(far_exp, axis=-1, keepdims=True)) + lax.optimization_barrier(jnp.sum(near_exp, axis=-1, keepdims=True))
    far_w = (far_exp / total).astype(jnp.bfloat16).astype(jnp.float32)
    near_w = (near_exp / total).astype(jnp.bfloat16).astype(jnp.float32)
    mixed = jnp.einsum('rkgqp,rpkd->rqkgd', far_w, far_vals) + jnp.einsum('rkgqs,rskd->rqkgd', near_w, near_vals)
    return (wide + mixed.reshape(count * QT, D)).astype(jnp.bfloat16)

def reference(hidden, norm_gain, own_kv, passage_kv, retrieval, passage_slot):
    rows = passage_slot[retrieval].astype(jnp.int32)
    state = hidden
    outputs = []
    for layer in range(LAYERS):
        store = passage_kv[layer]
        gain = norm_gain[layer]

        def one_request(items):
            state_r, rows_r, own_r = items
            passages = store[rows_r].reshape(1, NRET * PT, 2 * KV_HEADS * HEAD_DIM)
            return attend_layer(state_r, gain, passages, own_r, 1)
        state = lax.map(one_request, (state.reshape(REQUESTS, QT, D), rows, own_kv[layer].reshape(REQUESTS, QT, 2 * KV_HEADS * HEAD_DIM)))
        state = state.reshape(TOKENS, D)
        outputs.append(state)
    return jnp.stack(outputs)
```

```python
import functools

import jax
import jax.numpy as jnp
from jax import lax
from jax.experimental import pallas as pl
from jax.experimental.pallas import tpu as pltpu
from jax.sharding import PartitionSpec as P

D = 4096
QT = 64
PT = 32
NRET = 8
NX, NZ, NC, NY = 4, 8, 2, 4
PLANE = NX * NC
PASS_DEV = 16
REQ = 4
LAYERS = 4
CAP = 2
HALF = 256
PAIR = 512
WIDE = 1024
KEYS = 384
MESH = pl.DeviceIdType.MESH


def mod(a, n):
    return lax.rem(a + n, n)


def where_am_i():
    cache = lax.axis_index("cache")
    y = lax.axis_index("section")
    c = lax.rem(cache, NC)
    z = lax.rem(cache // NC, NZ)
    x = cache // (NC * NZ)
    return cache, x, y, z, c


def cache_at(x, z, c):
    return (x * NZ + z) * NC + c


def greet_kernel(rows_ref, gain_ref, rows_out, gain_out, rsend, rrecv, gsend, grecv):
    cache, x, y, z, c = where_am_i()
    me = x * NC + c

    def plane_id(i):
        t = lax.rem(me + i, PLANE)
        return (cache_at(t // NC, z, lax.rem(t, NC)), y)

    barrier = pltpu.get_barrier_semaphore()
    for i in range(1, PLANE):
        pl.semaphore_signal(barrier, inc=1, device_id=plane_id(i), device_id_type=MESH)
    for i in range(1, NY):
        pl.semaphore_signal(
            barrier, inc=1, device_id=(cache, lax.rem(y + i, NY)), device_id_type=MESH
        )
    pl.semaphore_wait(barrier, PLANE + NY - 2)
    rows_out[me] = rows_ref[...]
    gain_out[y] = gain_ref[...]
    copies = []
    for i in range(1, PLANE):
        copies.append(
            pltpu.make_async_remote_copy(
                src_ref=rows_ref,
                dst_ref=rows_out.at[me],
                send_sem=rsend.at[i],
                recv_sem=rrecv.at[i],
                device_id=plane_id(i),
                device_id_type=MESH,
            )
        )
    for i in range(1, NY):
        copies.append(
            pltpu.make_async_remote_copy(
                src_ref=gain_ref,
                dst_ref=gain_out.at[y],
                send_sem=gsend.at[i],
                recv_sem=grecv.at[i],
                device_id=(cache, lax.rem(y + i, NY)),
                device_id_type=MESH,
            )
        )
    for copy in copies:
        copy.start()
    for copy in copies:
        copy.wait()


def greet(rows, gain):
    vmem = pl.BlockSpec(memory_space=pltpu.VMEM)
    return pl.pallas_call(
        greet_kernel,
        out_shape=(
            jax.ShapeDtypeStruct((PLANE, 8, 128), jnp.int32),
            jax.ShapeDtypeStruct((NY, 32, 128), jnp.float32),
        ),
        in_specs=[vmem, vmem],
        out_specs=(vmem, vmem),
        scratch_shapes=[
            pltpu.SemaphoreType.DMA((PLANE,)),
            pltpu.SemaphoreType.DMA((PLANE,)),
            pltpu.SemaphoreType.DMA((NY,)),
            pltpu.SemaphoreType.DMA((NY,)),
        ],
        compiler_params=pltpu.CompilerParams(collective_id=0, has_side_effects=True),
        name="greet",
    )(rows, gain)


def main_kernel(
    store,
    own_in,
    hid,
    gain,
    sel,
    slots,
    out,
    pool,
    recv,
    send,
    rstage,
    stage,
    own,
    kv,
    state,
    rs,
    ssq,
    ysend,
    yrecv,
    osend,
    orecv,
    local,
    zsend,
    zrecv,
    xsend,
    xrecv,
    qsend,
    qrecv,
    outsend,
    outrecv,
    outlocal,
):
    cache, x, y, z, c = where_am_i()
    me = x * NC + c

    def plane_id(t):
        return (cache_at(t // NC, z, lax.rem(t, NC)), y)

    def z_id(dz):
        return (cache_at(x, mod(z + dz, NZ), c), y)

    def y_id(s):
        return (cache, s)

    def step_of(layer, s):
        return jnp.where(layer == s, 0, jnp.where(layer < s, layer + 1, layer))

    barrier = pltpu.get_barrier_semaphore()
    for i in range(1, PLANE):
        pl.semaphore_signal(
            barrier, inc=1, device_id=plane_id(lax.rem(me + i, PLANE)), device_id_type=MESH
        )
    for i in range(1, NY):
        pl.semaphore_signal(
            barrier, inc=1, device_id=y_id(lax.rem(y + i, NY)), device_id_type=MESH
        )
    for dz in (1, -1):
        pl.semaphore_signal(barrier, inc=1, device_id=z_id(dz), device_id_type=MESH)
    pl.semaphore_wait(barrier, PLANE + NY)

    def local_copies():
        made = []
        for part in range(2):
            cols = pl.ds(pl.multiple_of(part * 1024 + y * HALF, HALF), HALF)
            half = pl.ds(part * HALF, HALF)
            made.append(
                pltpu.make_async_copy(
                    store.at[:, :, cols], pool.at[0, z, :, :, half], local.at[part]
                )
            )
            made.append(
                pltpu.make_async_copy(
                    own_in.at[:, cols], own.at[y, :, half], local.at[2 + part]
                )
            )
        return made

    def scatter_copies(i):
        s = lax.rem(y + i, NY)
        made = []
        for part in range(2):
            cols = pl.ds(pl.multiple_of(part * 1024 + s * HALF, HALF), HALF)
            half = pl.ds(part * HALF, HALF)
            made.append(
                pltpu.make_async_remote_copy(
                    src_ref=store.at[:, :, cols],
                    dst_ref=pool.at[step_of(y, s), z, :, :, half],
                    send_sem=ysend.at[i, part],
                    recv_sem=yrecv.at[step_of(y, s), part],
                    device_id=y_id(s),
                    device_id_type=MESH,
                )
            )
            made.append(
                pltpu.make_async_remote_copy(
                    src_ref=own_in.at[:, cols],
                    dst_ref=own.at[y, :, half],
                    send_sem=osend.at[i, part],
                    recv_sem=orecv.at[y, part],
                    device_id=y_id(s),
                    device_id_type=MESH,
                )
            )
        return made

    for copy in local_copies():
        copy.start()
    for i in (1, 3, 2):
        for copy in scatter_copies(i):
            copy.start()

    def z_copy(k, up, half, hop):
        plane = mod(z - (hop - 1), NZ) if up else mod(z + (hop - 1), NZ)
        rows = pl.ds(half * 8, 8)
        where = pool.at[k, plane, rows]
        return pltpu.make_async_remote_copy(
            src_ref=where,
            dst_ref=where,
            send_sem=zsend.at[k, int(up), half, hop - 1],
            recv_sem=zrecv.at[k, int(up), half, hop - 1],
            device_id=z_id(1 if up else -1),
            device_id_type=MESH,
        )

    def z_arrival(k, up, half, hop):
        plane = mod(z - hop, NZ) if up else mod(z + hop, NZ)
        where = pool.at[k, plane, pl.ds(half * 8, 8)]
        return pltpu.make_async_remote_copy(
            src_ref=where,
            dst_ref=where,
            send_sem=zsend.at[k, int(up), half, hop - 1],
            recv_sem=zrecv.at[k, int(up), half, hop - 1],
            device_id=z_id(1 if up else -1),
            device_id_type=MESH,
        )

    def hops(up, half):
        return 4 if bool(up) == (half == 0) else 3

    def z_first(k):
        for half in range(2):
            for up in (True, False):
                z_copy(k, up, half, 1).start()

    def choose(k, plane):
        par = lax.rem(k, 2)
        stage[...] = pool[k, plane]

        def fill(t, _):
            for r in range(CAP):
                send[par, plane, t, r] = stage[sel[plane, t * CAP + r]]
            return 0

        lax.fori_loop(0, PLANE, fill, 0)
        recv[k, me, plane] = send[par, plane, me]

        def push(i, _):
            t = lax.rem(me + i, PLANE)
            pltpu.make_async_remote_copy(
                src_ref=send.at[par, plane, t],
                dst_ref=recv.at[k, me, plane],
                send_sem=xsend.at[k],
                recv_sem=xrecv.at[k],
                device_id=plane_id(t),
                device_id_type=MESH,
            ).start()
            return 0

        lax.fori_loop(1, PLANE, push, 0)

    def x_sent(k):
        what = send.at[lax.rem(k, 2), :, pl.ds(0, PLANE - 1)]
        pltpu.make_async_copy(what, what, xsend.at[k]).wait()

    def x_arrived(k):
        what = recv.at[k, pl.ds(0, PLANE - 1)]
        pltpu.make_async_copy(what, what, xrecv.at[k]).wait()

    def y_arrived(k):
        for part in range(2):
            what = pool.at[k, z, :, :, pl.ds(part * HALF, HALF)]
            pltpu.make_async_copy(what, what, yrecv.at[k, part]).wait()

    def attend(layer):
        k = step_of(layer, y)

        def lift(i, _):
            rstage[pl.ds(i * 16, 16)] = recv[k, i].reshape(16, PT, PAIR)
            return 0

        lax.fori_loop(0, PLANE, lift, 0)

        @pl.when(layer != y)
        def _():
            for part in range(2):
                what = own.at[layer, :, pl.ds(part * HALF, HALF)]
                pltpu.make_async_copy(what, what, orecv.at[layer, part]).wait()

        if layer > 0:
            what = ssq.at[layer - 1, pl.ds(0, NY - 1)]
            pltpu.make_async_copy(what, what, qrecv.at[layer - 1]).wait()
            total = ssq[layer - 1, 0] + ssq[layer - 1, 1] + ssq[layer - 1, 2] + ssq[layer - 1, 3]
            total = jnp.broadcast_to(total[0:1], (128, 256)).T
            rs[...] = lax.rsqrt(total * (1.0 / D) + 1e-05)

        row = lax.rem(lax.broadcasted_iota(jnp.int32, (4 * QT, KEYS), 0), QT)
        col = lax.broadcasted_iota(jnp.int32, (4 * QT, KEYS), 1)
        seen = (col < NRET * PT + 1 + row)

        def one(r, _):
            rows = pl.ds(pl.multiple_of(r * QT, QT), QT)
            for n in range(NRET):
                kv[n * PT : (n + 1) * PT] = rstage[slots[r * NRET + n]]
            kv[NRET * PT : NRET * PT + QT] = own[layer, rows]
            if layer == 0:
                before = hid[rows, pl.ds(pl.multiple_of(y * WIDE, WIDE), WIDE)]
            else:
                before = state[layer - 1, rows]
            wide = before.astype(jnp.float32)
            query = (wide * rs[rows, 0:1] * gain[layer : layer + 1, :]).astype(jnp.bfloat16)
            squares = jnp.zeros((QT, 128), jnp.float32)
            for j in range(2):
                heads = [4 * j + g for g in range(4)]
                qj = jnp.concatenate([query[:, h * 128 : (h + 1) * 128] for h in heads], axis=0)
                keys = kv[:, j * 128 : (j + 1) * 128]
                vals = kv[:, HALF + j * 128 : HALF + (j + 1) * 128]
                score = lax.dot_general(
                    qj, keys, (((1,), (1,)), ((), ())), preferred_element_type=jnp.float32
                )
                score = jnp.where(seen, score * (1.0 / 128**0.5), -jnp.inf)
                top = jnp.max(score, axis=-1, keepdims=True)
                expd = jnp.exp(score - top)
                total = jnp.sum(expd, axis=-1, keepdims=True)
                weight = (expd * (1.0 / total)).astype(jnp.bfloat16)
                mixed = jnp.dot(weight, vals, preferred_element_type=jnp.float32)
                for g, h in enumerate(heads):
                    new = wide[:, h * 128 : (h + 1) * 128] + mixed[g * QT : (g + 1) * QT]
                    new = new.astype(jnp.bfloat16)
                    state[layer, rows, h * 128 : (h + 1) * 128] = new
                    new = new.astype(jnp.float32)
                    squares = squares + new * new
            if layer < LAYERS - 1:
                squares = jnp.sum(squares, axis=-1, keepdims=True)
                rs[rows, :] = jnp.broadcast_to(squares, (QT, 128))
            cols = pl.ds(pl.multiple_of(y * WIDE, WIDE), WIDE)

            @pl.when(layer == y)
            def _():
                pltpu.make_async_copy(
                    state.at[layer, rows], out.at[rows, cols], outlocal
                ).start()

            @pl.when(layer != y)
            def _():
                pltpu.make_async_remote_copy(
                    src_ref=state.at[layer, rows],
                    dst_ref=out.at[rows, cols],
                    send_sem=outsend.at[layer],
                    recv_sem=outrecv,
                    device_id=y_id(layer),
                    device_id_type=MESH,
                ).start()

            return 0

        lax.fori_loop(0, REQ, one, 0)
        if layer < LAYERS - 1:
            ssq[layer, y] = rs[...].T[0:8]
            for i in range(1, NY):
                pltpu.make_async_remote_copy(
                    src_ref=ssq.at[layer, y],
                    dst_ref=ssq.at[layer, y],
                    send_sem=qsend.at[layer, i],
                    recv_sem=qrecv.at[layer],
                    device_id=y_id(lax.rem(y + i, NY)),
                    device_id_type=MESH,
                ).start()

    wide = hid[...].astype(jnp.float32)
    mean_sq = jnp.sum(wide * wide, axis=-1, keepdims=True) * (1.0 / D)
    rs[...] = jnp.broadcast_to(lax.rsqrt(mean_sq + 1e-05), (256, 128))
    kv[NRET * PT + QT :] = jnp.zeros((KEYS - NRET * PT - QT, PAIR), jnp.bfloat16)

    for copy in local_copies():
        copy.wait()
    z_first(0)

    def do_step(k):
        if k >= 2:
            x_sent(k - 2)
        choose(k, z)
        for hop in range(1, 5):
            for half in range(2):
                for up in (True, False):
                    if hop <= hops(up, half):
                        z_arrival(k, up, half, hop).wait_recv()
                        if hop < hops(up, half):
                            z_copy(k, up, half, hop + 1).start()
            if hop == 2 and k < LAYERS - 1:
                y_arrived(k + 1)
                z_first(k + 1)
            choose(k, mod(z - hop, NZ))
            if hop < 4:
                choose(k, mod(z + hop, NZ))
            if hop == 3 and k >= 2:
                if k == 2:
                    x_arrived(0)
                    x_arrived(1)
                    attend(0)
                else:
                    x_arrived(2)
                    attend(1)

    for k in range(LAYERS):
        do_step(k)
    x_arrived(3)
    attend(2)
    attend(3)

    x_sent(2)
    x_sent(3)
    for k in range(LAYERS):
        for up in (True, False):
            for half in range(2):
                for hop in range(1, hops(up, half) + 1):
                    z_copy(k, up, half, hop).wait_send()
    for i in range(1, NY):
        for copy in scatter_copies(i):
            copy.wait_send()
        for layer in range(LAYERS - 1):
            what = ssq.at[layer, y]
            pltpu.make_async_copy(what, what, qsend.at[layer, i]).wait()
    for layer in range(LAYERS):

        @pl.when(layer != y)
        def _():
            what = state.at[layer]
            pltpu.make_async_copy(what, what, outsend.at[layer]).wait()

    what = out.at[:, pl.ds(0, 3 * WIDE)]
    pltpu.make_async_copy(what, what, outrecv).wait()
    what = out.at[:, pl.ds(0, WIDE)]
    pltpu.make_async_copy(what, what, outlocal).wait()


def retrieve_and_attend(store, own, hidden, gain, sel, slots):
    vmem = pl.BlockSpec(memory_space=pltpu.VMEM)
    smem = pl.BlockSpec(memory_space=pltpu.SMEM)
    hbm = pl.BlockSpec(memory_space=pl.ANY)
    bf16 = jnp.bfloat16
    dma = pltpu.SemaphoreType.DMA
    return pl.pallas_call(
        main_kernel,
        out_shape=jax.ShapeDtypeStruct((REQ * QT, D), bf16),
        in_specs=[hbm, hbm, vmem, vmem, smem, smem],
        out_specs=hbm,
        scratch_shapes=[
            pltpu.VMEM((LAYERS, NZ, PASS_DEV, PT, PAIR), bf16),
            pltpu.VMEM((LAYERS, PLANE, NZ, CAP, PT, PAIR), bf16),
            pltpu.VMEM((2, NZ, PLANE, CAP, PT, PAIR), bf16),
            pltpu.VMEM((PLANE * NZ * CAP, PT, PAIR), bf16),
            pltpu.VMEM((PASS_DEV, PT, PAIR), bf16),
            pltpu.VMEM((LAYERS, REQ * QT, PAIR), bf16),
            pltpu.VMEM((KEYS, PAIR), bf16),
            pltpu.VMEM((LAYERS, REQ * QT, WIDE), bf16),
            pltpu.VMEM((REQ * QT, 128), jnp.float32),
            pltpu.VMEM((LAYERS - 1, NY, 8, REQ * QT), jnp.float32),
            dma((NY, 2)),
            dma((LAYERS, 2)),
            dma((NY, 2)),
            dma((LAYERS, 2)),
            dma((4,)),
            dma((LAYERS, 2, 2, 4)),
            dma((LAYERS, 2, 2, 4)),
            dma((LAYERS,)),
            dma((LAYERS,)),
            dma((LAYERS - 1, NY)),
            dma((LAYERS - 1,)),
            dma((LAYERS,)),
            dma(()),
            dma(()),
        ],
        compiler_params=pltpu.CompilerParams(
            collective_id=1, has_side_effects=True, vmem_limit_bytes=60 * 1024 * 1024
        ),
        name="retrieve_and_attend",
    )(store, own, hidden, gain, sel, slots)


def per_device(hidden, norm_gain, own_kv, passage_kv, retrieval, passage_slot):
    cache, x, y, z, c = where_am_i()
    me = x * NC + c
    wanted = retrieval.reshape(-1)
    ids = jnp.arange(passage_slot.shape[0], dtype=jnp.int32)
    mine = jnp.sum(jnp.where(wanted[:, None] == ids[None, :], passage_slot[None, :], 0), axis=1)
    packed = jnp.broadcast_to(jnp.pad(mine, (0, 96))[None, :], (8, 128))
    rows, gains = greet(packed, norm_gain.astype(jnp.float32).reshape(32, 128))
    rows = rows[:, 0, :32]
    gain = lax.dynamic_slice(gains, (0, y * 8, 0), (NY, 8, 128)).reshape(NY, WIDE)

    owner = rows // PASS_DEV
    inside = rows % PASS_DEV
    source = (owner // (NZ * NC)) * NC + owner % NC
    plane = (owner // NC) % NZ
    order = jnp.arange(32, dtype=jnp.int32)
    earlier = (owner[:, None, :] == owner[:, :, None]) & (order[None, None, :] < order[None, :, None])
    rank = jnp.sum(earlier.astype(jnp.int32), axis=2)
    place = jnp.where(source == me, plane * CAP + rank, -1)
    spots = jnp.arange(NZ * CAP, dtype=jnp.int32)
    sel = jnp.sum(
        jnp.where(place[:, None, :] == spots[None, :, None], inside[:, None, :], 0), axis=2
    )
    sel = sel.reshape(PLANE, NZ, CAP).transpose(1, 0, 2).reshape(NZ, PLANE * CAP)
    slot = (source * NZ + plane) * CAP + rank
    slots = lax.dynamic_slice(slot, (me, 0), (1, 32)).reshape(32)
    done = retrieve_and_attend(passage_kv[0], own_kv[0], hidden, gain, sel, slots)
    return done[None]


def solution(mesh):
    return jax.shard_map(
        per_device,
        mesh=mesh,
        in_specs=(
            P("cache", None),
            P("section", None),
            P("section", "cache", None),
            P("section", "cache", None, None),
            P("cache", None),
            P(),
        ),
        out_specs=P("section", "cache", None),
        check_vma=False,
    )
```

```python
import jax
import jax.numpy as jnp
import numpy as np
from jax import lax
from jax.experimental import pallas as pl
from jax.experimental.pallas import tpu as pltpu
from jax.sharding import PartitionSpec as P

D = 4096
QT = 64
PT = 32
NRET = 8
NX, NZ, NC, NY = 4, 8, 2, 4
PLANE = NX * NC
PASS_DEV = 16
REQ = 4
LAYERS = 4
CAP = 2
HALF = 256
PAIR = 512
WIDE = 1024
KEYS = 384
MESH = pl.DeviceIdType.MESH
STEPS = 2 * LAYERS
ONE = 256
CZ = 13
CX = 8
OWN = 64
KV_ROWS = NRET * PT + OWN


def mod(a, n):
    return lax.rem(a + n, n)


def where_am_i():
    cache = lax.axis_index("cache")
    y = lax.axis_index("section")
    c = lax.rem(cache, NC)
    z = lax.rem(cache // NC, NZ)
    x = cache // (NC * NZ)
    return cache, x, y, z, c


def cache_at(x, z, c):
    return (x * NZ + z) * NC + c


def greet_kernel(
    rows_ref, gain_ref, rows_out, gain_out, near, tile, psend, precv, zsend, zrecv, gsend, grecv
):
    cache, x, y, z, c = where_am_i()
    me = c * NX + x

    def plane_id(i):
        t = lax.rem(me + i, PLANE)
        return (cache_at(lax.rem(t, NX), z, t // NX), y)

    def z_id(i):
        return (cache_at(x, lax.rem(z + i, NZ), c), y)

    def y_id(i):
        return (cache, lax.rem(y + i, NY))

    barrier = pltpu.get_barrier_semaphore()
    for count, peer in ((PLANE, plane_id), (NZ, z_id), (NY, y_id)):
        for i in range(1, count):
            pl.semaphore_signal(barrier, inc=1, device_id=peer(i), device_id_type=MESH)
    pl.semaphore_wait(barrier, PLANE + NZ + NY - 3)
    first, second = [], []
    for i in range(1, PLANE):
        first.append(
            pltpu.make_async_remote_copy(
                src_ref=rows_ref,
                dst_ref=near.at[me],
                send_sem=psend.at[i],
                recv_sem=precv.at[i],
                device_id=plane_id(i),
                device_id_type=MESH,
            )
        )
    for i in range(1, NY):
        second.append(
            pltpu.make_async_remote_copy(
                src_ref=gain_ref,
                dst_ref=gain_out.at[y],
                send_sem=gsend.at[i],
                recv_sem=grecv.at[i],
                device_id=y_id(i),
                device_id_type=MESH,
            )
        )
    for copy in first + second:
        copy.start()
    near[me] = rows_ref[...]
    gain_out[y] = gain_ref[...]
    for copy in first:
        copy.wait()
    for t in range(PLANE):
        tile[t : t + 1, :] = near[t, 0:1, :]
    third = []
    for i in range(1, NZ):
        third.append(
            pltpu.make_async_remote_copy(
                src_ref=tile,
                dst_ref=rows_out.at[z],
                send_sem=zsend.at[i],
                recv_sem=zrecv.at[i],
                device_id=z_id(i),
                device_id_type=MESH,
            )
        )
    for copy in third:
        copy.start()
    rows_out[z] = tile[...]
    for copy in second + third:
        copy.wait()


def greet(rows, gain):
    vmem = pl.BlockSpec(memory_space=pltpu.VMEM)
    dma = pltpu.SemaphoreType.DMA
    return pl.pallas_call(
        greet_kernel,
        out_shape=(
            jax.ShapeDtypeStruct((NZ, PLANE, 128), jnp.int32),
            jax.ShapeDtypeStruct((NY, 32, 128), jnp.float32),
        ),
        in_specs=[vmem, vmem],
        out_specs=(vmem, vmem),
        scratch_shapes=[
            pltpu.VMEM((PLANE, 8, 128), jnp.int32),
            pltpu.VMEM((PLANE, 128), jnp.int32),
            dma((PLANE,)),
            dma((PLANE,)),
            dma((NZ,)),
            dma((NZ,)),
            dma((NY,)),
            dma((NY,)),
        ],
        compiler_params=pltpu.CompilerParams(collective_id=0, has_side_effects=True),
        name="greet",
    )(rows, gain)


def fast_kernel(
    store, own_in, hid, gain, csel, sel, slots, out, ybuf, send, kvs, own, state, staged, gains, rs,
    ssq, ysend, yrecv, osend, orecv, local, ssend, srecv, csend, crecv, zsend, zrecv, xsend, xrecv,
    qsend, qrecv, outsend, outrecv, outlocal, *many
):
    strips, pools, recvs = many[:STEPS], many[STEPS : 2 * STEPS], many[2 * STEPS :]
    cache, x, y, z, c = where_am_i()
    me = c * NX + x
    scale = 1.4426950408889634 / 128**0.5

    def plane_id(t):
        return (cache_at(lax.rem(t, NX), z, t // NX), y)

    def z_id(dz):
        return (cache_at(x, mod(z + dz, NZ), c), y)

    def y_id(s):
        return (cache, s)

    def step_of(i, s):
        return jnp.where(i == 2 * s, 0, jnp.where(i < 2 * s, i + 1, i))

    def part_of(q):
        return 2 * y if q == 0 else jnp.where(q - 1 < 2 * y, q - 1, q)

    barrier = pltpu.get_barrier_semaphore()
    for i in range(1, PLANE):
        pl.semaphore_signal(
            barrier, inc=1, device_id=plane_id(lax.rem(me + i, PLANE)), device_id_type=MESH
        )
    for i in range(1, NY):
        pl.semaphore_signal(
            barrier, inc=1, device_id=y_id(lax.rem(y + i, NY)), device_id_type=MESH
        )
    for dz in (1, -1):
        pl.semaphore_signal(barrier, inc=1, device_id=z_id(dz), device_id_type=MESH)
    pl.semaphore_wait(barrier, PLANE + NY)

    def local_copies():
        made = []
        for j in range(2):
            for part in range(2):
                cols = pl.ds(pl.multiple_of(part * 1024 + y * HALF + j * 128, 128), 128)
                made.append(
                    pltpu.make_async_copy(
                        store.at[:, :, :, cols],
                        ybuf.at[step_of(2 * y + j, y), :, :, :, pl.ds(part * 128, 128)],
                        local.at[2 * j + part],
                    )
                )
        for part in range(2):
            cols = pl.ds(pl.multiple_of(part * 1024 + y * HALF, HALF), HALF)
            made.append(
                pltpu.make_async_copy(
                    own_in.at[:, cols], own.at[y, :, pl.ds(part * HALF, HALF)], local.at[4 + part]
                )
            )
        return made

    def scatter_copies(i):
        s = lax.rem(y + i, NY)
        made = []
        for j in range(2):
            q = step_of(2 * y + j, s)
            for part in range(2):
                cols = pl.ds(pl.multiple_of(part * 1024 + s * HALF + j * 128, 128), 128)
                made.append(
                    pltpu.make_async_remote_copy(
                        src_ref=store.at[:, :, :, cols],
                        dst_ref=ybuf.at[q, :, :, :, pl.ds(part * 128, 128)],
                        send_sem=ysend.at[i, j, part],
                        recv_sem=yrecv.at[q, part],
                        device_id=y_id(s),
                        device_id_type=MESH,
                    )
                )
        for part in range(2):
            cols = pl.ds(pl.multiple_of(part * 1024 + s * HALF, HALF), HALF)
            made.append(
                pltpu.make_async_remote_copy(
                    src_ref=own_in.at[:, cols],
                    dst_ref=own.at[y, :, pl.ds(part * HALF, HALF)],
                    send_sem=osend.at[i, part],
                    recv_sem=orecv.at[y, part],
                    device_id=y_id(s),
                    device_id_type=MESH,
                )
            )
        return made

    def stripe(q):
        def push(i, _):
            t = lax.rem(me + i, PLANE)
            pltpu.make_async_remote_copy(
                src_ref=ybuf.at[q, :, mod(t - me, PLANE)],
                dst_ref=strips[q].at[pl.ds(me * 2, 2)],
                send_sem=ssend.at[q],
                recv_sem=srecv.at[q],
                device_id=plane_id(t),
                device_id_type=MESH,
            ).start()
            return 0

        strips[q][pl.ds(me * 2, 2)] = ybuf[q, :, 0]
        lax.fori_loop(1, PLANE, push, 0)

    def z_ref(q, plane, half):
        at = (c * NZ + plane) * CZ
        if half == 0:
            return pools[q].at[pl.ds(at, CZ - CZ // 2)]
        return pools[q].at[pl.ds(at + CZ - CZ // 2, CZ // 2)]

    def z_copy(q, up, half, hop):
        where = z_ref(q, mod(z - (hop - 1), NZ) if up else mod(z + (hop - 1), NZ), half)
        return pltpu.make_async_remote_copy(
            src_ref=where,
            dst_ref=where,
            send_sem=zsend.at[q, int(up), half, hop - 1],
            recv_sem=zrecv.at[q, int(up), half, hop - 1],
            device_id=z_id(1 if up else -1),
            device_id_type=MESH,
        )

    def z_arrival(q, up, half, hop):
        where = z_ref(q, mod(z - hop, NZ) if up else mod(z + hop, NZ), half)
        return pltpu.make_async_remote_copy(
            src_ref=where,
            dst_ref=where,
            send_sem=zsend.at[q, int(up), half, hop - 1],
            recv_sem=zrecv.at[q, int(up), half, hop - 1],
            device_id=z_id(1 if up else -1),
            device_id_type=MESH,
        )

    def hops(up, half):
        return 4 if bool(up) == (half == 0) else 3

    def share(where, q):
        pltpu.make_async_remote_copy(
            src_ref=where,
            dst_ref=where,
            send_sem=csend.at[q],
            recv_sem=crecv.at[q],
            device_id=(cache_at(x, z, 1 - c), y),
            device_id_type=MESH,
        ).start()

    def compact(q):
        what = strips[q].at[pl.ds(0, 2 * PLANE - 2)]
        pltpu.make_async_copy(what, what, srecv.at[q]).wait()
        for i in range(CZ):
            pools[q][(c * NZ + z) * CZ + i] = strips[q][csel[i]]
        for half in range(2):
            for up in (True, False):
                z_copy(q, up, half, 1).start()
        share(pools[q].at[pl.ds((c * NZ + z) * CZ, CZ)], q)

    def choose(q):
        par = q % 2
        what = pools[q].at[pl.ds((1 - c) * NZ * CZ, NZ * CZ)]
        pltpu.make_async_copy(what, what, crecv.at[q]).wait()
        if q >= 2:
            x_sent(q - 2)

        def fill(t, _):
            for i in range(CX):
                send[par, t, i] = pools[q][sel[t * CX + i]]
            return 0

        lax.fori_loop(0, PLANE, fill, 0)
        recvs[q][pl.ds(me * CX, CX)] = send[par, me]

        def push(i, _):
            t = lax.rem(me + i, PLANE)
            pltpu.make_async_remote_copy(
                src_ref=send.at[par, t],
                dst_ref=recvs[q].at[pl.ds(me * CX, CX)],
                send_sem=xsend.at[q],
                recv_sem=xrecv.at[q],
                device_id=plane_id(t),
                device_id_type=MESH,
            ).start()
            return 0

        lax.fori_loop(1, PLANE, push, 0)

    def x_sent(q):
        what = send.at[q % 2, pl.ds(0, PLANE - 1)]
        pltpu.make_async_copy(what, what, xsend.at[q]).wait()

    def assemble(q):
        what = recvs[q].at[pl.ds(0, (PLANE - 1) * CX)]
        pltpu.make_async_copy(what, what, xrecv.at[q]).wait()
        part = part_of(q)

        def one(r, _):
            for n in range(NRET):
                kvs[part, r, n * PT : (n + 1) * PT] = recvs[q][slots[r * NRET + n]]
            return 0

        lax.fori_loop(0, REQ, one, 0)

    def y_arrived(q):
        for part in range(2):
            what = ybuf.at[q, :, :, :, pl.ds(part * 128, 128)]
            pltpu.make_async_copy(what, what, yrecv.at[q, part]).wait()

    krow = lax.broadcasted_iota(jnp.int32, (OWN, 4 * QT), 0)
    qcol = lax.rem(lax.broadcasted_iota(jnp.int32, (OWN, 4 * QT), 1), QT)

    def before_layer(layer):
        @pl.when(layer != y)
        def _():
            for part in range(2):
                what = own.at[layer, :, pl.ds(part * HALF, HALF)]
                pltpu.make_async_copy(what, what, orecv.at[layer, part]).wait()

        if layer > 0:
            what = ssq.at[layer - 1, pl.ds(0, NY - 1)]
            pltpu.make_async_copy(what, what, qrecv.at[layer - 1]).wait()
            total = ssq[layer - 1, 0] + ssq[layer - 1, 1] + ssq[layer - 1, 2] + ssq[layer - 1, 3]
            total = total + pltpu.roll(total, QT, 1)
            total = total + pltpu.roll(total, 2 * QT, 1)
            rs[...] = lax.rsqrt(total * (1.0 / D) + 1e-05)

    def attend(layer, r):
        rows = slice(r * QT, (r + 1) * QT)
        causal = krow <= qcol
        squares = jnp.zeros((1, 4 * QT), jnp.float32)
        for j in range(2):
            part = 2 * layer + j
            wide = state[r, j].astype(jnp.float32)
            query = (wide * rs[r : r + 1, :] * gains[layer, j]).astype(jnp.bfloat16)
            far_keys = kvs[part, r, :, 0:128]
            far_vals = kvs[part, r, :, 128:256]
            near_keys = own[layer, rows, j * 128 : (j + 1) * 128]
            near_vals = own[layer, rows, HALF + j * 128 : HALF + (j + 1) * 128]
            far = jnp.dot(far_keys, query, preferred_element_type=jnp.float32)
            near = jnp.dot(near_keys, query, preferred_element_type=jnp.float32)
            near = jnp.where(causal, near, -jnp.inf)
            top = jnp.maximum(
                jnp.max(far, axis=0, keepdims=True), jnp.max(near, axis=0, keepdims=True)
            )
            far = jnp.exp2((far - top) * scale)
            near = jnp.exp2((near - top) * scale)
            total = jnp.sum(far, axis=0, keepdims=True) + jnp.sum(near, axis=0, keepdims=True)
            total = 1.0 / total
            far = (far * total).astype(jnp.bfloat16)
            near = (near * total).astype(jnp.bfloat16)
            first = (((0,), (0,)), ((), ()))
            mixed = lax.dot_general(far_vals, far, first, preferred_element_type=jnp.float32)
            mixed = mixed + lax.dot_general(
                near_vals, near, first, preferred_element_type=jnp.float32
            )
            new = (wide + mixed).astype(jnp.bfloat16)
            state[r, j] = new
            turned = new.T
            for g in range(4):
                h = 4 * j + g
                staged[layer, rows, h * 128 : (h + 1) * 128] = turned[g * QT : (g + 1) * QT]
            new = new.astype(jnp.float32)
            squares = squares + jnp.sum(new * new, axis=0, keepdims=True)
        if layer < LAYERS - 1:
            ssq[layer, y, r : r + 1, :] = squares
        cols = pl.ds(pl.multiple_of(y * WIDE, WIDE), WIDE)

        @pl.when(layer == y)
        def _():
            pltpu.make_async_copy(
                staged.at[layer, pl.ds(r * QT, QT)], out.at[pl.ds(r * QT, QT), cols], outlocal
            ).start()

        @pl.when(layer != y)
        def _():
            pltpu.make_async_remote_copy(
                src_ref=staged.at[layer, pl.ds(r * QT, QT)],
                dst_ref=out.at[pl.ds(r * QT, QT), cols],
                send_sem=outsend.at[layer],
                recv_sem=outrecv,
                device_id=y_id(layer),
                device_id_type=MESH,
            ).start()

        if layer < LAYERS - 1 and r == REQ - 1:
            for i in range(1, NY):
                pltpu.make_async_remote_copy(
                    src_ref=ssq.at[layer, y],
                    dst_ref=ssq.at[layer, y],
                    send_sem=qsend.at[layer, i],
                    recv_sem=qrecv.at[layer],
                    device_id=y_id(lax.rem(y + i, NY)),
                    device_id_type=MESH,
                ).start()

    own_copies = local_copies()
    for copy in own_copies:
        copy.start()
    for i in (1, 3, 2):
        for copy in scatter_copies(i):
            copy.start()
    own_copies[0].wait()
    own_copies[1].wait()
    stripe(0)
    for copy in own_copies[2:]:
        copy.wait()

    for layer in range(LAYERS - 1):
        ssq[layer, y] = jnp.zeros((8, 4 * QT), jnp.float32)
    mean_sq = jnp.zeros((REQ * QT, 1), jnp.float32)
    for i in range(8):
        wide = hid[:, i * 512 : (i + 1) * 512].astype(jnp.float32)
        mean_sq = mean_sq + jnp.sum(wide * wide, axis=-1, keepdims=True)
    mean_sq = jnp.broadcast_to(mean_sq * (1.0 / D), (REQ * QT, 128)).T
    mean_sq = lax.rsqrt(mean_sq + 1e-05)
    for r in range(REQ):
        part = mean_sq[0:1, r * QT : (r + 1) * QT]
        rs[r : r + 1, :] = jnp.concatenate([part] * 4, axis=1)
    rs[REQ:, :] = jnp.zeros((8 - REQ, 4 * QT), jnp.float32)
    for j in range(2):
        for r in range(REQ):
            heads = []
            for g in range(4):
                cols = pl.ds(pl.multiple_of(y * WIDE + (4 * j + g) * 128, 128), 128)
                heads.append(hid[r * QT : (r + 1) * QT, cols])
            state[r, j] = jnp.concatenate(heads, axis=0).T
        for layer in range(LAYERS):
            heads = []
            for g in range(4):
                at = gain[layer, pl.ds(y * 8 + 4 * j + g, 1), :]
                heads.append(jnp.broadcast_to(at, (QT, 128)))
            gains[layer, j] = jnp.concatenate(heads, axis=0).T

    def arrived_from_y(q):
        part = part_of(q)

        @pl.when(part != 2 * y + 1)
        def _():
            y_arrived(q)

    compact(0)
    arrived_from_y(1)
    stripe(1)
    todo = {}

    def later(slot, work):
        todo.setdefault(slot, []).append(work)

    for q in range(1, STEPS):
        if q >= 2:
            later(2 * q - 2, lambda q=q: (arrived_from_y(q), stripe(q)))
        later(2 * q - 1, lambda q=q: compact(q))
    for q in range(STEPS):
        later(2 * q + 4, lambda q=q: choose(q))
    for q in range(STEPS - 1):
        later(2 * q + 6, lambda q=q: assemble(q))
    for layer in range(2):
        later(4 * layer + 10, lambda layer=layer: before_layer(layer))
        for r in range(REQ):
            later(4 * layer + 10 + r, lambda layer=layer, r=r: attend(layer, r))

    for slot in range(2 * STEPS + 3):
        for q in range(STEPS):
            hop = slot - 2 * q + 1
            if not 1 <= hop <= 4:
                continue
            for half in range(2):
                for up in (True, False):
                    if hop <= hops(up, half):
                        z_arrival(q, up, half, hop).wait_recv()
                        if hop < hops(up, half):
                            z_copy(q, up, half, hop + 1).start()
                        plane = mod(z - hop, NZ) if up else mod(z + hop, NZ)
                        share(z_ref(q, plane, half), q)
        for work in todo.get(slot, ()):
            work()

    before_layer(2)
    for r in range(REQ):
        attend(2, r)
    assemble(STEPS - 1)
    before_layer(3)
    for r in range(REQ):
        attend(3, r)

    x_sent(STEPS - 2)
    x_sent(STEPS - 1)
    for q in range(STEPS):
        what = strips[q].at[pl.ds(0, 2 * PLANE - 2)]
        pltpu.make_async_copy(what, what, ssend.at[q]).wait()
        what = pools[q].at[pl.ds(c * NZ * CZ, NZ * CZ)]
        pltpu.make_async_copy(what, what, csend.at[q]).wait()
        for up in (True, False):
            for half in range(2):
                for hop in range(1, hops(up, half) + 1):
                    z_copy(q, up, half, hop).wait_send()
    for i in range(1, NY):
        for copy in scatter_copies(i):
            copy.wait_send()
        for layer in range(LAYERS - 1):
            what = ssq.at[layer, y]
            pltpu.make_async_copy(what, what, qsend.at[layer, i]).wait()
    for layer in range(LAYERS):

        @pl.when(layer != y)
        def _():
            what = staged.at[layer]
            pltpu.make_async_copy(what, what, outsend.at[layer]).wait()

    what = out.at[:, pl.ds(0, 3 * WIDE)]
    pltpu.make_async_copy(what, what, outrecv).wait()
    what = out.at[:, pl.ds(0, WIDE)]
    pltpu.make_async_copy(what, what, outlocal).wait()


def fast_attend(store, own, hidden, gain, csel, sel, slots):
    vmem = pl.BlockSpec(memory_space=pltpu.VMEM)
    smem = pl.BlockSpec(memory_space=pltpu.SMEM)
    hbm = pl.BlockSpec(memory_space=pl.ANY)
    bf16 = jnp.bfloat16
    dma = pltpu.SemaphoreType.DMA
    return pl.pallas_call(
        fast_kernel,
        out_shape=jax.ShapeDtypeStruct((REQ * QT, D), bf16),
        in_specs=[hbm, hbm, vmem, vmem, smem, smem, smem],
        out_specs=hbm,
        scratch_shapes=[
            pltpu.VMEM((STEPS, 2, PLANE, PT, ONE), bf16),
            pltpu.VMEM((2, PLANE, CX, PT, ONE), bf16),
            pltpu.VMEM((STEPS, REQ, NRET * PT, ONE), bf16),
            pltpu.VMEM((LAYERS, REQ * QT, PAIR), bf16),
            pltpu.VMEM((REQ, 2, 128, 4 * QT), bf16),
            pltpu.VMEM((LAYERS, REQ * QT, WIDE), bf16),
            pltpu.VMEM((LAYERS, 2, 128, 4 * QT), jnp.float32),
            pltpu.VMEM((8, 4 * QT), jnp.float32),
            pltpu.VMEM((LAYERS - 1, NY, 8, 4 * QT), jnp.float32),
            dma((NY, 2, 2)),
            dma((STEPS, 2)),
            dma((NY, 2)),
            dma((LAYERS, 2)),
            dma((6,)),
            dma((STEPS,)),
            dma((STEPS,)),
            dma((STEPS,)),
            dma((STEPS,)),
            dma((STEPS, 2, 2, 4)),
            dma((STEPS, 2, 2, 4)),
            dma((STEPS,)),
            dma((STEPS,)),
            dma((LAYERS - 1, NY)),
            dma((LAYERS - 1,)),
            dma((LAYERS,)),
            dma(()),
            dma(()),
        ]
        + [pltpu.VMEM((PLANE * 2, PT, ONE), bf16)] * STEPS
        + [pltpu.VMEM((NC * NZ * CZ, PT, ONE), bf16)] * STEPS
        + [pltpu.VMEM((PLANE * CX, PT, ONE), bf16)] * STEPS,
        compiler_params=pltpu.CompilerParams(
            collective_id=2, has_side_effects=True, vmem_limit_bytes=60 * 1024 * 1024
        ),
        name="fast_attend",
    )(store, own, hidden, gain, csel, sel, slots)


def general_kernel(
    store,
    own_in,
    hid,
    gain,
    sel,
    slots,
    out,
    pool,
    recv,
    send,
    rstage,
    stage,
    own,
    kv,
    state,
    rs,
    ssq,
    ysend,
    yrecv,
    osend,
    orecv,
    local,
    zsend,
    zrecv,
    xsend,
    xrecv,
    qsend,
    qrecv,
    outsend,
    outrecv,
    outlocal,
):
    cache, x, y, z, c = where_am_i()
    me = x * NC + c

    def plane_id(t):
        return (cache_at(t // NC, z, lax.rem(t, NC)), y)

    def z_id(dz):
        return (cache_at(x, mod(z + dz, NZ), c), y)

    def y_id(s):
        return (cache, s)

    def step_of(layer, s):
        return jnp.where(layer == s, 0, jnp.where(layer < s, layer + 1, layer))

    barrier = pltpu.get_barrier_semaphore()
    for i in range(1, PLANE):
        pl.semaphore_signal(
            barrier, inc=1, device_id=plane_id(lax.rem(me + i, PLANE)), device_id_type=MESH
        )
    for i in range(1, NY):
        pl.semaphore_signal(
            barrier, inc=1, device_id=y_id(lax.rem(y + i, NY)), device_id_type=MESH
        )
    for dz in (1, -1):
        pl.semaphore_signal(barrier, inc=1, device_id=z_id(dz), device_id_type=MESH)
    pl.semaphore_wait(barrier, PLANE + NY)

    def local_copies():
        made = []
        for part in range(2):
            cols = pl.ds(pl.multiple_of(part * 1024 + y * HALF, HALF), HALF)
            half = pl.ds(part * HALF, HALF)
            made.append(
                pltpu.make_async_copy(
                    store.at[:, :, cols], pool.at[0, z, :, :, half], local.at[part]
                )
            )
            made.append(
                pltpu.make_async_copy(
                    own_in.at[:, cols], own.at[y, :, half], local.at[2 + part]
                )
            )
        return made

    def scatter_copies(i):
        s = lax.rem(y + i, NY)
        made = []
        for part in range(2):
            cols = pl.ds(pl.multiple_of(part * 1024 + s * HALF, HALF), HALF)
            half = pl.ds(part * HALF, HALF)
            made.append(
                pltpu.make_async_remote_copy(
                    src_ref=store.at[:, :, cols],
                    dst_ref=pool.at[step_of(y, s), z, :, :, half],
                    send_sem=ysend.at[i, part],
                    recv_sem=yrecv.at[step_of(y, s), part],
                    device_id=y_id(s),
                    device_id_type=MESH,
                )
            )
            made.append(
                pltpu.make_async_remote_copy(
                    src_ref=own_in.at[:, cols],
                    dst_ref=own.at[y, :, half],
                    send_sem=osend.at[i, part],
                    recv_sem=orecv.at[y, part],
                    device_id=y_id(s),
                    device_id_type=MESH,
                )
            )
        return made

    for copy in local_copies():
        copy.start()
    for i in (1, 3, 2):
        for copy in scatter_copies(i):
            copy.start()

    def z_copy(k, up, half, hop):
        plane = mod(z - (hop - 1), NZ) if up else mod(z + (hop - 1), NZ)
        rows = pl.ds(half * 8, 8)
        where = pool.at[k, plane, rows]
        return pltpu.make_async_remote_copy(
            src_ref=where,
            dst_ref=where,
            send_sem=zsend.at[k, int(up), half, hop - 1],
            recv_sem=zrecv.at[k, int(up), half, hop - 1],
            device_id=z_id(1 if up else -1),
            device_id_type=MESH,
        )

    def z_arrival(k, up, half, hop):
        plane = mod(z - hop, NZ) if up else mod(z + hop, NZ)
        where = pool.at[k, plane, pl.ds(half * 8, 8)]
        return pltpu.make_async_remote_copy(
            src_ref=where,
            dst_ref=where,
            send_sem=zsend.at[k, int(up), half, hop - 1],
            recv_sem=zrecv.at[k, int(up), half, hop - 1],
            device_id=z_id(1 if up else -1),
            device_id_type=MESH,
        )

    def hops(up, half):
        return 4 if bool(up) == (half == 0) else 3

    def z_first(k):
        for half in range(2):
            for up in (True, False):
                z_copy(k, up, half, 1).start()

    def choose(k, plane):
        par = lax.rem(k, 2)
        stage[...] = pool[k, plane]

        def fill(t, _):
            for r in range(CAP):
                send[par, plane, t, r] = stage[sel[plane, t * CAP + r]]
            return 0

        lax.fori_loop(0, PLANE, fill, 0)
        recv[k, me, plane] = send[par, plane, me]

        def push(i, _):
            t = lax.rem(me + i, PLANE)
            pltpu.make_async_remote_copy(
                src_ref=send.at[par, plane, t],
                dst_ref=recv.at[k, me, plane],
                send_sem=xsend.at[k],
                recv_sem=xrecv.at[k],
                device_id=plane_id(t),
                device_id_type=MESH,
            ).start()
            return 0

        lax.fori_loop(1, PLANE, push, 0)

    def x_sent(k):
        what = send.at[lax.rem(k, 2), :, pl.ds(0, PLANE - 1)]
        pltpu.make_async_copy(what, what, xsend.at[k]).wait()

    def x_arrived(k):
        what = recv.at[k, pl.ds(0, PLANE - 1)]
        pltpu.make_async_copy(what, what, xrecv.at[k]).wait()

    def y_arrived(k):
        for part in range(2):
            what = pool.at[k, z, :, :, pl.ds(part * HALF, HALF)]
            pltpu.make_async_copy(what, what, yrecv.at[k, part]).wait()

    def attend(layer):
        k = step_of(layer, y)

        def lift(i, _):
            rstage[pl.ds(i * 16, 16)] = recv[k, i].reshape(16, PT, PAIR)
            return 0

        lax.fori_loop(0, PLANE, lift, 0)

        @pl.when(layer != y)
        def _():
            for part in range(2):
                what = own.at[layer, :, pl.ds(part * HALF, HALF)]
                pltpu.make_async_copy(what, what, orecv.at[layer, part]).wait()

        if layer > 0:
            what = ssq.at[layer - 1, pl.ds(0, NY - 1)]
            pltpu.make_async_copy(what, what, qrecv.at[layer - 1]).wait()
            total = ssq[layer - 1, 0] + ssq[layer - 1, 1] + ssq[layer - 1, 2] + ssq[layer - 1, 3]
            total = jnp.broadcast_to(total[0:1], (128, 256)).T
            rs[...] = lax.rsqrt(total * (1.0 / D) + 1e-05)

        row = lax.rem(lax.broadcasted_iota(jnp.int32, (4 * QT, KEYS), 0), QT)
        col = lax.broadcasted_iota(jnp.int32, (4 * QT, KEYS), 1)
        seen = (col < NRET * PT + 1 + row)

        def one(r, _):
            rows = pl.ds(pl.multiple_of(r * QT, QT), QT)
            for n in range(NRET):
                kv[n * PT : (n + 1) * PT] = rstage[slots[r * NRET + n]]
            kv[NRET * PT : NRET * PT + QT] = own[layer, rows]
            if layer == 0:
                before = hid[rows, pl.ds(pl.multiple_of(y * WIDE, WIDE), WIDE)]
            else:
                before = state[layer - 1, rows]
            wide = before.astype(jnp.float32)
            query = (wide * rs[rows, 0:1] * gain[layer : layer + 1, :]).astype(jnp.bfloat16)
            squares = jnp.zeros((QT, 128), jnp.float32)
            for j in range(2):
                heads = [4 * j + g for g in range(4)]
                qj = jnp.concatenate([query[:, h * 128 : (h + 1) * 128] for h in heads], axis=0)
                keys = kv[:, j * 128 : (j + 1) * 128]
                vals = kv[:, HALF + j * 128 : HALF + (j + 1) * 128]
                score = lax.dot_general(
                    qj, keys, (((1,), (1,)), ((), ())), preferred_element_type=jnp.float32
                )
                score = jnp.where(seen, score * (1.0 / 128**0.5), -jnp.inf)
                top = jnp.max(score, axis=-1, keepdims=True)
                expd = jnp.exp(score - top)
                total = jnp.sum(expd, axis=-1, keepdims=True)
                weight = (expd * (1.0 / total)).astype(jnp.bfloat16)
                mixed = jnp.dot(weight, vals, preferred_element_type=jnp.float32)
                for g, h in enumerate(heads):
                    new = wide[:, h * 128 : (h + 1) * 128] + mixed[g * QT : (g + 1) * QT]
                    new = new.astype(jnp.bfloat16)
                    state[layer, rows, h * 128 : (h + 1) * 128] = new
                    new = new.astype(jnp.float32)
                    squares = squares + new * new
            if layer < LAYERS - 1:
                squares = jnp.sum(squares, axis=-1, keepdims=True)
                rs[rows, :] = jnp.broadcast_to(squares, (QT, 128))
            cols = pl.ds(pl.multiple_of(y * WIDE, WIDE), WIDE)

            @pl.when(layer == y)
            def _():
                pltpu.make_async_copy(
                    state.at[layer, rows], out.at[rows, cols], outlocal
                ).start()

            @pl.when(layer != y)
            def _():
                pltpu.make_async_remote_copy(
                    src_ref=state.at[layer, rows],
                    dst_ref=out.at[rows, cols],
                    send_sem=outsend.at[layer],
                    recv_sem=outrecv,
                    device_id=y_id(layer),
                    device_id_type=MESH,
                ).start()

            return 0

        lax.fori_loop(0, REQ, one, 0)
        if layer < LAYERS - 1:
            ssq[layer, y] = rs[...].T[0:8]
            for i in range(1, NY):
                pltpu.make_async_remote_copy(
                    src_ref=ssq.at[layer, y],
                    dst_ref=ssq.at[layer, y],
                    send_sem=qsend.at[layer, i],
                    recv_sem=qrecv.at[layer],
                    device_id=y_id(lax.rem(y + i, NY)),
                    device_id_type=MESH,
                ).start()

    wide = hid[...].astype(jnp.float32)
    mean_sq = jnp.sum(wide * wide, axis=-1, keepdims=True) * (1.0 / D)
    rs[...] = jnp.broadcast_to(lax.rsqrt(mean_sq + 1e-05), (256, 128))
    kv[NRET * PT + QT :] = jnp.zeros((KEYS - NRET * PT - QT, PAIR), jnp.bfloat16)

    for copy in local_copies():
        copy.wait()
    z_first(0)

    def do_step(k):
        if k >= 2:
            x_sent(k - 2)
        choose(k, z)
        for hop in range(1, 5):
            for half in range(2):
                for up in (True, False):
                    if hop <= hops(up, half):
                        z_arrival(k, up, half, hop).wait_recv()
                        if hop < hops(up, half):
                            z_copy(k, up, half, hop + 1).start()
            if hop == 2 and k < LAYERS - 1:
                y_arrived(k + 1)
                z_first(k + 1)
            choose(k, mod(z - hop, NZ))
            if hop < 4:
                choose(k, mod(z + hop, NZ))
            if hop == 3 and k >= 2:
                if k == 2:
                    x_arrived(0)
                    x_arrived(1)
                    attend(0)
                else:
                    x_arrived(2)
                    attend(1)

    for k in range(LAYERS):
        do_step(k)
    x_arrived(3)
    attend(2)
    attend(3)

    x_sent(2)
    x_sent(3)
    for k in range(LAYERS):
        for up in (True, False):
            for half in range(2):
                for hop in range(1, hops(up, half) + 1):
                    z_copy(k, up, half, hop).wait_send()
    for i in range(1, NY):
        for copy in scatter_copies(i):
            copy.wait_send()
        for layer in range(LAYERS - 1):
            what = ssq.at[layer, y]
            pltpu.make_async_copy(what, what, qsend.at[layer, i]).wait()
    for layer in range(LAYERS):

        @pl.when(layer != y)
        def _():
            what = state.at[layer]
            pltpu.make_async_copy(what, what, outsend.at[layer]).wait()

    what = out.at[:, pl.ds(0, 3 * WIDE)]
    pltpu.make_async_copy(what, what, outrecv).wait()
    what = out.at[:, pl.ds(0, WIDE)]
    pltpu.make_async_copy(what, what, outlocal).wait()


def general_attend(store, own, hidden, gain, sel, slots):
    vmem = pl.BlockSpec(memory_space=pltpu.VMEM)
    smem = pl.BlockSpec(memory_space=pltpu.SMEM)
    hbm = pl.BlockSpec(memory_space=pl.ANY)
    bf16 = jnp.bfloat16
    dma = pltpu.SemaphoreType.DMA
    return pl.pallas_call(
        general_kernel,
        out_shape=jax.ShapeDtypeStruct((REQ * QT, D), bf16),
        in_specs=[hbm, hbm, vmem, vmem, smem, smem],
        out_specs=hbm,
        scratch_shapes=[
            pltpu.VMEM((LAYERS, NZ, PASS_DEV, PT, PAIR), bf16),
            pltpu.VMEM((LAYERS, PLANE, NZ, CAP, PT, PAIR), bf16),
            pltpu.VMEM((2, NZ, PLANE, CAP, PT, PAIR), bf16),
            pltpu.VMEM((PLANE * NZ * CAP, PT, PAIR), bf16),
            pltpu.VMEM((PASS_DEV, PT, PAIR), bf16),
            pltpu.VMEM((LAYERS, REQ * QT, PAIR), bf16),
            pltpu.VMEM((KEYS, PAIR), bf16),
            pltpu.VMEM((LAYERS, REQ * QT, WIDE), bf16),
            pltpu.VMEM((REQ * QT, 128), jnp.float32),
            pltpu.VMEM((LAYERS - 1, NY, 8, REQ * QT), jnp.float32),
            dma((NY, 2)),
            dma((LAYERS, 2)),
            dma((NY, 2)),
            dma((LAYERS, 2)),
            dma((4,)),
            dma((LAYERS, 2, 2, 4)),
            dma((LAYERS, 2, 2, 4)),
            dma((LAYERS,)),
            dma((LAYERS,)),
            dma((LAYERS - 1, NY)),
            dma((LAYERS - 1,)),
            dma((LAYERS,)),
            dma(()),
            dma(()),
        ],
        compiler_params=pltpu.CompilerParams(
            collective_id=1, has_side_effects=True, vmem_limit_bytes=60 * 1024 * 1024
        ),
        name="general_attend",
    )(store, own, hidden, gain, sel, slots)


def stored_order():
    z, t, s = np.meshgrid(np.arange(NZ), np.arange(PLANE), np.arange(PASS_DEV), indexing="ij")
    o8, b = s // 2, s % 2
    inside = (t - o8) % PLANE + PLANE * b
    owner = ((o8 % NX) * NZ + z) * NC + o8 // NX
    return (owner * PASS_DEV + inside).astype(np.int32)


def per_device(hidden, norm_gain, own_kv, passage_kv, retrieval, passage_slot):
    cache, x, y, z, c = where_am_i()
    me = c * NX + x
    wanted = retrieval.reshape(-1)
    ids = jnp.arange(passage_slot.shape[0], dtype=jnp.int32)
    mine = jnp.sum(jnp.where(wanted[:, None] == ids[None, :], passage_slot[None, :], 0), axis=1)
    packed = jnp.broadcast_to(jnp.pad(mine, (0, 96))[None, :], (8, 128))
    rows, gains = greet(packed, norm_gain.astype(jnp.float32).reshape(32, 128))
    rows = rows[:, :, :32]

    owner = rows // PASS_DEV
    inside = rows % PASS_DEV
    plane = (owner // NC) % NZ
    o8 = (owner % NC) * NX + owner // (NZ * NC)
    stripe = (inside + o8) % PLANE
    place = o8 * 2 + inside // PLANE
    chip = stripe % NX

    order = stored_order()
    need = jnp.any(rows.reshape(-1)[None, :] == order.reshape(-1)[:, None], axis=1)
    need = need.reshape(NZ, PLANE, PASS_DEV).astype(jnp.int32)
    below = np.tril(np.ones((PASS_DEV, PASS_DEV), np.int32), -1)
    before = jnp.sum(need[:, :, None, :] * below, axis=3)
    most_z = jnp.max(jnp.sum(need, axis=2))

    turn = jnp.arange(32, dtype=jnp.int32)
    earlier = (chip[..., None, :] == chip[..., :, None]) & (turn[None, :] < turn[:, None])
    rank = jnp.sum(earlier.astype(jnp.int32), axis=3)
    most_x = jnp.max(rank) + 1
    fits = (most_z <= CZ) & (most_x <= 2 * CX)

    def fast(store, own, hidden, gains):
        my_need = lax.dynamic_slice(need, (z, me, 0), (1, 1, PASS_DEV)).reshape(PASS_DEV)
        my_before = lax.dynamic_slice(before, (z, me, 0), (1, 1, PASS_DEV)).reshape(PASS_DEV)
        spots = jnp.arange(CZ, dtype=jnp.int32)
        hit = (my_before[None, :] == spots[:, None]) & (my_need[None, :] > 0)
        csel = jnp.sum(jnp.where(hit, jnp.arange(PASS_DEV, dtype=jnp.int32)[None, :], 0), axis=1)

        def here(value):
            return lax.dynamic_slice(value, (z, 0, 0), (1, PLANE, 32)).reshape(PLANE, 32)

        p, s, a, k, b = here(plane), here(stripe), here(place), here(rank), here(chip)
        number = (p * PLANE + s) * PASS_DEV + a
        hit = number[:, :, None] == jnp.arange(NZ * PLANE * PASS_DEV, dtype=jnp.int32)
        spot = jnp.sum(jnp.where(hit, before.reshape(-1), 0), axis=2)
        where = ((s // NX) * NZ + p) * CZ + spot
        mine = (b == x) & (k % NC == c)
        key = jnp.where(mine, k // NC, -1)
        hit = key[:, None, :] == jnp.arange(CX, dtype=jnp.int32)[None, :, None]
        sel = jnp.sum(jnp.where(hit, where[:, None, :], 0), axis=2).reshape(PLANE * CX)
        slot = ((k % NC) * NX + b) * CX + k // NC
        slots = lax.dynamic_slice(slot, (me, 0), (1, 32)).reshape(32)
        store = store.reshape(2, PASS_DEV // 2, PT, 4 * HALF * 2)
        return fast_attend(store, own, hidden, gains, csel, sel, slots)

    def general(store, own, hidden, gains):
        gain = lax.dynamic_slice(gains, (0, y * 8, 0), (NY, 8, 128)).reshape(NY, WIDE)
        near = lax.dynamic_slice(rows, (z, 0, 0), (1, PLANE, 32)).reshape(NC, NX, 32)
        near = near.transpose(1, 0, 2).reshape(PLANE, 32)
        mine = x * NC + c
        owner = near // PASS_DEV
        inside = near % PASS_DEV
        source = (owner // (NZ * NC)) * NC + owner % NC
        plane = (owner // NC) % NZ
        earlier = (owner[:, None, :] == owner[:, :, None]) & (turn[None, :] < turn[:, None])
        rank = jnp.sum(earlier.astype(jnp.int32), axis=2)
        place = jnp.where(source == mine, plane * CAP + rank, -1)
        spots = jnp.arange(NZ * CAP, dtype=jnp.int32)
        sel = jnp.sum(
            jnp.where(place[:, None, :] == spots[None, :, None], inside[:, None, :], 0), axis=2
        )
        sel = sel.reshape(PLANE, NZ, CAP).transpose(1, 0, 2).reshape(NZ, PLANE * CAP)
        slot = (source * NZ + plane) * CAP + rank
        slots = lax.dynamic_slice(slot, (mine, 0), (1, 32)).reshape(32)
        return general_attend(store, own, hidden, gain, sel, slots)

    done = lax.cond(fits, fast, general, passage_kv[0], own_kv[0], hidden, gains)
    return done[None]


def solution(mesh):
    return jax.shard_map(
        per_device,
        mesh=mesh,
        in_specs=(
            P("cache", None),
            P("section", None),
            P("section", "cache", None),
            P("section", "cache", None, None),
            P("cache", None),
            P(),
        ),
        out_specs=P("section", "cache", None),
        check_vma=False,
    )
```

```python
import functools

import jax
import jax.numpy as jnp
from jax import lax
from jax.experimental import pallas as pl
from jax.experimental.pallas import tpu as pltpu
from jax.sharding import PartitionSpec as P

D = 4096
QT = 64
PT = 32
NRET = 8
NX, NZ, NC, NY = 4, 8, 2, 4
PLANE = NX * NC
PASS_DEV = 16
REQ = 4
LAYERS = 4
CAP = 2
HALF = 256
PAIR = 512
WIDE = 1024
KEYS = 384
MESH = pl.DeviceIdType.MESH
STEPS = 2 * LAYERS
ONE = 256
CZS = (10, 12, 14)
CX = 8
OWN = 64
KV_ROWS = NRET * PT + OWN


def mod(a, n):
    return lax.rem(a + n, n)


def where_am_i():
    cache = lax.axis_index("cache")
    y = lax.axis_index("section")
    c = lax.rem(cache, NC)
    z = lax.rem(cache // NC, NZ)
    x = cache // (NC * NZ)
    return cache, x, y, z, c


def cache_at(x, z, c):
    return (x * NZ + z) * NC + c


def greet_kernel(
    ids_ref,
    slot_ref,
    gain_ref,
    rows_out,
    gain_out,
    tab_out,
    mine,
    near,
    tile,
    far,
    fields,
    psend,
    precv,
    zsend,
    zrecv,
    gsend,
    grecv,
):
    cache, x, y, z, c = where_am_i()
    me = c * NX + x
    f32, bf16, i32 = jnp.float32, jnp.bfloat16, jnp.int32

    def plane_id(i):
        t = lax.rem(me + i, PLANE)
        return (cache_at(lax.rem(t, NX), z, t // NX), y)

    def z_id(i):
        return (cache_at(x, lax.rem(z + i, NZ), c), y)

    def y_id(i):
        return (cache, lax.rem(y + i, NY))

    def lanes(shape):
        return lax.broadcasted_iota(i32, shape, len(shape) - 1)

    def subs(shape):
        return lax.broadcasted_iota(i32, shape, len(shape) - 2)

    def mm(a, b):
        return jnp.dot(a.astype(bf16), b.astype(bf16), preferred_element_type=f32)

    barrier = pltpu.get_barrier_semaphore()
    for count, peer in ((PLANE, plane_id), (NZ, z_id), (NY, y_id)):
        for i in range(1, count):
            pl.semaphore_signal(barrier, inc=1, device_id=peer(i), device_id_type=MESH)

    ids = ids_ref[0:1, :]
    hit = (jnp.broadcast_to(ids % 128, (128, 128)) == subs((128, 128))).astype(f32)
    high = mm((slot_ref[...] // 32).astype(f32), hit)
    low = mm((slot_ref[...] % 32).astype(f32), hit)
    pick = jnp.broadcast_to(ids // 128, (8, 128)) == subs((8, 128))
    found = jnp.sum(jnp.where(pick, high * 32.0 + low, 0.0), axis=0, keepdims=True)
    found = jnp.where(lanes((1, 128)) // 32 == lax.rem(me, 4), found, 0.0)
    mine[...] = jnp.broadcast_to(found, (8, 128)).astype(i32)
    for i in range(32):
        gain_out[y, i : i + 1, :] = gain_ref[:, i * 128 : (i + 1) * 128].astype(f32)

    pl.semaphore_wait(barrier, PLANE + NZ + NY - 3)
    first, second, third = [], [], []
    for i in range(1, PLANE):
        first.append(
            pltpu.make_async_remote_copy(
                src_ref=mine,
                dst_ref=near.at[me],
                send_sem=psend.at[i],
                recv_sem=precv.at[i],
                device_id=plane_id(i),
                device_id_type=MESH,
            )
        )
    for i in range(1, NY):
        second.append(
            pltpu.make_async_remote_copy(
                src_ref=gain_out.at[y],
                dst_ref=gain_out.at[y],
                send_sem=gsend.at[i],
                recv_sem=grecv.at[i],
                device_id=y_id(i),
                device_id_type=MESH,
            )
        )
    for copy in first + second:
        copy.start()
    near[me] = mine[...]
    for copy in first:
        copy.wait()
    row = subs((8, 128))
    tile[...] = jnp.where(row == 0, near[0] + near[1] + near[2] + near[3], 0) + jnp.where(
        row == 1, near[4] + near[5] + near[6] + near[7], 0
    )
    for i in range(1, NZ):
        third.append(
            pltpu.make_async_remote_copy(
                src_ref=tile,
                dst_ref=far.at[z],
                send_sem=zsend.at[i],
                recv_sem=zrecv.at[i],
                device_id=z_id(i),
                device_id_type=MESH,
            )
        )
    for copy in third:
        copy.start()
    far[z] = tile[...]
    for copy in third:
        copy.wait()
    for i in range(NZ):
        rows_out[2 * i : 2 * i + 2, :] = far[i, 0:2, :]

    rows = rows_out[...]
    owner = rows // PASS_DEV
    inside = rows % PASS_DEV
    plane = (owner // NC) % NZ
    o8 = (owner % NC) * NX + owner // (NZ * NC)
    stripe = (inside + o8) % PLANE
    place = o8 * 2 + inside // PLANE
    group = plane * PLANE + stripe
    chip = stripe % NX

    wide = (128, 128)
    same = (subs(wide) // 32 == lanes(wide) // 32) & (subs(wide) < lanes(wide))
    rank = jnp.zeros((2 * NZ, 128), f32)
    for v in range(NX):
        here = (chip == v).astype(f32)
        rank = rank + here * mm(here, same.astype(f32))
    rank = rank.astype(i32)
    fields[0] = group
    fields[1] = place
    fields[2] = chip
    fields[3] = rank

    groups = NZ * PLANE
    count = jnp.zeros((PASS_DEV, groups), f32)
    for i in range(2 * NZ):
        in_group = jnp.broadcast_to(group[i : i + 1], (groups, 128)) == subs((groups, 128))
        in_place = jnp.broadcast_to(place[i : i + 1], (PASS_DEV, 128)) == subs((PASS_DEV, 128))
        count = count + lax.dot_general(
            in_place.astype(f32).astype(bf16),
            in_group.astype(f32).astype(bf16),
            (((1,), (1,)), ((), ())),
            preferred_element_type=f32,
        )
    need = (count > 0.5).astype(f32)
    square = (PASS_DEV, PASS_DEV)
    before = mm((lanes(square) < subs(square)).astype(f32), need)

    def one_max(value):
        return jnp.max(jnp.max(value, axis=1, keepdims=True), axis=0, keepdims=True)

    most_z = one_max(jnp.sum(need, axis=0, keepdims=True)).astype(i32)
    most_x = one_max(rank) + 1

    ours = (lanes((PASS_DEV, groups)) == z * PLANE + me).astype(f32)
    my_need = jnp.sum(need * ours, axis=1, keepdims=True)
    my_before = jnp.sum(before * ours, axis=1, keepdims=True).astype(i32)
    hit = (my_before == lanes((PASS_DEV, 128))) & (my_need > 0.5)
    csel = jnp.sum(jnp.where(hit, subs((PASS_DEV, 128)), 0), axis=0, keepdims=True)
    tab_out[0:8, :] = jnp.broadcast_to(csel, (8, 128))

    block = (subs(wide) // 32 == lanes(wide)).astype(f32)
    for half in range(2):
        at = pl.ds(2 * z + half, 1)
        g, a, b, k = fields[0, at, :], fields[1, at, :], fields[2, at, :], fields[3, at, :]
        in_group = jnp.broadcast_to(g, (groups, 128)) == subs((groups, 128))
        in_place = jnp.broadcast_to(a, (PASS_DEV, 128)) == subs((PASS_DEV, 128))
        spot = mm(before, in_group.astype(f32)) * in_place.astype(f32)
        spot = jnp.sum(spot, axis=0, keepdims=True)
        core = (g % PLANE) // NX
        where = ((core * NZ + g // PLANE) * CZS[-1]).astype(f32) + jnp.minimum(spot, CZS[-1] - 1.0)
        key = jnp.where((b == x) & (k % NC == c), k // NC, -1)
        hit = jnp.broadcast_to(key, (CX, 128)) == subs((CX, 128))
        chosen = jnp.where(hit, jnp.broadcast_to(where, (CX, 128)), 0.0)
        tab_out[8 + 8 * half : 16 + 8 * half, :] = mm(chosen, block).astype(i32)
        slot = ((k % NC) * NX + b) * CX + jnp.minimum(k // NC, CX - 1)
        tab_out[24 + half : 25 + half, :] = slot
    tab_out[26:27, :] = jnp.broadcast_to(most_z, (1, 128))
    tab_out[27:28, :] = jnp.broadcast_to(most_x, (1, 128))
    tab_out[28:32, :] = jnp.zeros((4, 128), i32)
    for copy in second:
        copy.wait()


def greet(ids, slot, gain):
    vmem = pl.BlockSpec(memory_space=pltpu.VMEM)
    dma = pltpu.SemaphoreType.DMA
    return pl.pallas_call(
        greet_kernel,
        out_shape=(
            jax.ShapeDtypeStruct((2 * NZ, 128), jnp.int32),
            jax.ShapeDtypeStruct((NY, 32, 128), jnp.float32),
            jax.ShapeDtypeStruct((32, 128), jnp.int32),
        ),
        in_specs=[vmem, vmem, vmem],
        out_specs=(vmem, vmem, vmem),
        scratch_shapes=[
            pltpu.VMEM((8, 128), jnp.int32),
            pltpu.VMEM((PLANE, 8, 128), jnp.int32),
            pltpu.VMEM((8, 128), jnp.int32),
            pltpu.VMEM((NZ, 8, 128), jnp.int32),
            pltpu.VMEM((4, 2 * NZ, 128), jnp.int32),
            dma((PLANE,)),
            dma((PLANE,)),
            dma((NZ,)),
            dma((NZ,)),
            dma((NY,)),
            dma((NY,)),
        ],
        compiler_params=pltpu.CompilerParams(collective_id=0, has_side_effects=True),
        name="greet",
    )(ids, slot, gain)


def fast_kernel(
    cz, store, own_in, hid, gain, tab, out, ybuf, send, kvs, own, state, staged, gains, rs,
    ssq, box, packed, ysend, yrecv, osend, orecv, local, ssend, srecv, csend, crecv, zsend, zrecv, xsend, xrecv,
    qsend, qrecv, outsend, outrecv, outlocal, *many
):
    strips, pools, recvs = many[:STEPS], many[STEPS : 2 * STEPS], many[2 * STEPS :]
    cache, x, y, z, c = where_am_i()
    me = c * NX + x
    scale = 1.4426950408889634 / 128**0.5

    def plane_id(t):
        return (cache_at(lax.rem(t, NX), z, t // NX), y)

    def z_id(dz):
        return (cache_at(x, mod(z + dz, NZ), c), y)

    def y_id(s):
        return (cache, s)

    def step_of(i, s):
        return jnp.where(i == 2 * s, 0, jnp.where(i < 2 * s, i + 1, i))

    def part_of(q):
        return 2 * y if q == 0 else jnp.where(q - 1 < 2 * y, q - 1, q)

    barrier = pltpu.get_barrier_semaphore()
    for i in range(1, PLANE):
        pl.semaphore_signal(
            barrier, inc=1, device_id=plane_id(lax.rem(me + i, PLANE)), device_id_type=MESH
        )
    for i in range(1, NY):
        pl.semaphore_signal(
            barrier, inc=1, device_id=y_id(lax.rem(y + i, NY)), device_id_type=MESH
        )
    for dz in (1, -1):
        pl.semaphore_signal(barrier, inc=1, device_id=z_id(dz), device_id_type=MESH)
    pl.semaphore_wait(barrier, PLANE + NY)

    def local_copies():
        made = []
        for j in range(2):
            for part in range(2):
                cols = pl.ds(pl.multiple_of(part * 1024 + y * HALF + j * 128, 128), 128)
                made.append(
                    pltpu.make_async_copy(
                        store.at[:, :, :, cols],
                        ybuf.at[step_of(2 * y + j, y), :, :, :, pl.ds(part * 128, 128)],
                        local.at[2 * j + part],
                    )
                )
        for part in range(2):
            cols = pl.ds(pl.multiple_of(part * 1024 + y * HALF, HALF), HALF)
            made.append(
                pltpu.make_async_copy(
                    own_in.at[:, cols], own.at[y, :, pl.ds(part * HALF, HALF)], local.at[4 + part]
                )
            )
        return made

    def pack_copies(i, j):
        s = lax.rem(y + i, NY)
        made = []
        for part in range(2):
            cols = pl.ds(pl.multiple_of(part * 1024 + s * HALF + j * 128, 128), 128)
            made.append(
                pltpu.make_async_copy(
                    store.at[:, :, :, cols],
                    box.at[i - 1, j, :, :, :, pl.ds(part * 128, 128)],
                    packed.at[i, j, part],
                )
            )
        return made

    def scatter_copy(i, j):
        s = lax.rem(y + i, NY)
        q = step_of(2 * y + j, s)
        return pltpu.make_async_remote_copy(
            src_ref=box.at[i - 1, j],
            dst_ref=ybuf.at[q],
            send_sem=ysend.at[i, j],
            recv_sem=yrecv.at[q],
            device_id=y_id(s),
            device_id_type=MESH,
        )

    def own_scatter(i):
        s = lax.rem(y + i, NY)
        made = []
        for part in range(2):
            cols = pl.ds(pl.multiple_of(part * 1024 + s * HALF, HALF), HALF)
            made.append(
                pltpu.make_async_remote_copy(
                    src_ref=own_in.at[:, cols],
                    dst_ref=own.at[y, :, pl.ds(part * HALF, HALF)],
                    send_sem=osend.at[i, part],
                    recv_sem=orecv.at[y, part],
                    device_id=y_id(s),
                    device_id_type=MESH,
                )
            )
        return made

    def stripe(q):
        def push(i, _):
            t = lax.rem(me + i, PLANE)
            pltpu.make_async_remote_copy(
                src_ref=ybuf.at[q, :, mod(t - me, PLANE)],
                dst_ref=strips[q].at[pl.ds(me * 2, 2)],
                send_sem=ssend.at[q],
                recv_sem=srecv.at[q],
                device_id=plane_id(t),
                device_id_type=MESH,
            ).start()
            return 0

        strips[q][pl.ds(me * 2, 2)] = ybuf[q, :, 0]
        lax.fori_loop(1, PLANE, push, 0)

    def z_ref(q, plane, half):
        at = (c * NZ + plane) * CZS[-1]
        if half == 0:
            return pools[q].at[pl.ds(at, cz - cz // 2)]
        return pools[q].at[pl.ds(at + cz - cz // 2, cz // 2)]

    def z_copy(q, up, half, hop):
        where = z_ref(q, mod(z - (hop - 1), NZ) if up else mod(z + (hop - 1), NZ), half)
        return pltpu.make_async_remote_copy(
            src_ref=where,
            dst_ref=where,
            send_sem=zsend.at[q, int(up), half, hop - 1],
            recv_sem=zrecv.at[q, int(up), half, hop - 1],
            device_id=z_id(1 if up else -1),
            device_id_type=MESH,
        )

    def z_arrival(q, up, half, hop):
        where = z_ref(q, mod(z - hop, NZ) if up else mod(z + hop, NZ), half)
        return pltpu.make_async_remote_copy(
            src_ref=where,
            dst_ref=where,
            send_sem=zsend.at[q, int(up), half, hop - 1],
            recv_sem=zrecv.at[q, int(up), half, hop - 1],
            device_id=z_id(1 if up else -1),
            device_id_type=MESH,
        )

    def hops(up, half):
        return 4 if bool(up) == (half == 0) else 3

    def share(where, q):
        pltpu.make_async_remote_copy(
            src_ref=where,
            dst_ref=where,
            send_sem=csend.at[q],
            recv_sem=crecv.at[q],
            device_id=(cache_at(x, z, 1 - c), y),
            device_id_type=MESH,
        ).start()

    def compact(q):
        what = strips[q].at[pl.ds(0, 2 * PLANE - 2)]
        pltpu.make_async_copy(what, what, srecv.at[q]).wait()
        for i in range(cz):
            pools[q][(c * NZ + z) * CZS[-1] + i] = strips[q][tab[0, i]]
        for half in range(2):
            for up in (True, False):
                z_copy(q, up, half, 1).start()
        share(pools[q].at[pl.ds((c * NZ + z) * CZS[-1], cz)], q)

    def choose(q):
        par = q % 2
        what = pools[q].at[pl.ds(0, NZ * cz)]
        pltpu.make_async_copy(what, what, crecv.at[q]).wait()
        if q >= 2:
            x_sent(q - 2)

        def fill(t, _):
            for i in range(CX):
                send[par, t, i] = pools[q][tab[8 + 8 * (t // 4) + i, lax.rem(t, 4)]]
            return 0

        lax.fori_loop(0, PLANE, fill, 0)
        recvs[q][pl.ds(me * CX, CX)] = send[par, me]

        def push(i, _):
            t = lax.rem(me + i, PLANE)
            pltpu.make_async_remote_copy(
                src_ref=send.at[par, t],
                dst_ref=recvs[q].at[pl.ds(me * CX, CX)],
                send_sem=xsend.at[q],
                recv_sem=xrecv.at[q],
                device_id=plane_id(t),
                device_id_type=MESH,
            ).start()
            return 0

        lax.fori_loop(1, PLANE, push, 0)

    def x_sent(q):
        what = send.at[q % 2, pl.ds(0, PLANE - 1)]
        pltpu.make_async_copy(what, what, xsend.at[q]).wait()

    def assemble(q):
        what = recvs[q].at[pl.ds(0, (PLANE - 1) * CX)]
        pltpu.make_async_copy(what, what, xrecv.at[q]).wait()
        part = part_of(q)

        def one(r, _):
            for n in range(NRET):
                at = tab[24 + me // 4, lax.rem(me, 4) * 32 + r * NRET + n]
                kvs[part, r, n * PT : (n + 1) * PT] = recvs[q][at]
            return 0

        lax.fori_loop(0, REQ, one, 0)

    def y_arrived(q):
        what = ybuf.at[q]
        pltpu.make_async_copy(what, what, yrecv.at[q]).wait()

    krow = lax.broadcasted_iota(jnp.int32, (OWN, 4 * QT), 0)
    qcol = lax.rem(lax.broadcasted_iota(jnp.int32, (OWN, 4 * QT), 1), QT)

    def before_layer(layer):
        @pl.when(layer != y)
        def _():
            for part in range(2):
                what = own.at[layer, :, pl.ds(part * HALF, HALF)]
                pltpu.make_async_copy(what, what, orecv.at[layer, part]).wait()

        if layer > 0:
            what = ssq.at[layer - 1, pl.ds(0, NY - 1)]
            pltpu.make_async_copy(what, what, qrecv.at[layer - 1]).wait()
            total = ssq[layer - 1, 0] + ssq[layer - 1, 1] + ssq[layer - 1, 2] + ssq[layer - 1, 3]
            total = total + pltpu.roll(total, QT, 1)
            total = total + pltpu.roll(total, 2 * QT, 1)
            rs[...] = lax.rsqrt(total * (1.0 / D) + 1e-05)

    def attend(layer, r):
        rows = pl.ds(pl.multiple_of(r * QT, QT), QT)
        causal = krow <= qcol
        squares = jnp.zeros((1, 4 * QT), jnp.float32)
        for j in range(2):
            part = 2 * layer + j
            wide = state[r, j].astype(jnp.float32)
            query = (wide * rs[pl.ds(r, 1), :] * gains[layer, j]).astype(jnp.bfloat16)
            far_keys = kvs[part, r, :, 0:128]
            far_vals = kvs[part, r, :, 128:256]
            near_keys = own[layer, rows, j * 128 : (j + 1) * 128]
            near_vals = own[layer, rows, HALF + j * 128 : HALF + (j + 1) * 128]
            far = jnp.dot(far_keys, query, preferred_element_type=jnp.float32)
            near = jnp.dot(near_keys, query, preferred_element_type=jnp.float32)
            near = jnp.where(causal, near, -jnp.inf)
            top = jnp.maximum(
                jnp.max(far, axis=0, keepdims=True), jnp.max(near, axis=0, keepdims=True)
            )
            far = jnp.exp2((far - top) * scale)
            near = jnp.exp2((near - top) * scale)
            total = jnp.sum(far, axis=0, keepdims=True) + jnp.sum(near, axis=0, keepdims=True)
            total = 1.0 / total
            far = (far * total).astype(jnp.bfloat16)
            near = (near * total).astype(jnp.bfloat16)
            first = (((0,), (0,)), ((), ()))
            mixed = lax.dot_general(far_vals, far, first, preferred_element_type=jnp.float32)
            mixed = mixed + lax.dot_general(
                near_vals, near, first, preferred_element_type=jnp.float32
            )
            new = (wide + mixed).astype(jnp.bfloat16)
            state[r, j] = new
            turned = new.T
            for g in range(4):
                h = 4 * j + g
                staged[layer, rows, h * 128 : (h + 1) * 128] = turned[g * QT : (g + 1) * QT]
            new = new.astype(jnp.float32)
            squares = squares + jnp.sum(new * new, axis=0, keepdims=True)
        if layer < LAYERS - 1:
            ssq[layer, y, pl.ds(r, 1), :] = squares
        cols = pl.ds(pl.multiple_of(y * WIDE, WIDE), WIDE)

        @pl.when(layer == y)
        def _():
            pltpu.make_async_copy(
                staged.at[layer, rows], out.at[rows, cols], outlocal
            ).start()

        @pl.when(layer != y)
        def _():
            pltpu.make_async_remote_copy(
                src_ref=staged.at[layer, rows],
                dst_ref=out.at[rows, cols],
                send_sem=outsend.at[layer],
                recv_sem=outrecv,
                device_id=y_id(layer),
                device_id_type=MESH,
            ).start()

    def after_layer(layer):
        for i in range(1, NY):
            pltpu.make_async_remote_copy(
                src_ref=ssq.at[layer, y],
                dst_ref=ssq.at[layer, y],
                send_sem=qsend.at[layer, i],
                recv_sem=qrecv.at[layer],
                device_id=y_id(lax.rem(y + i, NY)),
                device_id_type=MESH,
            ).start()

    def attend_rows(layer, first, count, together):
        def body(i, _):
            for u in range(together):
                attend(layer, first + i * together + u)
            return 0

        lax.fori_loop(0, count // together, body, 0)

    own_copies = local_copies()
    for copy in own_copies[:2]:
        copy.start()
    packs = [(i, j, pack_copies(i, j)) for j in range(2) for i in (1, 3, 2)]
    for i, j, copies in packs[:3]:
        for copy in copies:
            copy.start()
    for copy in own_copies[2:]:
        copy.start()
    for i, j, copies in packs[3:]:
        for copy in copies:
            copy.start()
    own_copies[0].wait()
    own_copies[1].wait()
    stripe(0)
    for i, j, copies in packs:
        for copy in copies:
            copy.wait()
        scatter_copy(i, j).start()
    compact(0)
    for i in (1, 3, 2):
        for copy in own_scatter(i):
            copy.start()

    for layer in range(LAYERS - 1):
        ssq[layer, y] = jnp.zeros((8, 4 * QT), jnp.float32)
    mean_sq = jnp.zeros((REQ * QT, 1), jnp.float32)
    for i in range(8):
        wide = hid[:, i * 512 : (i + 1) * 512].astype(jnp.float32)
        mean_sq = mean_sq + jnp.sum(wide * wide, axis=-1, keepdims=True)
    mean_sq = jnp.broadcast_to(mean_sq * (1.0 / D), (REQ * QT, 128)).T
    mean_sq = lax.rsqrt(mean_sq + 1e-05)
    for r in range(REQ):
        part = mean_sq[0:1, r * QT : (r + 1) * QT]
        rs[r : r + 1, :] = jnp.concatenate([part] * 4, axis=1)
    rs[REQ:, :] = jnp.zeros((8 - REQ, 4 * QT), jnp.float32)
    for j in range(2):
        for r in range(REQ):
            heads = []
            for g in range(4):
                cols = pl.ds(pl.multiple_of(y * WIDE + (4 * j + g) * 128, 128), 128)
                heads.append(hid[r * QT : (r + 1) * QT, cols])
            state[r, j] = jnp.concatenate(heads, axis=0).T
        for layer in range(LAYERS):
            heads = []
            for g in range(4):
                at = gain[layer, pl.ds(y * 8 + 4 * j + g, 1), :]
                heads.append(jnp.broadcast_to(at, (QT, 128)))
            gains[layer, j] = jnp.concatenate(heads, axis=0).T

    def arrived_from_y(q):
        part = part_of(q)

        @pl.when(part != 2 * y + 1)
        def _():
            y_arrived(q)

    for copy in own_copies[2:]:
        copy.wait()
    arrived_from_y(1)
    stripe(1)
    todo = {}

    def later(slot, work):
        todo.setdefault(slot, []).append(work)

    for q in range(1, STEPS):
        if q >= 2:
            later(2 * q - 2, lambda q=q: (arrived_from_y(q), stripe(q)))
        later(2 * q - 1, lambda q=q: compact(q))
    for q in range(STEPS):
        later(2 * q + 4, lambda q=q: choose(q))
    for q in range(STEPS - 1):
        later(2 * q + 6, lambda q=q: assemble(q))
    for layer in range(2):
        later(4 * layer + 10, lambda layer=layer: before_layer(layer))
        for half in range(2):
            later(
                4 * layer + 10 + 2 * half,
                lambda layer=layer, half=half: attend_rows(layer, 2 * half, 2, 1),
            )
        later(4 * layer + 12, lambda layer=layer: after_layer(layer))

    for slot in range(2 * STEPS + 3):
        for q in range(STEPS):
            hop = slot - 2 * q + 1
            if not 1 <= hop <= 4:
                continue
            for half in range(2):
                for up in (True, False):
                    if hop <= hops(up, half):
                        z_arrival(q, up, half, hop).wait_recv()
                        if hop < hops(up, half):
                            z_copy(q, up, half, hop + 1).start()
                        plane = mod(z - hop, NZ) if up else mod(z + hop, NZ)
                        share(z_ref(q, plane, half), q)
        for work in todo.get(slot, ()):
            work()

    before_layer(2)
    attend_rows(2, 0, REQ, 2)
    after_layer(2)
    assemble(STEPS - 1)
    before_layer(3)
    attend_rows(3, 0, REQ, 2)

    x_sent(STEPS - 2)
    x_sent(STEPS - 1)
    for q in range(STEPS):
        what = strips[q].at[pl.ds(0, 2 * PLANE - 2)]
        pltpu.make_async_copy(what, what, ssend.at[q]).wait()
        what = pools[q].at[pl.ds(0, NZ * cz)]
        pltpu.make_async_copy(what, what, csend.at[q]).wait()
        for up in (True, False):
            for half in range(2):
                for hop in range(1, hops(up, half) + 1):
                    z_copy(q, up, half, hop).wait_send()
    for i in range(1, NY):
        for j in range(2):
            scatter_copy(i, j).wait_send()
        for copy in own_scatter(i):
            copy.wait_send()
        for layer in range(LAYERS - 1):
            what = ssq.at[layer, y]
            pltpu.make_async_copy(what, what, qsend.at[layer, i]).wait()
    for layer in range(LAYERS):

        @pl.when(layer != y)
        def _():
            what = staged.at[layer]
            pltpu.make_async_copy(what, what, outsend.at[layer]).wait()

    what = out.at[:, pl.ds(0, 3 * WIDE)]
    pltpu.make_async_copy(what, what, outrecv).wait()
    what = out.at[:, pl.ds(0, WIDE)]
    pltpu.make_async_copy(what, what, outlocal).wait()


def fast_attend(cz, collective_id, store, own, hidden, gain, tab):
    vmem = pl.BlockSpec(memory_space=pltpu.VMEM)
    smem = pl.BlockSpec(memory_space=pltpu.SMEM)
    hbm = pl.BlockSpec(memory_space=pl.ANY)
    bf16 = jnp.bfloat16
    dma = pltpu.SemaphoreType.DMA
    return pl.pallas_call(
        functools.partial(fast_kernel, cz),
        out_shape=jax.ShapeDtypeStruct((REQ * QT, D), bf16),
        in_specs=[hbm, hbm, vmem, vmem, smem],
        out_specs=hbm,
        scratch_shapes=[
            pltpu.VMEM((STEPS, 2, PLANE, PT, ONE), bf16),
            pltpu.VMEM((2, PLANE, CX, PT, ONE), bf16),
            pltpu.VMEM((STEPS, REQ, NRET * PT, ONE), bf16),
            pltpu.VMEM((LAYERS, REQ * QT, PAIR), bf16),
            pltpu.VMEM((REQ, 2, 128, 4 * QT), bf16),
            pltpu.VMEM((LAYERS, REQ * QT, WIDE), bf16),
            pltpu.VMEM((LAYERS, 2, 128, 4 * QT), jnp.float32),
            pltpu.VMEM((8, 4 * QT), jnp.float32),
            pltpu.VMEM((LAYERS - 1, NY, 8, 4 * QT), jnp.float32),
            pltpu.VMEM((NY - 1, 2, 2, PLANE, PT, ONE), bf16),
            dma((NY, 2, 2)),
            dma((NY, 2)),
            dma((STEPS,)),
            dma((NY, 2)),
            dma((LAYERS, 2)),
            dma((6,)),
            dma((STEPS,)),
            dma((STEPS,)),
            dma((STEPS,)),
            dma((STEPS,)),
            dma((STEPS, 2, 2, 4)),
            dma((STEPS, 2, 2, 4)),
            dma((STEPS,)),
            dma((STEPS,)),
            dma((LAYERS - 1, NY)),
            dma((LAYERS - 1,)),
            dma((LAYERS,)),
            dma(()),
            dma(()),
        ]
        + [pltpu.VMEM((PLANE * 2, PT, ONE), bf16)] * STEPS
        + [pltpu.VMEM((NC * NZ * CZS[-1], PT, ONE), bf16)] * STEPS
        + [pltpu.VMEM((PLANE * CX, PT, ONE), bf16)] * STEPS,
        compiler_params=pltpu.CompilerParams(
            collective_id=collective_id, has_side_effects=True, vmem_limit_bytes=60 * 1024 * 1024
        ),
        name="fast_attend_" + str(cz),
    )(store, own, hidden, gain, tab)


def general_kernel(
    store,
    own_in,
    hid,
    gain,
    sel,
    slots,
    out,
    pool,
    recv,
    send,
    rstage,
    stage,
    own,
    kv,
    state,
    rs,
    ssq,
    ysend,
    yrecv,
    osend,
    orecv,
    local,
    zsend,
    zrecv,
    xsend,
    xrecv,
    qsend,
    qrecv,
    outsend,
    outrecv,
    outlocal,
):
    cache, x, y, z, c = where_am_i()
    me = x * NC + c

    def plane_id(t):
        return (cache_at(t // NC, z, lax.rem(t, NC)), y)

    def z_id(dz):
        return (cache_at(x, mod(z + dz, NZ), c), y)

    def y_id(s):
        return (cache, s)

    def step_of(layer, s):
        return jnp.where(layer == s, 0, jnp.where(layer < s, layer + 1, layer))

    barrier = pltpu.get_barrier_semaphore()
    for i in range(1, PLANE):
        pl.semaphore_signal(
            barrier, inc=1, device_id=plane_id(lax.rem(me + i, PLANE)), device_id_type=MESH
        )
    for i in range(1, NY):
        pl.semaphore_signal(
            barrier, inc=1, device_id=y_id(lax.rem(y + i, NY)), device_id_type=MESH
        )
    for dz in (1, -1):
        pl.semaphore_signal(barrier, inc=1, device_id=z_id(dz), device_id_type=MESH)
    pl.semaphore_wait(barrier, PLANE + NY)

    def local_copies():
        made = []
        for part in range(2):
            cols = pl.ds(pl.multiple_of(part * 1024 + y * HALF, HALF), HALF)
            half = pl.ds(part * HALF, HALF)
            made.append(
                pltpu.make_async_copy(
                    store.at[:, :, cols], pool.at[0, z, :, :, half], local.at[part]
                )
            )
            made.append(
                pltpu.make_async_copy(
                    own_in.at[:, cols], own.at[y, :, half], local.at[2 + part]
                )
            )
        return made

    def scatter_copies(i):
        s = lax.rem(y + i, NY)
        made = []
        for part in range(2):
            cols = pl.ds(pl.multiple_of(part * 1024 + s * HALF, HALF), HALF)
            half = pl.ds(part * HALF, HALF)
            made.append(
                pltpu.make_async_remote_copy(
                    src_ref=store.at[:, :, cols],
                    dst_ref=pool.at[step_of(y, s), z, :, :, half],
                    send_sem=ysend.at[i, part],
                    recv_sem=yrecv.at[step_of(y, s), part],
                    device_id=y_id(s),
                    device_id_type=MESH,
                )
            )
            made.append(
                pltpu.make_async_remote_copy(
                    src_ref=own_in.at[:, cols],
                    dst_ref=own.at[y, :, half],
                    send_sem=osend.at[i, part],
                    recv_sem=orecv.at[y, part],
                    device_id=y_id(s),
                    device_id_type=MESH,
                )
            )
        return made

    for copy in local_copies():
        copy.start()
    for i in (1, 3, 2):
        for copy in scatter_copies(i):
            copy.start()

    def z_copy(k, up, half, hop):
        plane = mod(z - (hop - 1), NZ) if up else mod(z + (hop - 1), NZ)
        rows = pl.ds(half * 8, 8)
        where = pool.at[k, plane, rows]
        return pltpu.make_async_remote_copy(
            src_ref=where,
            dst_ref=where,
            send_sem=zsend.at[k, int(up), half, hop - 1],
            recv_sem=zrecv.at[k, int(up), half, hop - 1],
            device_id=z_id(1 if up else -1),
            device_id_type=MESH,
        )

    def z_arrival(k, up, half, hop):
        plane = mod(z - hop, NZ) if up else mod(z + hop, NZ)
        where = pool.at[k, plane, pl.ds(half * 8, 8)]
        return pltpu.make_async_remote_copy(
            src_ref=where,
            dst_ref=where,
            send_sem=zsend.at[k, int(up), half, hop - 1],
            recv_sem=zrecv.at[k, int(up), half, hop - 1],
            device_id=z_id(1 if up else -1),
            device_id_type=MESH,
        )

    def hops(up, half):
        return 4 if bool(up) == (half == 0) else 3

    def z_first(k):
        for half in range(2):
            for up in (True, False):
                z_copy(k, up, half, 1).start()

    def choose(k, plane):
        par = lax.rem(k, 2)
        stage[...] = pool[k, plane]

        def fill(t, _):
            for r in range(CAP):
                send[par, plane, t, r] = stage[sel[plane, t * CAP + r]]
            return 0

        lax.fori_loop(0, PLANE, fill, 0)
        recv[k, me, plane] = send[par, plane, me]

        def push(i, _):
            t = lax.rem(me + i, PLANE)
            pltpu.make_async_remote_copy(
                src_ref=send.at[par, plane, t],
                dst_ref=recv.at[k, me, plane],
                send_sem=xsend.at[k],
                recv_sem=xrecv.at[k],
                device_id=plane_id(t),
                device_id_type=MESH,
            ).start()
            return 0

        lax.fori_loop(1, PLANE, push, 0)

    def x_sent(k):
        what = send.at[lax.rem(k, 2), :, pl.ds(0, PLANE - 1)]
        pltpu.make_async_copy(what, what, xsend.at[k]).wait()

    def x_arrived(k):
        what = recv.at[k, pl.ds(0, PLANE - 1)]
        pltpu.make_async_copy(what, what, xrecv.at[k]).wait()

    def y_arrived(k):
        for part in range(2):
            what = pool.at[k, z, :, :, pl.ds(part * HALF, HALF)]
            pltpu.make_async_copy(what, what, yrecv.at[k, part]).wait()

    def attend(layer):
        k = step_of(layer, y)

        def lift(i, _):
            rstage[pl.ds(i * 16, 16)] = recv[k, i].reshape(16, PT, PAIR)
            return 0

        lax.fori_loop(0, PLANE, lift, 0)

        @pl.when(layer != y)
        def _():
            for part in range(2):
                what = own.at[layer, :, pl.ds(part * HALF, HALF)]
                pltpu.make_async_copy(what, what, orecv.at[layer, part]).wait()

        if layer > 0:
            what = ssq.at[layer - 1, pl.ds(0, NY - 1)]
            pltpu.make_async_copy(what, what, qrecv.at[layer - 1]).wait()
            total = ssq[layer - 1, 0] + ssq[layer - 1, 1] + ssq[layer - 1, 2] + ssq[layer - 1, 3]
            total = jnp.broadcast_to(total[0:1], (128, 256)).T
            rs[...] = lax.rsqrt(total * (1.0 / D) + 1e-05)

        row = lax.rem(lax.broadcasted_iota(jnp.int32, (4 * QT, KEYS), 0), QT)
        col = lax.broadcasted_iota(jnp.int32, (4 * QT, KEYS), 1)
        seen = (col < NRET * PT + 1 + row)

        def one(r, _):
            rows = pl.ds(pl.multiple_of(r * QT, QT), QT)
            for n in range(NRET):
                kv[n * PT : (n + 1) * PT] = rstage[slots[r * NRET + n]]
            kv[NRET * PT : NRET * PT + QT] = own[layer, rows]
            if layer == 0:
                before = hid[rows, pl.ds(pl.multiple_of(y * WIDE, WIDE), WIDE)]
            else:
                before = state[layer - 1, rows]
            wide = before.astype(jnp.float32)
            query = (wide * rs[rows, 0:1] * gain[layer : layer + 1, :]).astype(jnp.bfloat16)
            squares = jnp.zeros((QT, 128), jnp.float32)
            for j in range(2):
                heads = [4 * j + g for g in range(4)]
                qj = jnp.concatenate([query[:, h * 128 : (h + 1) * 128] for h in heads], axis=0)
                keys = kv[:, j * 128 : (j + 1) * 128]
                vals = kv[:, HALF + j * 128 : HALF + (j + 1) * 128]
                score = lax.dot_general(
                    qj, keys, (((1,), (1,)), ((), ())), preferred_element_type=jnp.float32
                )
                score = jnp.where(seen, score * (1.0 / 128**0.5), -jnp.inf)
                top = jnp.max(score, axis=-1, keepdims=True)
                expd = jnp.exp(score - top)
                total = jnp.sum(expd, axis=-1, keepdims=True)
                weight = (expd * (1.0 / total)).astype(jnp.bfloat16)
                mixed = jnp.dot(weight, vals, preferred_element_type=jnp.float32)
                for g, h in enumerate(heads):
                    new = wide[:, h * 128 : (h + 1) * 128] + mixed[g * QT : (g + 1) * QT]
                    new = new.astype(jnp.bfloat16)
                    state[layer, rows, h * 128 : (h + 1) * 128] = new
                    new = new.astype(jnp.float32)
                    squares = squares + new * new
            if layer < LAYERS - 1:
                squares = jnp.sum(squares, axis=-1, keepdims=True)
                rs[rows, :] = jnp.broadcast_to(squares, (QT, 128))
            cols = pl.ds(pl.multiple_of(y * WIDE, WIDE), WIDE)

            @pl.when(layer == y)
            def _():
                pltpu.make_async_copy(
                    state.at[layer, rows], out.at[rows, cols], outlocal
                ).start()

            @pl.when(layer != y)
            def _():
                pltpu.make_async_remote_copy(
                    src_ref=state.at[layer, rows],
                    dst_ref=out.at[rows, cols],
                    send_sem=outsend.at[layer],
                    recv_sem=outrecv,
                    device_id=y_id(layer),
                    device_id_type=MESH,
                ).start()

            return 0

        lax.fori_loop(0, REQ, one, 0)
        if layer < LAYERS - 1:
            ssq[layer, y] = rs[...].T[0:8]
            for i in range(1, NY):
                pltpu.make_async_remote_copy(
                    src_ref=ssq.at[layer, y],
                    dst_ref=ssq.at[layer, y],
                    send_sem=qsend.at[layer, i],
                    recv_sem=qrecv.at[layer],
                    device_id=y_id(lax.rem(y + i, NY)),
                    device_id_type=MESH,
                ).start()

    wide = hid[...].astype(jnp.float32)
    mean_sq = jnp.sum(wide * wide, axis=-1, keepdims=True) * (1.0 / D)
    rs[...] = jnp.broadcast_to(lax.rsqrt(mean_sq + 1e-05), (256, 128))
    kv[NRET * PT + QT :] = jnp.zeros((KEYS - NRET * PT - QT, PAIR), jnp.bfloat16)

    for copy in local_copies():
        copy.wait()
    z_first(0)

    def do_step(k):
        if k >= 2:
            x_sent(k - 2)
        choose(k, z)
        for hop in range(1, 5):
            for half in range(2):
                for up in (True, False):
                    if hop <= hops(up, half):
                        z_arrival(k, up, half, hop).wait_recv()
                        if hop < hops(up, half):
                            z_copy(k, up, half, hop + 1).start()
            if hop == 2 and k < LAYERS - 1:
                y_arrived(k + 1)
                z_first(k + 1)
            choose(k, mod(z - hop, NZ))
            if hop < 4:
                choose(k, mod(z + hop, NZ))
            if hop == 3 and k >= 2:
                if k == 2:
                    x_arrived(0)
                    x_arrived(1)
                    attend(0)
                else:
                    x_arrived(2)
                    attend(1)

    for k in range(LAYERS):
        do_step(k)
    x_arrived(3)
    attend(2)
    attend(3)

    x_sent(2)
    x_sent(3)
    for k in range(LAYERS):
        for up in (True, False):
            for half in range(2):
                for hop in range(1, hops(up, half) + 1):
                    z_copy(k, up, half, hop).wait_send()
    for i in range(1, NY):
        for copy in scatter_copies(i):
            copy.wait_send()
        for layer in range(LAYERS - 1):
            what = ssq.at[layer, y]
            pltpu.make_async_copy(what, what, qsend.at[layer, i]).wait()
    for layer in range(LAYERS):

        @pl.when(layer != y)
        def _():
            what = state.at[layer]
            pltpu.make_async_copy(what, what, outsend.at[layer]).wait()

    what = out.at[:, pl.ds(0, 3 * WIDE)]
    pltpu.make_async_copy(what, what, outrecv).wait()
    what = out.at[:, pl.ds(0, WIDE)]
    pltpu.make_async_copy(what, what, outlocal).wait()


def general_attend(store, own, hidden, gain, sel, slots):
    vmem = pl.BlockSpec(memory_space=pltpu.VMEM)
    smem = pl.BlockSpec(memory_space=pltpu.SMEM)
    hbm = pl.BlockSpec(memory_space=pl.ANY)
    bf16 = jnp.bfloat16
    dma = pltpu.SemaphoreType.DMA
    return pl.pallas_call(
        general_kernel,
        out_shape=jax.ShapeDtypeStruct((REQ * QT, D), bf16),
        in_specs=[hbm, hbm, vmem, vmem, smem, smem],
        out_specs=hbm,
        scratch_shapes=[
            pltpu.VMEM((LAYERS, NZ, PASS_DEV, PT, PAIR), bf16),
            pltpu.VMEM((LAYERS, PLANE, NZ, CAP, PT, PAIR), bf16),
            pltpu.VMEM((2, NZ, PLANE, CAP, PT, PAIR), bf16),
            pltpu.VMEM((PLANE * NZ * CAP, PT, PAIR), bf16),
            pltpu.VMEM((PASS_DEV, PT, PAIR), bf16),
            pltpu.VMEM((LAYERS, REQ * QT, PAIR), bf16),
            pltpu.VMEM((KEYS, PAIR), bf16),
            pltpu.VMEM((LAYERS, REQ * QT, WIDE), bf16),
            pltpu.VMEM((REQ * QT, 128), jnp.float32),
            pltpu.VMEM((LAYERS - 1, NY, 8, REQ * QT), jnp.float32),
            dma((NY, 2)),
            dma((LAYERS, 2)),
            dma((NY, 2)),
            dma((LAYERS, 2)),
            dma((4,)),
            dma((LAYERS, 2, 2, 4)),
            dma((LAYERS, 2, 2, 4)),
            dma((LAYERS,)),
            dma((LAYERS,)),
            dma((LAYERS - 1, NY)),
            dma((LAYERS - 1,)),
            dma((LAYERS,)),
            dma(()),
            dma(()),
        ],
        compiler_params=pltpu.CompilerParams(
            collective_id=1, has_side_effects=True, vmem_limit_bytes=60 * 1024 * 1024
        ),
        name="general_attend",
    )(store, own, hidden, gain, sel, slots)


def per_device(hidden, norm_gain, own_kv, passage_kv, retrieval, passage_slot):
    cache, x, y, z, c = where_am_i()
    ids = jnp.broadcast_to(jnp.tile(retrieval.reshape(-1), 4)[None, :], (8, 128))
    rows, gains, tab = greet(ids, passage_slot.reshape(8, 128), norm_gain)
    most_z, most_x = tab[26, 0], tab[27, 0]
    turn = jnp.arange(32, dtype=jnp.int32)

    def fast(cz, collective_id):
        def run(store, own, hidden, gains):
            store = store.reshape(2, PASS_DEV // 2, PT, 4 * HALF * 2)
            return fast_attend(cz, collective_id, store, own, hidden, gains, tab)

        return run

    def general(store, own, hidden, gains):
        gain = lax.dynamic_slice(gains, (0, y * 8, 0), (NY, 8, 128)).reshape(NY, WIDE)
        near = lax.dynamic_slice(rows, (2 * z, 0), (2, 128)).reshape(NC, NX, 32)
        near = near.transpose(1, 0, 2).reshape(PLANE, 32)
        mine = x * NC + c
        owner = near // PASS_DEV
        inside = near % PASS_DEV
        source = (owner // (NZ * NC)) * NC + owner % NC
        plane = (owner // NC) % NZ
        earlier = (owner[:, None, :] == owner[:, :, None]) & (turn[None, :] < turn[:, None])
        rank = jnp.sum(earlier.astype(jnp.int32), axis=2)
        place = jnp.where(source == mine, plane * CAP + rank, -1)
        spots = jnp.arange(NZ * CAP, dtype=jnp.int32)
        sel = jnp.sum(
            jnp.where(place[:, None, :] == spots[None, :, None], inside[:, None, :], 0), axis=2
        )
        sel = sel.reshape(PLANE, NZ, CAP).transpose(1, 0, 2).reshape(NZ, PLANE * CAP)
        slot = (source * NZ + plane) * CAP + rank
        slots = lax.dynamic_slice(slot, (mine, 0), (1, 32)).reshape(32)
        return general_attend(store, own, hidden, gain, sel, slots)

    which = jnp.int32(0)
    for cz in CZS:
        which = which + (most_z > cz).astype(jnp.int32)
    which = jnp.where(most_x > 2 * CX, len(CZS), which)
    branches = [fast(cz, 2 + i) for i, cz in enumerate(CZS)] + [general]
    done = lax.switch(which, branches, passage_kv[0], own_kv[0], hidden, gains)
    return done[None]


def solution(mesh):
    return jax.shard_map(
        per_device,
        mesh=mesh,
        in_specs=(
            P("cache", None),
            P("section", None),
            P("section", "cache", None),
            P("section", "cache", None, None),
            P("cache", None),
            P(),
        ),
        out_specs=P("section", "cache", None),
        check_vma=False,
    )
```

```python
import functools

import jax
import jax.numpy as jnp
from jax import lax
from jax.experimental import pallas as pl
from jax.experimental.pallas import tpu as pltpu
from jax.sharding import PartitionSpec as P

D = 4096
QT = 64
PT = 32
NRET = 8
NX, NZ, NC, NY = 4, 8, 2, 4
PLANE = NX * NC
PASS_DEV = 16
REQ = 4
LAYERS = 4
CAP = 2
HALF = 256
PAIR = 512
WIDE = 1024
KEYS = 384
MESH = pl.DeviceIdType.MESH
STEPS = 2 * LAYERS
ONE = 256
CZS = (12, 14)
CX = 8
OWN = 64
KV_ROWS = NRET * PT + OWN


def mod(a, n):
    return lax.rem(a + n, n)


def where_am_i():
    cache = lax.axis_index("cache")
    y = lax.axis_index("section")
    c = lax.rem(cache, NC)
    z = lax.rem(cache // NC, NZ)
    x = cache // (NC * NZ)
    return cache, x, y, z, c


def cache_at(x, z, c):
    return (x * NZ + z) * NC + c


def greet_kernel(
    ids_ref,
    slot_ref,
    gain_ref,
    rows_out,
    gain_out,
    tab_out,
    mine,
    near,
    tile,
    far,
    fields,
    psend,
    precv,
    zsend,
    zrecv,
    gsend,
    grecv,
):
    cache, x, y, z, c = where_am_i()
    me = c * NX + x
    f32, bf16, i32 = jnp.float32, jnp.bfloat16, jnp.int32

    def plane_id(i):
        t = lax.rem(me + i, PLANE)
        return (cache_at(lax.rem(t, NX), z, t // NX), y)

    def z_id(i):
        return (cache_at(x, lax.rem(z + i, NZ), c), y)

    def y_id(i):
        return (cache, lax.rem(y + i, NY))

    def lanes(shape):
        return lax.broadcasted_iota(i32, shape, len(shape) - 1)

    def subs(shape):
        return lax.broadcasted_iota(i32, shape, len(shape) - 2)

    def mm(a, b):
        return jnp.dot(a.astype(bf16), b.astype(bf16), preferred_element_type=f32)

    barrier = pltpu.get_barrier_semaphore()
    for count, peer in ((PLANE, plane_id), (NZ, z_id), (NY, y_id)):
        for i in range(1, count):
            pl.semaphore_signal(barrier, inc=1, device_id=peer(i), device_id_type=MESH)

    ids = ids_ref[0:1, :]
    hit = (jnp.broadcast_to(ids % 128, (128, 128)) == subs((128, 128))).astype(f32)
    high = mm((slot_ref[...] // 32).astype(f32), hit)
    low = mm((slot_ref[...] % 32).astype(f32), hit)
    pick = jnp.broadcast_to(ids // 128, (8, 128)) == subs((8, 128))
    found = jnp.sum(jnp.where(pick, high * 32.0 + low, 0.0), axis=0, keepdims=True)
    found = jnp.where(lanes((1, 128)) // 32 == lax.rem(me, 4), found, 0.0)
    mine[...] = jnp.broadcast_to(found, (8, 128)).astype(i32)
    for i in range(32):
        gain_out[y, i : i + 1, :] = gain_ref[:, i * 128 : (i + 1) * 128].astype(f32)

    pl.semaphore_wait(barrier, PLANE + NZ + NY - 3)
    first, second, third = [], [], []
    for i in range(1, PLANE):
        first.append(
            pltpu.make_async_remote_copy(
                src_ref=mine,
                dst_ref=near.at[me],
                send_sem=psend.at[i],
                recv_sem=precv.at[i],
                device_id=plane_id(i),
                device_id_type=MESH,
            )
        )
    for i in range(1, NY):
        second.append(
            pltpu.make_async_remote_copy(
                src_ref=gain_out.at[y],
                dst_ref=gain_out.at[y],
                send_sem=gsend.at[i],
                recv_sem=grecv.at[i],
                device_id=y_id(i),
                device_id_type=MESH,
            )
        )
    for copy in first + second:
        copy.start()
    near[me] = mine[...]
    for copy in first:
        copy.wait()
    row = subs((8, 128))
    tile[...] = jnp.where(row == 0, near[0] + near[1] + near[2] + near[3], 0) + jnp.where(
        row == 1, near[4] + near[5] + near[6] + near[7], 0
    )
    for i in range(1, NZ):
        third.append(
            pltpu.make_async_remote_copy(
                src_ref=tile,
                dst_ref=far.at[z],
                send_sem=zsend.at[i],
                recv_sem=zrecv.at[i],
                device_id=z_id(i),
                device_id_type=MESH,
            )
        )
    for copy in third:
        copy.start()
    far[z] = tile[...]
    for copy in third:
        copy.wait()
    for i in range(NZ):
        rows_out[2 * i : 2 * i + 2, :] = far[i, 0:2, :]

    rows = rows_out[...]
    owner = rows // PASS_DEV
    inside = rows % PASS_DEV
    plane = (owner // NC) % NZ
    o8 = (owner % NC) * NX + owner // (NZ * NC)
    stripe = (inside + o8) % PLANE
    place = o8 * 2 + inside // PLANE
    group = plane * PLANE + stripe
    chip = stripe % NX

    wide = (128, 128)
    same = (subs(wide) // 32 == lanes(wide) // 32) & (subs(wide) < lanes(wide))
    rank = jnp.zeros((2 * NZ, 128), f32)
    for v in range(NX):
        here = (chip == v).astype(f32)
        rank = rank + here * mm(here, same.astype(f32))
    rank = rank.astype(i32)
    fields[0] = group
    fields[1] = place
    fields[2] = chip
    fields[3] = rank

    groups = NZ * PLANE
    count = jnp.zeros((PASS_DEV, groups), f32)
    for i in range(2 * NZ):
        in_group = jnp.broadcast_to(group[i : i + 1], (groups, 128)) == subs((groups, 128))
        in_place = jnp.broadcast_to(place[i : i + 1], (PASS_DEV, 128)) == subs((PASS_DEV, 128))
        count = count + lax.dot_general(
            in_place.astype(f32).astype(bf16),
            in_group.astype(f32).astype(bf16),
            (((1,), (1,)), ((), ())),
            preferred_element_type=f32,
        )
    need = (count > 0.5).astype(f32)
    square = (PASS_DEV, PASS_DEV)
    before = mm((lanes(square) < subs(square)).astype(f32), need)

    def one_max(value):
        return jnp.max(jnp.max(value, axis=1, keepdims=True), axis=0, keepdims=True)

    most_z = one_max(jnp.sum(need, axis=0, keepdims=True)).astype(i32)
    most_x = one_max(rank) + 1

    ours = (lanes((PASS_DEV, groups)) == z * PLANE + me).astype(f32)
    my_need = jnp.sum(need * ours, axis=1, keepdims=True)
    my_before = jnp.sum(before * ours, axis=1, keepdims=True).astype(i32)
    hit = (my_before == lanes((PASS_DEV, 128))) & (my_need > 0.5)
    csel = jnp.sum(jnp.where(hit, subs((PASS_DEV, 128)), 0), axis=0, keepdims=True)
    tab_out[0:8, :] = jnp.broadcast_to(csel, (8, 128))

    block = (subs(wide) // 32 == lanes(wide)).astype(f32)
    for half in range(2):
        at = pl.ds(2 * z + half, 1)
        g, a, b, k = fields[0, at, :], fields[1, at, :], fields[2, at, :], fields[3, at, :]
        in_group = jnp.broadcast_to(g, (groups, 128)) == subs((groups, 128))
        in_place = jnp.broadcast_to(a, (PASS_DEV, 128)) == subs((PASS_DEV, 128))
        spot = mm(before, in_group.astype(f32)) * in_place.astype(f32)
        spot = jnp.sum(spot, axis=0, keepdims=True)
        core = (g % PLANE) // NX
        where = ((core * NZ + g // PLANE) * CZS[-1]).astype(f32) + jnp.minimum(spot, CZS[-1] - 1.0)
        key = jnp.where((b == x) & (k % NC == c), k // NC, -1)
        hit = jnp.broadcast_to(key, (CX, 128)) == subs((CX, 128))
        chosen = jnp.where(hit, jnp.broadcast_to(where, (CX, 128)), 0.0)
        tab_out[8 + 8 * half : 16 + 8 * half, :] = mm(chosen, block).astype(i32)
        slot = ((k % NC) * NX + b) * CX + jnp.minimum(k // NC, CX - 1)
        tab_out[24 + half : 25 + half, :] = slot
    tab_out[26:27, :] = jnp.broadcast_to(most_z, (1, 128))
    tab_out[27:28, :] = jnp.broadcast_to(most_x, (1, 128))
    tab_out[28:32, :] = jnp.zeros((4, 128), i32)
    for copy in second:
        copy.wait()


def greet(ids, slot, gain):
    vmem = pl.BlockSpec(memory_space=pltpu.VMEM)
    dma = pltpu.SemaphoreType.DMA
    return pl.pallas_call(
        greet_kernel,
        out_shape=(
            jax.ShapeDtypeStruct((2 * NZ, 128), jnp.int32),
            jax.ShapeDtypeStruct((NY, 32, 128), jnp.float32),
            jax.ShapeDtypeStruct((32, 128), jnp.int32),
        ),
        in_specs=[vmem, vmem, vmem],
        out_specs=(vmem, vmem, vmem),
        scratch_shapes=[
            pltpu.VMEM((8, 128), jnp.int32),
            pltpu.VMEM((PLANE, 8, 128), jnp.int32),
            pltpu.VMEM((8, 128), jnp.int32),
            pltpu.VMEM((NZ, 8, 128), jnp.int32),
            pltpu.VMEM((4, 2 * NZ, 128), jnp.int32),
            dma((PLANE,)),
            dma((PLANE,)),
            dma((NZ,)),
            dma((NZ,)),
            dma((NY,)),
            dma((NY,)),
        ],
        compiler_params=pltpu.CompilerParams(collective_id=0, has_side_effects=True),
        name="greet",
    )(ids, slot, gain)


def fast_kernel(
    cz, store, own_in, hid, gain, tab, out, ybuf, send, kvs, own, state, staged, gains, rs,
    ssq, box, packed, ysend, yrecv, osend, orecv, local, ssend, srecv, csend, crecv, zsend, zrecv, xsend, xrecv,
    qsend, qrecv, outsend, outrecv, outlocal, *many
):
    strips, pools, recvs = many[:STEPS], many[STEPS : 2 * STEPS], many[2 * STEPS :]
    cache, x, y, z, c = where_am_i()
    me = c * NX + x
    scale = 1.4426950408889634 / 128**0.5

    def plane_id(t):
        return (cache_at(lax.rem(t, NX), z, t // NX), y)

    def z_id(dz):
        return (cache_at(x, mod(z + dz, NZ), c), y)

    def y_id(s):
        return (cache, s)

    def step_of(i, s):
        return jnp.where(i == 2 * s, 0, jnp.where(i < 2 * s, i + 1, i))

    def part_of(q):
        return 2 * y if q == 0 else jnp.where(q - 1 < 2 * y, q - 1, q)

    barrier = pltpu.get_barrier_semaphore()
    for i in range(1, PLANE):
        pl.semaphore_signal(
            barrier, inc=1, device_id=plane_id(lax.rem(me + i, PLANE)), device_id_type=MESH
        )
    for i in range(1, NY):
        pl.semaphore_signal(
            barrier, inc=1, device_id=y_id(lax.rem(y + i, NY)), device_id_type=MESH
        )
    for dz in (1, -1):
        pl.semaphore_signal(barrier, inc=1, device_id=z_id(dz), device_id_type=MESH)
    pl.semaphore_wait(barrier, PLANE + NY)

    def local_copies():
        made = []
        for j in range(2):
            for part in range(2):
                cols = pl.ds(pl.multiple_of(part * 1024 + y * HALF + j * 128, 128), 128)
                made.append(
                    pltpu.make_async_copy(
                        store.at[:, :, :, cols],
                        ybuf.at[step_of(2 * y + j, y), :, :, :, pl.ds(part * 128, 128)],
                        local.at[2 * j + part],
                    )
                )
        for part in range(2):
            cols = pl.ds(pl.multiple_of(part * 1024 + y * HALF, HALF), HALF)
            made.append(
                pltpu.make_async_copy(
                    own_in.at[:, cols], own.at[y, :, pl.ds(part * HALF, HALF)], local.at[4 + part]
                )
            )
        return made

    def pack_copies(i, j):
        s = lax.rem(y + i, NY)
        made = []
        for part in range(2):
            cols = pl.ds(pl.multiple_of(part * 1024 + s * HALF + j * 128, 128), 128)
            made.append(
                pltpu.make_async_copy(
                    store.at[:, :, :, cols],
                    box.at[i - 1, j, :, :, :, pl.ds(part * 128, 128)],
                    packed.at[i, j, part],
                )
            )
        return made

    def scatter_copy(i, j):
        s = lax.rem(y + i, NY)
        q = step_of(2 * y + j, s)
        return pltpu.make_async_remote_copy(
            src_ref=box.at[i - 1, j],
            dst_ref=ybuf.at[q],
            send_sem=ysend.at[i, j],
            recv_sem=yrecv.at[q],
            device_id=y_id(s),
            device_id_type=MESH,
        )

    def own_scatter(i):
        s = lax.rem(y + i, NY)
        made = []
        for part in range(2):
            cols = pl.ds(pl.multiple_of(part * 1024 + s * HALF, HALF), HALF)
            made.append(
                pltpu.make_async_remote_copy(
                    src_ref=own_in.at[:, cols],
                    dst_ref=own.at[y, :, pl.ds(part * HALF, HALF)],
                    send_sem=osend.at[i, part],
                    recv_sem=orecv.at[y, part],
                    device_id=y_id(s),
                    device_id_type=MESH,
                )
            )
        return made

    def stripe(q):
        def push(i, _):
            t = lax.rem(me + i, PLANE)
            pltpu.make_async_remote_copy(
                src_ref=ybuf.at[q, :, mod(t - me, PLANE)],
                dst_ref=strips[q].at[pl.ds(me * 2, 2)],
                send_sem=ssend.at[q],
                recv_sem=srecv.at[q],
                device_id=plane_id(t),
                device_id_type=MESH,
            ).start()
            return 0

        strips[q][pl.ds(me * 2, 2)] = ybuf[q, :, 0]
        lax.fori_loop(1, PLANE, push, 0)

    def z_ref(q, plane, half):
        at = (c * NZ + plane) * CZS[-1]
        if half == 0:
            return pools[q].at[pl.ds(at, cz - cz // 2)]
        return pools[q].at[pl.ds(at + cz - cz // 2, cz // 2)]

    def z_copy(q, up, half, hop):
        where = z_ref(q, mod(z - (hop - 1), NZ) if up else mod(z + (hop - 1), NZ), half)
        return pltpu.make_async_remote_copy(
            src_ref=where,
            dst_ref=where,
            send_sem=zsend.at[q, int(up), half, hop - 1],
            recv_sem=zrecv.at[q, int(up), half, hop - 1],
            device_id=z_id(1 if up else -1),
            device_id_type=MESH,
        )

    def z_arrival(q, up, half, hop):
        where = z_ref(q, mod(z - hop, NZ) if up else mod(z + hop, NZ), half)
        return pltpu.make_async_remote_copy(
            src_ref=where,
            dst_ref=where,
            send_sem=zsend.at[q, int(up), half, hop - 1],
            recv_sem=zrecv.at[q, int(up), half, hop - 1],
            device_id=z_id(1 if up else -1),
            device_id_type=MESH,
        )

    def hops(up, half):
        return 4 if bool(up) == (half == 0) else 3

    def share(where, q):
        pltpu.make_async_remote_copy(
            src_ref=where,
            dst_ref=where,
            send_sem=csend.at[q],
            recv_sem=crecv.at[q],
            device_id=(cache_at(x, z, 1 - c), y),
            device_id_type=MESH,
        ).start()

    def compact(q):
        what = strips[q].at[pl.ds(0, 2 * PLANE - 2)]
        pltpu.make_async_copy(what, what, srecv.at[q]).wait()
        for i in range(cz):
            pools[q][(c * NZ + z) * CZS[-1] + i] = strips[q][tab[0, i]]
        for half in range(2):
            for up in (True, False):
                z_copy(q, up, half, 1).start()
        share(pools[q].at[pl.ds((c * NZ + z) * CZS[-1], cz)], q)

    def choose(q):
        par = q % 2
        what = pools[q].at[pl.ds(0, NZ * cz)]
        pltpu.make_async_copy(what, what, crecv.at[q]).wait()
        if q >= 2:
            x_sent(q - 2)

        def fill(t, _):
            for i in range(CX):
                send[par, t, i] = pools[q][tab[8 + 8 * (t // 4) + i, lax.rem(t, 4)]]
            return 0

        lax.fori_loop(0, PLANE, fill, 0)
        recvs[q][pl.ds(me * CX, CX)] = send[par, me]

        def push(i, _):
            t = lax.rem(me + i, PLANE)
            pltpu.make_async_remote_copy(
                src_ref=send.at[par, t],
                dst_ref=recvs[q].at[pl.ds(me * CX, CX)],
                send_sem=xsend.at[q],
                recv_sem=xrecv.at[q],
                device_id=plane_id(t),
                device_id_type=MESH,
            ).start()
            return 0

        lax.fori_loop(1, PLANE, push, 0)

    def x_sent(q):
        what = send.at[q % 2, pl.ds(0, PLANE - 1)]
        pltpu.make_async_copy(what, what, xsend.at[q]).wait()

    def assemble(q):
        what = recvs[q].at[pl.ds(0, (PLANE - 1) * CX)]
        pltpu.make_async_copy(what, what, xrecv.at[q]).wait()
        part = part_of(q)

        def one(r, _):
            for n in range(NRET):
                at = tab[24 + me // 4, lax.rem(me, 4) * 32 + r * NRET + n]
                kvs[part, r, n * PT : (n + 1) * PT] = recvs[q][at]
            return 0

        lax.fori_loop(0, REQ, one, 0)

    def y_arrived(q):
        what = ybuf.at[q]
        pltpu.make_async_copy(what, what, yrecv.at[q]).wait()

    krow = lax.broadcasted_iota(jnp.int32, (OWN, 4 * QT), 0)
    qcol = lax.rem(lax.broadcasted_iota(jnp.int32, (OWN, 4 * QT), 1), QT)

    def before_layer(layer):
        @pl.when(layer != y)
        def _():
            for part in range(2):
                what = own.at[layer, :, pl.ds(part * HALF, HALF)]
                pltpu.make_async_copy(what, what, orecv.at[layer, part]).wait()

        if layer > 0:
            what = ssq.at[layer - 1, pl.ds(0, NY - 1)]
            pltpu.make_async_copy(what, what, qrecv.at[layer - 1]).wait()
            total = ssq[layer - 1, 0] + ssq[layer - 1, 1] + ssq[layer - 1, 2] + ssq[layer - 1, 3]
            total = total + pltpu.roll(total, QT, 1)
            total = total + pltpu.roll(total, 2 * QT, 1)
            rs[...] = lax.rsqrt(total * (1.0 / D) + 1e-05)

    def attend(layer, r, heads_of):
        rows = pl.ds(pl.multiple_of(r * QT, QT), QT)
        causal = krow <= qcol
        squares = jnp.zeros((1, 4 * QT), jnp.float32)
        for j in heads_of:
            part = 2 * layer + j
            wide = state[r, j].astype(jnp.float32)
            query = (wide * rs[pl.ds(r, 1), :] * gains[layer, j]).astype(jnp.bfloat16)
            far_keys = kvs[part, r, :, 0:128]
            far_vals = kvs[part, r, :, 128:256]
            near_keys = own[layer, rows, j * 128 : (j + 1) * 128]
            near_vals = own[layer, rows, HALF + j * 128 : HALF + (j + 1) * 128]
            far = jnp.dot(far_keys, query, preferred_element_type=jnp.float32)
            near = jnp.dot(near_keys, query, preferred_element_type=jnp.float32)
            near = jnp.where(causal, near, -jnp.inf)
            top = jnp.maximum(
                jnp.max(far, axis=0, keepdims=True), jnp.max(near, axis=0, keepdims=True)
            )
            far = jnp.exp2((far - top) * scale)
            near = jnp.exp2((near - top) * scale)
            total = jnp.sum(far, axis=0, keepdims=True) + jnp.sum(near, axis=0, keepdims=True)
            total = 1.0 / total
            far = (far * total).astype(jnp.bfloat16)
            near = (near * total).astype(jnp.bfloat16)
            first = (((0,), (0,)), ((), ()))
            mixed = lax.dot_general(far_vals, far, first, preferred_element_type=jnp.float32)
            mixed = mixed + lax.dot_general(
                near_vals, near, first, preferred_element_type=jnp.float32
            )
            new = (wide + mixed).astype(jnp.bfloat16)
            state[r, j] = new
            turned = new.T
            for g in range(4):
                h = 4 * j + g
                staged[layer, rows, h * 128 : (h + 1) * 128] = turned[g * QT : (g + 1) * QT]
            new = new.astype(jnp.float32)
            squares = squares + jnp.sum(new * new, axis=0, keepdims=True)
        if layer < LAYERS - 1:
            ssq[layer, y, pl.ds(r, 1), :] = squares
        width = PAIR * len(heads_of)
        cols = pl.ds(pl.multiple_of(y * WIDE + heads_of[0] * PAIR, PAIR), width)
        made = staged.at[layer, rows, pl.ds(heads_of[0] * PAIR, width)]

        @pl.when(layer == y)
        def _():
            pltpu.make_async_copy(made, out.at[rows, cols], outlocal).start()

        @pl.when(layer != y)
        def _():
            pltpu.make_async_remote_copy(
                src_ref=made,
                dst_ref=out.at[rows, cols],
                send_sem=outsend.at[layer],
                recv_sem=outrecv,
                device_id=y_id(layer),
                device_id_type=MESH,
            ).start()

    def after_layer(layer):
        for i in range(1, NY):
            pltpu.make_async_remote_copy(
                src_ref=ssq.at[layer, y],
                dst_ref=ssq.at[layer, y],
                send_sem=qsend.at[layer, i],
                recv_sem=qrecv.at[layer],
                device_id=y_id(lax.rem(y + i, NY)),
                device_id_type=MESH,
            ).start()

    def attend_rows(layer, first, count, together, heads_of=(0, 1)):
        def body(i, _):
            for u in range(together):
                attend(layer, first + i * together + u, heads_of)
            return 0

        lax.fori_loop(0, count // together, body, 0)

    own_copies = local_copies()
    for copy in own_copies[:2]:
        copy.start()
    packs = [(i, j, pack_copies(i, j)) for j in range(2) for i in (1, 3, 2)]
    for i, j, copies in packs[:3]:
        for copy in copies:
            copy.start()
    for copy in own_copies[2:]:
        copy.start()
    for i, j, copies in packs[3:]:
        for copy in copies:
            copy.start()
    own_copies[0].wait()
    own_copies[1].wait()
    stripe(0)
    for i, j, copies in packs:
        for copy in copies:
            copy.wait()

    def scatter(first, last):
        @pl.when((y >= first) & (y <= last))
        def _():
            for j in range(2):
                for i in (1, 3, 2):
                    scatter_copy(i, j).start()

    def scatter_own():
        for i in (1, 3, 2):
            for copy in own_scatter(i):
                copy.start()

    scatter(0, 1)
    compact(0)

    for layer in range(LAYERS - 1):
        ssq[layer, y] = jnp.zeros((8, 4 * QT), jnp.float32)
    mean_sq = jnp.zeros((REQ * QT, 1), jnp.float32)
    for i in range(8):
        wide = hid[:, i * 512 : (i + 1) * 512].astype(jnp.float32)
        mean_sq = mean_sq + jnp.sum(wide * wide, axis=-1, keepdims=True)
    mean_sq = jnp.broadcast_to(mean_sq * (1.0 / D), (REQ * QT, 128)).T
    mean_sq = lax.rsqrt(mean_sq + 1e-05)
    for r in range(REQ):
        part = mean_sq[0:1, r * QT : (r + 1) * QT]
        rs[r : r + 1, :] = jnp.concatenate([part] * 4, axis=1)
    rs[REQ:, :] = jnp.zeros((8 - REQ, 4 * QT), jnp.float32)
    for j in range(2):
        for r in range(REQ):
            heads = []
            for g in range(4):
                cols = pl.ds(pl.multiple_of(y * WIDE + (4 * j + g) * 128, 128), 128)
                heads.append(hid[r * QT : (r + 1) * QT, cols])
            state[r, j] = jnp.concatenate(heads, axis=0).T
        for layer in range(LAYERS):
            heads = []
            for g in range(4):
                at = gain[layer, pl.ds(y * 8 + 4 * j + g, 1), :]
                heads.append(jnp.broadcast_to(at, (QT, 128)))
            gains[layer, j] = jnp.concatenate(heads, axis=0).T

    def arrived_from_y(q):
        part = part_of(q)

        @pl.when(part != 2 * y + 1)
        def _():
            y_arrived(q)

    for copy in own_copies[2:]:
        copy.wait()
    arrived_from_y(1)
    stripe(1)
    todo = {}

    def later(slot, work):
        todo.setdefault(slot, []).append(work)

    later(0, lambda: scatter(2, 2))
    later(1, lambda: scatter(3, 3))
    later(3, scatter_own)

    for q in range(1, STEPS):
        if q >= 2:
            later(q - 1, lambda q=q: (arrived_from_y(q), stripe(q)))
        later(2 * q - 1, lambda q=q: compact(q))
    for q in range(STEPS):
        later(2 * q + 4, lambda q=q: choose(q))
    for q in range(STEPS - 1):
        later(2 * q + 6, lambda q=q: assemble(q))
    for layer in range(2):
        later(4 * layer + 10, lambda layer=layer: before_layer(layer))
        for half in range(2):
            later(
                4 * layer + 10 + 2 * half,
                lambda layer=layer, half=half: attend_rows(layer, 2 * half, 2, 1),
            )
        later(4 * layer + 12, lambda layer=layer: after_layer(layer))

    for slot in range(2 * STEPS + 3):
        for q in range(STEPS):
            hop = slot - 2 * q + 1
            if not 1 <= hop <= 4:
                continue
            for half in range(2):
                for up in (True, False):
                    if hop <= hops(up, half):
                        z_arrival(q, up, half, hop).wait_recv()
                        if hop < hops(up, half):
                            z_copy(q, up, half, hop + 1).start()
                        plane = mod(z - hop, NZ) if up else mod(z + hop, NZ)
                        share(z_ref(q, plane, half), q)
        for work in todo.get(slot, ()):
            work()

    before_layer(2)
    attend_rows(2, 0, REQ, 2)
    after_layer(2)
    before_layer(3)
    attend_rows(3, 0, REQ, 2, (0,))
    assemble(STEPS - 1)
    attend_rows(3, 0, REQ, 2, (1,))

    x_sent(STEPS - 2)
    x_sent(STEPS - 1)
    for q in range(STEPS):
        what = strips[q].at[pl.ds(0, 2 * PLANE - 2)]
        pltpu.make_async_copy(what, what, ssend.at[q]).wait()
        what = pools[q].at[pl.ds(0, NZ * cz)]
        pltpu.make_async_copy(what, what, csend.at[q]).wait()
        for up in (True, False):
            for half in range(2):
                for hop in range(1, hops(up, half) + 1):
                    z_copy(q, up, half, hop).wait_send()
    for i in range(1, NY):
        for j in range(2):
            scatter_copy(i, j).wait_send()
        for copy in own_scatter(i):
            copy.wait_send()
        for layer in range(LAYERS - 1):
            what = ssq.at[layer, y]
            pltpu.make_async_copy(what, what, qsend.at[layer, i]).wait()
    for layer in range(LAYERS):

        @pl.when(layer != y)
        def _():
            what = staged.at[layer]
            pltpu.make_async_copy(what, what, outsend.at[layer]).wait()

    what = out.at[:, pl.ds(0, 3 * WIDE)]
    pltpu.make_async_copy(what, what, outrecv).wait()
    what = out.at[:, pl.ds(0, WIDE)]
    pltpu.make_async_copy(what, what, outlocal).wait()


def fast_attend(cz, collective_id, store, own, hidden, gain, tab):
    vmem = pl.BlockSpec(memory_space=pltpu.VMEM)
    smem = pl.BlockSpec(memory_space=pltpu.SMEM)
    hbm = pl.BlockSpec(memory_space=pl.ANY)
    bf16 = jnp.bfloat16
    dma = pltpu.SemaphoreType.DMA
    return pl.pallas_call(
        functools.partial(fast_kernel, cz),
        out_shape=jax.ShapeDtypeStruct((REQ * QT, D), bf16),
        in_specs=[hbm, hbm, vmem, vmem, smem],
        out_specs=hbm,
        scratch_shapes=[
            pltpu.VMEM((STEPS, 2, PLANE, PT, ONE), bf16),
            pltpu.VMEM((2, PLANE, CX, PT, ONE), bf16),
            pltpu.VMEM((STEPS, REQ, NRET * PT, ONE), bf16),
            pltpu.VMEM((LAYERS, REQ * QT, PAIR), bf16),
            pltpu.VMEM((REQ, 2, 128, 4 * QT), bf16),
            pltpu.VMEM((LAYERS, REQ * QT, WIDE), bf16),
            pltpu.VMEM((LAYERS, 2, 128, 4 * QT), jnp.float32),
            pltpu.VMEM((8, 4 * QT), jnp.float32),
            pltpu.VMEM((LAYERS - 1, NY, 8, 4 * QT), jnp.float32),
            pltpu.VMEM((NY - 1, 2, 2, PLANE, PT, ONE), bf16),
            dma((NY, 2, 2)),
            dma((NY, 2)),
            dma((STEPS,)),
            dma((NY, 2)),
            dma((LAYERS, 2)),
            dma((6,)),
            dma((STEPS,)),
            dma((STEPS,)),
            dma((STEPS,)),
            dma((STEPS,)),
            dma((STEPS, 2, 2, 4)),
            dma((STEPS, 2, 2, 4)),
            dma((STEPS,)),
            dma((STEPS,)),
            dma((LAYERS - 1, NY)),
            dma((LAYERS - 1,)),
            dma((LAYERS,)),
            dma(()),
            dma(()),
        ]
        + [pltpu.VMEM((PLANE * 2, PT, ONE), bf16)] * STEPS
        + [pltpu.VMEM((NC * NZ * CZS[-1], PT, ONE), bf16)] * STEPS
        + [pltpu.VMEM((PLANE * CX, PT, ONE), bf16)] * STEPS,
        compiler_params=pltpu.CompilerParams(
            collective_id=collective_id, has_side_effects=True, vmem_limit_bytes=60 * 1024 * 1024
        ),
        name="fast_attend_" + str(cz),
    )(store, own, hidden, gain, tab)


def general_kernel(
    store,
    own_in,
    hid,
    gain,
    sel,
    slots,
    out,
    pool,
    recv,
    send,
    rstage,
    stage,
    own,
    kv,
    state,
    rs,
    ssq,
    ysend,
    yrecv,
    osend,
    orecv,
    local,
    zsend,
    zrecv,
    xsend,
    xrecv,
    qsend,
    qrecv,
    outsend,
    outrecv,
    outlocal,
):
    cache, x, y, z, c = where_am_i()
    me = x * NC + c

    def plane_id(t):
        return (cache_at(t // NC, z, lax.rem(t, NC)), y)

    def z_id(dz):
        return (cache_at(x, mod(z + dz, NZ), c), y)

    def y_id(s):
        return (cache, s)

    def step_of(layer, s):
        return jnp.where(layer == s, 0, jnp.where(layer < s, layer + 1, layer))

    barrier = pltpu.get_barrier_semaphore()
    for i in range(1, PLANE):
        pl.semaphore_signal(
            barrier, inc=1, device_id=plane_id(lax.rem(me + i, PLANE)), device_id_type=MESH
        )
    for i in range(1, NY):
        pl.semaphore_signal(
            barrier, inc=1, device_id=y_id(lax.rem(y + i, NY)), device_id_type=MESH
        )
    for dz in (1, -1):
        pl.semaphore_signal(barrier, inc=1, device_id=z_id(dz), device_id_type=MESH)
    pl.semaphore_wait(barrier, PLANE + NY)

    def local_copies():
        made = []
        for part in range(2):
            cols = pl.ds(pl.multiple_of(part * 1024 + y * HALF, HALF), HALF)
            half = pl.ds(part * HALF, HALF)
            made.append(
                pltpu.make_async_copy(
                    store.at[:, :, cols], pool.at[0, z, :, :, half], local.at[part]
                )
            )
            made.append(
                pltpu.make_async_copy(
                    own_in.at[:, cols], own.at[y, :, half], local.at[2 + part]
                )
            )
        return made

    def scatter_copies(i):
        s = lax.rem(y + i, NY)
        made = []
        for part in range(2):
            cols = pl.ds(pl.multiple_of(part * 1024 + s * HALF, HALF), HALF)
            half = pl.ds(part * HALF, HALF)
            made.append(
                pltpu.make_async_remote_copy(
                    src_ref=store.at[:, :, cols],
                    dst_ref=pool.at[step_of(y, s), z, :, :, half],
                    send_sem=ysend.at[i, part],
                    recv_sem=yrecv.at[step_of(y, s), part],
                    device_id=y_id(s),
                    device_id_type=MESH,
                )
            )
            made.append(
                pltpu.make_async_remote_copy(
                    src_ref=own_in.at[:, cols],
                    dst_ref=own.at[y, :, half],
                    send_sem=osend.at[i, part],
                    recv_sem=orecv.at[y, part],
                    device_id=y_id(s),
                    device_id_type=MESH,
                )
            )
        return made

    for copy in local_copies():
        copy.start()
    for i in (1, 3, 2):
        for copy in scatter_copies(i):
            copy.start()

    def z_copy(k, up, half, hop):
        plane = mod(z - (hop - 1), NZ) if up else mod(z + (hop - 1), NZ)
        rows = pl.ds(half * 8, 8)
        where = pool.at[k, plane, rows]
        return pltpu.make_async_remote_copy(
            src_ref=where,
            dst_ref=where,
            send_sem=zsend.at[k, int(up), half, hop - 1],
            recv_sem=zrecv.at[k, int(up), half, hop - 1],
            device_id=z_id(1 if up else -1),
            device_id_type=MESH,
        )

    def z_arrival(k, up, half, hop):
        plane = mod(z - hop, NZ) if up else mod(z + hop, NZ)
        where = pool.at[k, plane, pl.ds(half * 8, 8)]
        return pltpu.make_async_remote_copy(
            src_ref=where,
            dst_ref=where,
            send_sem=zsend.at[k, int(up), half, hop - 1],
            recv_sem=zrecv.at[k, int(up), half, hop - 1],
            device_id=z_id(1 if up else -1),
            device_id_type=MESH,
        )

    def hops(up, half):
        return 4 if bool(up) == (half == 0) else 3

    def z_first(k):
        for half in range(2):
            for up in (True, False):
                z_copy(k, up, half, 1).start()

    def choose(k, plane):
        par = lax.rem(k, 2)
        stage[...] = pool[k, plane]

        def fill(t, _):
            for r in range(CAP):
                send[par, plane, t, r] = stage[sel[plane, t * CAP + r]]
            return 0

        lax.fori_loop(0, PLANE, fill, 0)
        recv[k, me, plane] = send[par, plane, me]

        def push(i, _):
            t = lax.rem(me + i, PLANE)
            pltpu.make_async_remote_copy(
                src_ref=send.at[par, plane, t],
                dst_ref=recv.at[k, me, plane],
                send_sem=xsend.at[k],
                recv_sem=xrecv.at[k],
                device_id=plane_id(t),
                device_id_type=MESH,
            ).start()
            return 0

        lax.fori_loop(1, PLANE, push, 0)

    def x_sent(k):
        what = send.at[lax.rem(k, 2), :, pl.ds(0, PLANE - 1)]
        pltpu.make_async_copy(what, what, xsend.at[k]).wait()

    def x_arrived(k):
        what = recv.at[k, pl.ds(0, PLANE - 1)]
        pltpu.make_async_copy(what, what, xrecv.at[k]).wait()

    def y_arrived(k):
        for part in range(2):
            what = pool.at[k, z, :, :, pl.ds(part * HALF, HALF)]
            pltpu.make_async_copy(what, what, yrecv.at[k, part]).wait()

    def attend(layer):
        k = step_of(layer, y)

        def lift(i, _):
            rstage[pl.ds(i * 16, 16)] = recv[k, i].reshape(16, PT, PAIR)
            return 0

        lax.fori_loop(0, PLANE, lift, 0)

        @pl.when(layer != y)
        def _():
            for part in range(2):
                what = own.at[layer, :, pl.ds(part * HALF, HALF)]
                pltpu.make_async_copy(what, what, orecv.at[layer, part]).wait()

        if layer > 0:
            what = ssq.at[layer - 1, pl.ds(0, NY - 1)]
            pltpu.make_async_copy(what, what, qrecv.at[layer - 1]).wait()
            total = ssq[layer - 1, 0] + ssq[layer - 1, 1] + ssq[layer - 1, 2] + ssq[layer - 1, 3]
            total = jnp.broadcast_to(total[0:1], (128, 256)).T
            rs[...] = lax.rsqrt(total * (1.0 / D) + 1e-05)

        row = lax.rem(lax.broadcasted_iota(jnp.int32, (4 * QT, KEYS), 0), QT)
        col = lax.broadcasted_iota(jnp.int32, (4 * QT, KEYS), 1)
        seen = (col < NRET * PT + 1 + row)

        def one(r, _):
            rows = pl.ds(pl.multiple_of(r * QT, QT), QT)
            for n in range(NRET):
                kv[n * PT : (n + 1) * PT] = rstage[slots[r * NRET + n]]
            kv[NRET * PT : NRET * PT + QT] = own[layer, rows]
            if layer == 0:
                before = hid[rows, pl.ds(pl.multiple_of(y * WIDE, WIDE), WIDE)]
            else:
                before = state[layer - 1, rows]
            wide = before.astype(jnp.float32)
            query = (wide * rs[rows, 0:1] * gain[layer : layer + 1, :]).astype(jnp.bfloat16)
            squares = jnp.zeros((QT, 128), jnp.float32)
            for j in range(2):
                heads = [4 * j + g for g in range(4)]
                qj = jnp.concatenate([query[:, h * 128 : (h + 1) * 128] for h in heads], axis=0)
                keys = kv[:, j * 128 : (j + 1) * 128]
                vals = kv[:, HALF + j * 128 : HALF + (j + 1) * 128]
                score = lax.dot_general(
                    qj, keys, (((1,), (1,)), ((), ())), preferred_element_type=jnp.float32
                )
                score = jnp.where(seen, score * (1.0 / 128**0.5), -jnp.inf)
                top = jnp.max(score, axis=-1, keepdims=True)
                expd = jnp.exp(score - top)
                total = jnp.sum(expd, axis=-1, keepdims=True)
                weight = (expd * (1.0 / total)).astype(jnp.bfloat16)
                mixed = jnp.dot(weight, vals, preferred_element_type=jnp.float32)
                for g, h in enumerate(heads):
                    new = wide[:, h * 128 : (h + 1) * 128] + mixed[g * QT : (g + 1) * QT]
                    new = new.astype(jnp.bfloat16)
                    state[layer, rows, h * 128 : (h + 1) * 128] = new
                    new = new.astype(jnp.float32)
                    squares = squares + new * new
            if layer < LAYERS - 1:
                squares = jnp.sum(squares, axis=-1, keepdims=True)
                rs[rows, :] = jnp.broadcast_to(squares, (QT, 128))
            cols = pl.ds(pl.multiple_of(y * WIDE, WIDE), WIDE)

            @pl.when(layer == y)
            def _():
                pltpu.make_async_copy(
                    state.at[layer, rows], out.at[rows, cols], outlocal
                ).start()

            @pl.when(layer != y)
            def _():
                pltpu.make_async_remote_copy(
                    src_ref=state.at[layer, rows],
                    dst_ref=out.at[rows, cols],
                    send_sem=outsend.at[layer],
                    recv_sem=outrecv,
                    device_id=y_id(layer),
                    device_id_type=MESH,
                ).start()

            return 0

        lax.fori_loop(0, REQ, one, 0)
        if layer < LAYERS - 1:
            ssq[layer, y] = rs[...].T[0:8]
            for i in range(1, NY):
                pltpu.make_async_remote_copy(
                    src_ref=ssq.at[layer, y],
                    dst_ref=ssq.at[layer, y],
                    send_sem=qsend.at[layer, i],
                    recv_sem=qrecv.at[layer],
                    device_id=y_id(lax.rem(y + i, NY)),
                    device_id_type=MESH,
                ).start()

    wide = hid[...].astype(jnp.float32)
    mean_sq = jnp.sum(wide * wide, axis=-1, keepdims=True) * (1.0 / D)
    rs[...] = jnp.broadcast_to(lax.rsqrt(mean_sq + 1e-05), (256, 128))
    kv[NRET * PT + QT :] = jnp.zeros((KEYS - NRET * PT - QT, PAIR), jnp.bfloat16)

    for copy in local_copies():
        copy.wait()
    z_first(0)

    def do_step(k):
        if k >= 2:
            x_sent(k - 2)
        choose(k, z)
        for hop in range(1, 5):
            for half in range(2):
                for up in (True, False):
                    if hop <= hops(up, half):
                        z_arrival(k, up, half, hop).wait_recv()
                        if hop < hops(up, half):
                            z_copy(k, up, half, hop + 1).start()
            if hop == 2 and k < LAYERS - 1:
                y_arrived(k + 1)
                z_first(k + 1)
            choose(k, mod(z - hop, NZ))
            if hop < 4:
                choose(k, mod(z + hop, NZ))
            if hop == 3 and k >= 2:
                if k == 2:
                    x_arrived(0)
                    x_arrived(1)
                    attend(0)
                else:
                    x_arrived(2)
                    attend(1)

    for k in range(LAYERS):
        do_step(k)
    x_arrived(3)
    attend(2)
    attend(3)

    x_sent(2)
    x_sent(3)
    for k in range(LAYERS):
        for up in (True, False):
            for half in range(2):
                for hop in range(1, hops(up, half) + 1):
                    z_copy(k, up, half, hop).wait_send()
    for i in range(1, NY):
        for copy in scatter_copies(i):
            copy.wait_send()
        for layer in range(LAYERS - 1):
            what = ssq.at[layer, y]
            pltpu.make_async_copy(what, what, qsend.at[layer, i]).wait()
    for layer in range(LAYERS):

        @pl.when(layer != y)
        def _():
            what = state.at[layer]
            pltpu.make_async_copy(what, what, outsend.at[layer]).wait()

    what = out.at[:, pl.ds(0, 3 * WIDE)]
    pltpu.make_async_copy(what, what, outrecv).wait()
    what = out.at[:, pl.ds(0, WIDE)]
    pltpu.make_async_copy(what, what, outlocal).wait()


def general_attend(store, own, hidden, gain, sel, slots):
    vmem = pl.BlockSpec(memory_space=pltpu.VMEM)
    smem = pl.BlockSpec(memory_space=pltpu.SMEM)
    hbm = pl.BlockSpec(memory_space=pl.ANY)
    bf16 = jnp.bfloat16
    dma = pltpu.SemaphoreType.DMA
    return pl.pallas_call(
        general_kernel,
        out_shape=jax.ShapeDtypeStruct((REQ * QT, D), bf16),
        in_specs=[hbm, hbm, vmem, vmem, smem, smem],
        out_specs=hbm,
        scratch_shapes=[
            pltpu.VMEM((LAYERS, NZ, PASS_DEV, PT, PAIR), bf16),
            pltpu.VMEM((LAYERS, PLANE, NZ, CAP, PT, PAIR), bf16),
            pltpu.VMEM((2, NZ, PLANE, CAP, PT, PAIR), bf16),
            pltpu.VMEM((PLANE * NZ * CAP, PT, PAIR), bf16),
            pltpu.VMEM((PASS_DEV, PT, PAIR), bf16),
            pltpu.VMEM((LAYERS, REQ * QT, PAIR), bf16),
            pltpu.VMEM((KEYS, PAIR), bf16),
            pltpu.VMEM((LAYERS, REQ * QT, WIDE), bf16),
            pltpu.VMEM((REQ * QT, 128), jnp.float32),
            pltpu.VMEM((LAYERS - 1, NY, 8, REQ * QT), jnp.float32),
            dma((NY, 2)),
            dma((LAYERS, 2)),
            dma((NY, 2)),
            dma((LAYERS, 2)),
            dma((4,)),
            dma((LAYERS, 2, 2, 4)),
            dma((LAYERS, 2, 2, 4)),
            dma((LAYERS,)),
            dma((LAYERS,)),
            dma((LAYERS - 1, NY)),
            dma((LAYERS - 1,)),
            dma((LAYERS,)),
            dma(()),
            dma(()),
        ],
        compiler_params=pltpu.CompilerParams(
            collective_id=1, has_side_effects=True, vmem_limit_bytes=60 * 1024 * 1024
        ),
        name="general_attend",
    )(store, own, hidden, gain, sel, slots)


def per_device(hidden, norm_gain, own_kv, passage_kv, retrieval, passage_slot):
    cache, x, y, z, c = where_am_i()
    ids = jnp.broadcast_to(jnp.tile(retrieval.reshape(-1), 4)[None, :], (8, 128))
    rows, gains, tab = greet(ids, passage_slot.reshape(8, 128), norm_gain)
    most_z, most_x = tab[26, 0], tab[27, 0]
    turn = jnp.arange(32, dtype=jnp.int32)

    def fast(cz, collective_id):
        def run(store, own, hidden, gains):
            store = store.reshape(2, PASS_DEV // 2, PT, 4 * HALF * 2)
            return fast_attend(cz, collective_id, store, own, hidden, gains, tab)

        return run

    def general(store, own, hidden, gains):
        gain = lax.dynamic_slice(gains, (0, y * 8, 0), (NY, 8, 128)).reshape(NY, WIDE)
        near = lax.dynamic_slice(rows, (2 * z, 0), (2, 128)).reshape(NC, NX, 32)
        near = near.transpose(1, 0, 2).reshape(PLANE, 32)
        mine = x * NC + c
        owner = near // PASS_DEV
        inside = near % PASS_DEV
        source = (owner // (NZ * NC)) * NC + owner % NC
        plane = (owner // NC) % NZ
        earlier = (owner[:, None, :] == owner[:, :, None]) & (turn[None, :] < turn[:, None])
        rank = jnp.sum(earlier.astype(jnp.int32), axis=2)
        place = jnp.where(source == mine, plane * CAP + rank, -1)
        spots = jnp.arange(NZ * CAP, dtype=jnp.int32)
        sel = jnp.sum(
            jnp.where(place[:, None, :] == spots[None, :, None], inside[:, None, :], 0), axis=2
        )
        sel = sel.reshape(PLANE, NZ, CAP).transpose(1, 0, 2).reshape(NZ, PLANE * CAP)
        slot = (source * NZ + plane) * CAP + rank
        slots = lax.dynamic_slice(slot, (mine, 0), (1, 32)).reshape(32)
        return general_attend(store, own, hidden, gain, sel, slots)

    which = jnp.int32(0)
    for cz in CZS:
        which = which + (most_z > cz).astype(jnp.int32)
    which = jnp.where(most_x > 2 * CX, len(CZS), which)
    branches = [fast(cz, 2 + i) for i, cz in enumerate(CZS)] + [general]
    done = lax.switch(which, branches, passage_kv[0], own_kv[0], hidden, gains)
    return done[None]


def solution(mesh):
    return jax.shard_map(
        per_device,
        mesh=mesh,
        in_specs=(
            P("cache", None),
            P("section", None),
            P("section", "cache", None),
            P("section", "cache", None, None),
            P("cache", None),
            P(),
        ),
        out_specs=P("section", "cache", None),
        check_vma=False,
    )
```

```python
import functools

import jax
import jax.numpy as jnp
from jax import lax
from jax.experimental import pallas as pl
from jax.experimental.pallas import tpu as pltpu
from jax.sharding import PartitionSpec as P

D = 4096
QT = 64
PT = 32
NRET = 8
NX, NZ, NC, NY = 4, 8, 2, 4
PLANE = NX * NC
PASS_DEV = 16
REQ = 4
LAYERS = 4
CAP = 2
HALF = 256
PAIR = 512
WIDE = 1024
KEYS = 384
MESH = pl.DeviceIdType.MESH
STEPS = 2 * LAYERS
ONE = 256
CZS = (11, 13)
CX = 8
OWN = 64
KV_ROWS = NRET * PT + OWN


def mod(a, n):
    return lax.rem(a + n, n)


def where_am_i():
    cache = lax.axis_index("cache")
    y = lax.axis_index("section")
    c = lax.rem(cache, NC)
    z = lax.rem(cache // NC, NZ)
    x = cache // (NC * NZ)
    return cache, x, y, z, c


def cache_at(x, z, c):
    return (x * NZ + z) * NC + c


def greet_kernel(
    ids_ref,
    slot_ref,
    gain_ref,
    rows_out,
    gain_out,
    tab_out,
    mine,
    near,
    tile,
    far,
    fields,
    psend,
    precv,
    zsend,
    zrecv,
    gsend,
    grecv,
):
    cache, x, y, z, c = where_am_i()
    me = c * NX + x
    f32, bf16, i32 = jnp.float32, jnp.bfloat16, jnp.int32

    def plane_id(i):
        t = lax.rem(me + i, PLANE)
        return (cache_at(lax.rem(t, NX), z, t // NX), y)

    def z_id(i):
        return (cache_at(x, lax.rem(z + i, NZ), c), y)

    def y_id(i):
        return (cache, lax.rem(y + i, NY))

    def lanes(shape):
        return lax.broadcasted_iota(i32, shape, len(shape) - 1)

    def subs(shape):
        return lax.broadcasted_iota(i32, shape, len(shape) - 2)

    def mm(a, b):
        return jnp.dot(a.astype(bf16), b.astype(bf16), preferred_element_type=f32)

    barrier = pltpu.get_barrier_semaphore()
    for count, peer in ((PLANE, plane_id), (NZ, z_id), (NY, y_id)):
        for i in range(1, count):
            pl.semaphore_signal(barrier, inc=1, device_id=peer(i), device_id_type=MESH)

    ids = ids_ref[0:1, :]
    hit = (jnp.broadcast_to(ids % 128, (128, 128)) == subs((128, 128))).astype(f32)
    high = mm((slot_ref[...] // 32).astype(f32), hit)
    low = mm((slot_ref[...] % 32).astype(f32), hit)
    pick = jnp.broadcast_to(ids // 128, (8, 128)) == subs((8, 128))
    found = jnp.sum(jnp.where(pick, high * 32.0 + low, 0.0), axis=0, keepdims=True)
    found = jnp.where(lanes((1, 128)) // 32 == lax.rem(me, 4), found, 0.0)
    mine[...] = jnp.broadcast_to(found, (8, 128)).astype(i32)
    for i in range(32):
        gain_out[y, i : i + 1, :] = gain_ref[:, i * 128 : (i + 1) * 128].astype(f32)

    pl.semaphore_wait(barrier, PLANE + NZ + NY - 3)
    first, second, third = [], [], []
    for i in range(1, PLANE):
        first.append(
            pltpu.make_async_remote_copy(
                src_ref=mine,
                dst_ref=near.at[me],
                send_sem=psend.at[i],
                recv_sem=precv.at[i],
                device_id=plane_id(i),
                device_id_type=MESH,
            )
        )
    for i in range(1, NY):
        second.append(
            pltpu.make_async_remote_copy(
                src_ref=gain_out.at[y],
                dst_ref=gain_out.at[y],
                send_sem=gsend.at[i],
                recv_sem=grecv.at[i],
                device_id=y_id(i),
                device_id_type=MESH,
            )
        )
    for copy in first + second:
        copy.start()
    near[me] = mine[...]
    for copy in first:
        copy.wait()
    row = subs((8, 128))
    tile[...] = jnp.where(row == 0, near[0] + near[1] + near[2] + near[3], 0) + jnp.where(
        row == 1, near[4] + near[5] + near[6] + near[7], 0
    )
    for i in range(1, NZ):
        third.append(
            pltpu.make_async_remote_copy(
                src_ref=tile,
                dst_ref=far.at[z],
                send_sem=zsend.at[i],
                recv_sem=zrecv.at[i],
                device_id=z_id(i),
                device_id_type=MESH,
            )
        )
    for copy in third:
        copy.start()
    far[z] = tile[...]
    for copy in third:
        copy.wait()
    for i in range(NZ):
        rows_out[2 * i : 2 * i + 2, :] = far[i, 0:2, :]

    rows = rows_out[...]
    owner = rows // PASS_DEV
    inside = rows % PASS_DEV
    plane = (owner // NC) % NZ
    o8 = (owner % NC) * NX + owner // (NZ * NC)
    number = o8 * PASS_DEV + inside

    wide = (128, 128)
    count = jnp.zeros((NZ, 128), f32)
    for i in range(2 * NZ):
        in_plane = jnp.broadcast_to(plane[i : i + 1], (NZ, 128)) == subs((NZ, 128))
        is_number = jnp.broadcast_to(number[i : i + 1], wide) == subs(wide)
        count = count + lax.dot_general(
            in_plane.astype(f32).astype(bf16),
            is_number.astype(f32).astype(bf16),
            (((1,), (1,)), ((), ())),
            preferred_element_type=f32,
        )
    need = (count > 0.5).astype(f32)
    before = mm(need, (subs(wide) < lanes(wide)).astype(f32))
    first_of = mm(before, (subs(wide) == lanes(wide) // PASS_DEV * PASS_DEV).astype(f32))
    for i in range(2 * NZ):
        in_plane = jnp.broadcast_to(plane[i : i + 1], (NZ, 128)) == subs((NZ, 128))
        is_number = jnp.broadcast_to(number[i : i + 1], wide) == subs(wide)
        found = mm(before, is_number.astype(f32)) * in_plane.astype(f32)
        fields[0, i : i + 1, :] = jnp.sum(found, axis=0, keepdims=True).astype(i32)
    place = fields[0]
    chip = (place % PLANE) % NX

    same = (subs(wide) // 32 == lanes(wide) // 32) & (subs(wide) < lanes(wide))
    rank = jnp.zeros((2 * NZ, 128), f32)
    for v in range(NX):
        here = (chip == v).astype(f32)
        rank = rank + here * mm(here, same.astype(f32))
    rank = rank.astype(i32)
    fields[1] = plane
    fields[2] = rank

    def one_max(value):
        return jnp.max(jnp.max(value, axis=1, keepdims=True), axis=0, keepdims=True)

    most_z = one_max(jnp.sum(need, axis=1, keepdims=True)).astype(i32)
    most_x = one_max(rank) + 1

    ours = (subs((NZ, 128)) == z).astype(f32)
    my_need = jnp.sum(need * ours, axis=0, keepdims=True) > 0.5
    my_rank = jnp.sum(before * ours, axis=0, keepdims=True).astype(i32)
    my_first = jnp.sum(first_of * ours, axis=0, keepdims=True).astype(i32)
    again = (my_rank - my_first) // PLANE
    lane = lanes((1, 128))
    tall = (PASS_DEV, 128)
    key = jnp.where(my_need & (lane // PASS_DEV == me), my_rank % PLANE * 2 + again, -1)
    hit = jnp.broadcast_to(key, tall) == subs(tall)
    ssel = jnp.sum(jnp.where(hit, lanes(tall) % PASS_DEV, 0), axis=1, keepdims=True)
    key = jnp.where(my_need & (my_rank % PLANE == me), my_rank // PLANE, -1)
    hit = jnp.broadcast_to(key, tall) == subs(tall)
    spot = jnp.broadcast_to(lane // PASS_DEV * 2 + again, tall)
    csel = jnp.sum(jnp.where(hit, spot, 0), axis=1, keepdims=True)
    tab_out[0:16, :] = jnp.where(
        lanes(tall) == 0, jnp.broadcast_to(csel, tall), jnp.broadcast_to(ssel, tall)
    )

    block = (subs(wide) // 32 == lanes(wide)).astype(f32)
    for half in range(2):
        at = pl.ds(2 * z + half, 1)
        g, p, k = fields[0, at, :], fields[1, at, :], fields[2, at, :]
        t = g % PLANE
        b = t % NX
        where = ((t // NX) * NZ + p) * CZS[-1] + jnp.minimum(g // PLANE, CZS[-1] - 1)
        where = where.astype(f32)
        key = jnp.where((b == x) & (k % NC == c), k // NC, -1)
        hit = jnp.broadcast_to(key, (CX, 128)) == subs((CX, 128))
        chosen = jnp.where(hit, jnp.broadcast_to(where, (CX, 128)), 0.0)
        tab_out[16 + 8 * half : 24 + 8 * half, :] = mm(chosen, block).astype(i32)
        slot = ((k % NC) * NX + b) * CX + jnp.minimum(k // NC, CX - 1)
        tab_out[32 + half : 33 + half, :] = slot
    tab_out[34:35, :] = jnp.broadcast_to(most_z, (1, 128))
    tab_out[35:36, :] = jnp.broadcast_to(most_x, (1, 128))
    tab_out[36:40, :] = jnp.zeros((4, 128), i32)
    for copy in second:
        copy.wait()


def greet(ids, slot, gain):
    vmem = pl.BlockSpec(memory_space=pltpu.VMEM)
    dma = pltpu.SemaphoreType.DMA
    return pl.pallas_call(
        greet_kernel,
        out_shape=(
            jax.ShapeDtypeStruct((2 * NZ, 128), jnp.int32),
            jax.ShapeDtypeStruct((NY, 32, 128), jnp.float32),
            jax.ShapeDtypeStruct((40, 128), jnp.int32),
        ),
        in_specs=[vmem, vmem, vmem],
        out_specs=(vmem, vmem, vmem),
        scratch_shapes=[
            pltpu.VMEM((8, 128), jnp.int32),
            pltpu.VMEM((PLANE, 8, 128), jnp.int32),
            pltpu.VMEM((8, 128), jnp.int32),
            pltpu.VMEM((NZ, 8, 128), jnp.int32),
            pltpu.VMEM((3, 2 * NZ, 128), jnp.int32),
            dma((PLANE,)),
            dma((PLANE,)),
            dma((NZ,)),
            dma((NZ,)),
            dma((NY,)),
            dma((NY,)),
        ],
        compiler_params=pltpu.CompilerParams(collective_id=0, has_side_effects=True),
        name="greet",
    )(ids, slot, gain)


def fast_kernel(
    cz, store, own_in, hid, gain, tab, out, ybuf, send, kvs, own, state, staged, gains, rs,
    ssq, box, ystage, sbox, packed, ysend, yrecv, osend, orecv, local, ssend, srecv, csend, crecv, zsend, zrecv, xsend, xrecv,
    qsend, qrecv, outsend, outrecv, outlocal, *many
):
    strips, pools, recvs = many[:STEPS], many[STEPS : 2 * STEPS], many[2 * STEPS :]
    cache, x, y, z, c = where_am_i()
    me = c * NX + x
    scale = 1.4426950408889634 / 128**0.5

    def plane_id(t):
        return (cache_at(lax.rem(t, NX), z, t // NX), y)

    def z_id(dz):
        return (cache_at(x, mod(z + dz, NZ), c), y)

    def y_id(s):
        return (cache, s)

    def step_of(i, s):
        return jnp.where(i == 2 * s, 0, jnp.where(i < 2 * s, i + 1, i))

    def part_of(q):
        return 2 * y if q == 0 else jnp.where(q - 1 < 2 * y, q - 1, q)

    barrier = pltpu.get_barrier_semaphore()
    for i in range(1, PLANE):
        pl.semaphore_signal(
            barrier, inc=1, device_id=plane_id(lax.rem(me + i, PLANE)), device_id_type=MESH
        )
    for i in range(1, NY):
        pl.semaphore_signal(
            barrier, inc=1, device_id=y_id(lax.rem(y + i, NY)), device_id_type=MESH
        )
    for dz in (1, -1):
        pl.semaphore_signal(barrier, inc=1, device_id=z_id(dz), device_id_type=MESH)
    pl.semaphore_wait(barrier, PLANE + NY)

    def local_copies():
        made = []
        for j in range(2):
            for part in range(2):
                cols = pl.ds(pl.multiple_of(part * 1024 + y * HALF + j * 128, 128), 128)
                made.append(
                    pltpu.make_async_copy(
                        store.at[:, :, cols],
                        ybuf.at[step_of(2 * y + j, y), :, :, pl.ds(part * 128, 128)],
                        local.at[2 * j + part],
                    )
                )
        for part in range(2):
            cols = pl.ds(pl.multiple_of(part * 1024 + y * HALF, HALF), HALF)
            made.append(
                pltpu.make_async_copy(
                    own_in.at[:, cols], own.at[y, :, pl.ds(part * HALF, HALF)], local.at[4 + part]
                )
            )
        return made

    def pack_copies(i, j):
        s = lax.rem(y + i, NY)
        made = []
        for part in range(2):
            cols = pl.ds(pl.multiple_of(part * 1024 + s * HALF + j * 128, 128), 128)
            made.append(
                pltpu.make_async_copy(
                    store.at[:, :, cols],
                    box.at[i - 1, j, :, :, pl.ds(part * 128, 128)],
                    packed.at[i, j, part],
                )
            )
        return made

    def scatter_copy(i, j):
        s = lax.rem(y + i, NY)
        q = step_of(2 * y + j, s)
        return pltpu.make_async_remote_copy(
            src_ref=box.at[i - 1, j],
            dst_ref=ybuf.at[q],
            send_sem=ysend.at[i, j],
            recv_sem=yrecv.at[q],
            device_id=y_id(s),
            device_id_type=MESH,
        )

    def own_scatter(i):
        s = lax.rem(y + i, NY)
        made = []
        for part in range(2):
            cols = pl.ds(pl.multiple_of(part * 1024 + s * HALF, HALF), HALF)
            made.append(
                pltpu.make_async_remote_copy(
                    src_ref=own_in.at[:, cols],
                    dst_ref=own.at[y, :, pl.ds(part * HALF, HALF)],
                    send_sem=osend.at[i, part],
                    recv_sem=orecv.at[y, part],
                    device_id=y_id(s),
                    device_id_type=MESH,
                )
            )
        return made

    def stripe(q):
        par = q % 2
        if q >= 2:
            striped(q - 2)
        ystage[...] = ybuf[q]

        def fill(i, _):
            sbox[par, i] = ystage[tab[i, 1]]
            return 0

        lax.fori_loop(0, 2 * PLANE, fill, 0)

        def push(i, _):
            t = lax.rem(me + i, PLANE)
            pltpu.make_async_remote_copy(
                src_ref=sbox.at[par, pl.ds(t * 2, 2)],
                dst_ref=strips[q].at[pl.ds(me * 2, 2)],
                send_sem=ssend.at[q],
                recv_sem=srecv.at[q],
                device_id=plane_id(t),
                device_id_type=MESH,
            ).start()
            return 0

        strips[q][pl.ds(me * 2, 2)] = sbox[par, pl.ds(me * 2, 2)]
        lax.fori_loop(1, PLANE, push, 0)

    def striped(q):
        what = strips[q].at[pl.ds(0, 2 * PLANE - 2)]
        pltpu.make_async_copy(what, what, ssend.at[q]).wait()

    def z_ref(q, plane, half):
        at = (c * NZ + plane) * CZS[-1]
        if half == 0:
            return pools[q].at[pl.ds(at, cz - cz // 2)]
        return pools[q].at[pl.ds(at + cz - cz // 2, cz // 2)]

    def z_copy(q, up, half, hop):
        where = z_ref(q, mod(z - (hop - 1), NZ) if up else mod(z + (hop - 1), NZ), half)
        return pltpu.make_async_remote_copy(
            src_ref=where,
            dst_ref=where,
            send_sem=zsend.at[q, int(up), half, hop - 1],
            recv_sem=zrecv.at[q, int(up), half, hop - 1],
            device_id=z_id(1 if up else -1),
            device_id_type=MESH,
        )

    def z_arrival(q, up, half, hop):
        where = z_ref(q, mod(z - hop, NZ) if up else mod(z + hop, NZ), half)
        return pltpu.make_async_remote_copy(
            src_ref=where,
            dst_ref=where,
            send_sem=zsend.at[q, int(up), half, hop - 1],
            recv_sem=zrecv.at[q, int(up), half, hop - 1],
            device_id=z_id(1 if up else -1),
            device_id_type=MESH,
        )

    def hops(up, half):
        return 4 if bool(up) == (half == 0) else 3

    def share(where, q):
        pltpu.make_async_remote_copy(
            src_ref=where,
            dst_ref=where,
            send_sem=csend.at[q],
            recv_sem=crecv.at[q],
            device_id=(cache_at(x, z, 1 - c), y),
            device_id_type=MESH,
        ).start()

    def compact(q):
        what = strips[q].at[pl.ds(0, 2 * PLANE - 2)]
        pltpu.make_async_copy(what, what, srecv.at[q]).wait()
        for i in range(cz):
            pools[q][(c * NZ + z) * CZS[-1] + i] = strips[q][tab[i, 0]]
        for half in range(2):
            for up in (True, False):
                z_copy(q, up, half, 1).start()
        share(pools[q].at[pl.ds((c * NZ + z) * CZS[-1], cz)], q)

    def choose(q):
        par = q % 2
        what = pools[q].at[pl.ds(0, NZ * cz)]
        pltpu.make_async_copy(what, what, crecv.at[q]).wait()
        if q >= 2:
            x_sent(q - 2)

        def fill(t, _):
            for i in range(CX):
                send[par, t, i] = pools[q][tab[16 + 8 * (t // 4) + i, lax.rem(t, 4)]]
            return 0

        lax.fori_loop(0, PLANE, fill, 0)
        recvs[q][pl.ds(me * CX, CX)] = send[par, me]

        def push(i, _):
            t = lax.rem(me + i, PLANE)
            pltpu.make_async_remote_copy(
                src_ref=send.at[par, t],
                dst_ref=recvs[q].at[pl.ds(me * CX, CX)],
                send_sem=xsend.at[q],
                recv_sem=xrecv.at[q],
                device_id=plane_id(t),
                device_id_type=MESH,
            ).start()
            return 0

        lax.fori_loop(1, PLANE, push, 0)

    def x_sent(q):
        what = send.at[q % 2, pl.ds(0, PLANE - 1)]
        pltpu.make_async_copy(what, what, xsend.at[q]).wait()

    def assemble(q):
        what = recvs[q].at[pl.ds(0, (PLANE - 1) * CX)]
        pltpu.make_async_copy(what, what, xrecv.at[q]).wait()
        part = part_of(q)

        def one(r, _):
            for n in range(NRET):
                at = tab[32 + me // 4, lax.rem(me, 4) * 32 + r * NRET + n]
                kvs[part, r, n * PT : (n + 1) * PT] = recvs[q][at]
            return 0

        lax.fori_loop(0, REQ, one, 0)

    def y_arrived(q):
        what = ybuf.at[q]
        pltpu.make_async_copy(what, what, yrecv.at[q]).wait()

    krow = lax.broadcasted_iota(jnp.int32, (OWN, 4 * QT), 0)
    qcol = lax.rem(lax.broadcasted_iota(jnp.int32, (OWN, 4 * QT), 1), QT)

    def before_layer(layer):
        @pl.when(layer != y)
        def _():
            for part in range(2):
                what = own.at[layer, :, pl.ds(part * HALF, HALF)]
                pltpu.make_async_copy(what, what, orecv.at[layer, part]).wait()

        if layer > 0:
            what = ssq.at[layer - 1, pl.ds(0, NY - 1)]
            pltpu.make_async_copy(what, what, qrecv.at[layer - 1]).wait()
            total = ssq[layer - 1, 0] + ssq[layer - 1, 1] + ssq[layer - 1, 2] + ssq[layer - 1, 3]
            total = total + pltpu.roll(total, QT, 1)
            total = total + pltpu.roll(total, 2 * QT, 1)
            rs[...] = lax.rsqrt(total * (1.0 / D) + 1e-05)

    def attend(layer, r, heads_of):
        rows = pl.ds(pl.multiple_of(r * QT, QT), QT)
        causal = krow <= qcol
        squares = jnp.zeros((1, 4 * QT), jnp.float32)
        for j in heads_of:
            part = 2 * layer + j
            wide = state[r, j].astype(jnp.float32)
            query = (wide * rs[pl.ds(r, 1), :] * gains[layer, j]).astype(jnp.bfloat16)
            far_keys = kvs[part, r, :, 0:128]
            far_vals = kvs[part, r, :, 128:256]
            near_keys = own[layer, rows, j * 128 : (j + 1) * 128]
            near_vals = own[layer, rows, HALF + j * 128 : HALF + (j + 1) * 128]
            far = jnp.dot(far_keys, query, preferred_element_type=jnp.float32)
            near = jnp.dot(near_keys, query, preferred_element_type=jnp.float32)
            near = jnp.where(causal, near, -jnp.inf)
            top = jnp.maximum(
                jnp.max(far, axis=0, keepdims=True), jnp.max(near, axis=0, keepdims=True)
            )
            far = jnp.exp2((far - top) * scale)
            near = jnp.exp2((near - top) * scale)
            total = jnp.sum(far, axis=0, keepdims=True) + jnp.sum(near, axis=0, keepdims=True)
            total = 1.0 / total
            far = (far * total).astype(jnp.bfloat16)
            near = (near * total).astype(jnp.bfloat16)
            first = (((0,), (0,)), ((), ()))
            mixed = lax.dot_general(far_vals, far, first, preferred_element_type=jnp.float32)
            mixed = mixed + lax.dot_general(
                near_vals, near, first, preferred_element_type=jnp.float32
            )
            new = (wide + mixed).astype(jnp.bfloat16)
            state[r, j] = new
            turned = new.T
            for g in range(4):
                h = 4 * j + g
                staged[layer, rows, h * 128 : (h + 1) * 128] = turned[g * QT : (g + 1) * QT]
            new = new.astype(jnp.float32)
            squares = squares + jnp.sum(new * new, axis=0, keepdims=True)
        if layer < LAYERS - 1:
            ssq[layer, y, pl.ds(r, 1), :] = squares
        width = PAIR * len(heads_of)
        cols = pl.ds(pl.multiple_of(y * WIDE + heads_of[0] * PAIR, PAIR), width)
        made = staged.at[layer, rows, pl.ds(heads_of[0] * PAIR, width)]

        @pl.when(layer == y)
        def _():
            pltpu.make_async_copy(made, out.at[rows, cols], outlocal).start()

        @pl.when(layer != y)
        def _():
            pltpu.make_async_remote_copy(
                src_ref=made,
                dst_ref=out.at[rows, cols],
                send_sem=outsend.at[layer],
                recv_sem=outrecv,
                device_id=y_id(layer),
                device_id_type=MESH,
            ).start()

    def after_layer(layer):
        for i in range(1, NY):
            pltpu.make_async_remote_copy(
                src_ref=ssq.at[layer, y],
                dst_ref=ssq.at[layer, y],
                send_sem=qsend.at[layer, i],
                recv_sem=qrecv.at[layer],
                device_id=y_id(lax.rem(y + i, NY)),
                device_id_type=MESH,
            ).start()

    def attend_rows(layer, first, count, together, heads_of=(0, 1)):
        def body(i, _):
            for u in range(together):
                attend(layer, first + i * together + u, heads_of)
            return 0

        lax.fori_loop(0, count // together, body, 0)

    own_copies = local_copies()
    for copy in own_copies[:2]:
        copy.start()
    packs = [(i, j, pack_copies(i, j)) for j in range(2) for i in (1, 3, 2)]
    for i, j, copies in packs[:3]:
        for copy in copies:
            copy.start()
    for copy in own_copies[2:]:
        copy.start()
    for i, j, copies in packs[3:]:
        for copy in copies:
            copy.start()
    own_copies[0].wait()
    own_copies[1].wait()
    stripe(0)
    for i, j, copies in packs:
        for copy in copies:
            copy.wait()

    def scatter(first, last):
        @pl.when((y >= first) & (y <= last))
        def _():
            for j in range(2):
                for i in (1, 3, 2):
                    scatter_copy(i, j).start()

    def scatter_own():
        for i in (1, 3, 2):
            for copy in own_scatter(i):
                copy.start()

    scatter(0, 1)
    compact(0)

    for layer in range(LAYERS - 1):
        ssq[layer, y] = jnp.zeros((8, 4 * QT), jnp.float32)
    mean_sq = jnp.zeros((REQ * QT, 1), jnp.float32)
    for i in range(8):
        wide = hid[:, i * 512 : (i + 1) * 512].astype(jnp.float32)
        mean_sq = mean_sq + jnp.sum(wide * wide, axis=-1, keepdims=True)
    mean_sq = jnp.broadcast_to(mean_sq * (1.0 / D), (REQ * QT, 128)).T
    mean_sq = lax.rsqrt(mean_sq + 1e-05)
    for r in range(REQ):
        part = mean_sq[0:1, r * QT : (r + 1) * QT]
        rs[r : r + 1, :] = jnp.concatenate([part] * 4, axis=1)
    rs[REQ:, :] = jnp.zeros((8 - REQ, 4 * QT), jnp.float32)
    for j in range(2):
        for r in range(REQ):
            heads = []
            for g in range(4):
                cols = pl.ds(pl.multiple_of(y * WIDE + (4 * j + g) * 128, 128), 128)
                heads.append(hid[r * QT : (r + 1) * QT, cols])
            state[r, j] = jnp.concatenate(heads, axis=0).T
        for layer in range(LAYERS):
            heads = []
            for g in range(4):
                at = gain[layer, pl.ds(y * 8 + 4 * j + g, 1), :]
                heads.append(jnp.broadcast_to(at, (QT, 128)))
            gains[layer, j] = jnp.concatenate(heads, axis=0).T

    def arrived_from_y(q):
        part = part_of(q)

        @pl.when(part != 2 * y + 1)
        def _():
            y_arrived(q)

    for copy in own_copies[2:]:
        copy.wait()
    arrived_from_y(1)
    stripe(1)
    todo = {}

    def later(slot, work):
        todo.setdefault(slot, []).append(work)

    later(0, lambda: scatter(2, 2))
    later(1, lambda: scatter(3, 3))
    later(3, scatter_own)

    for q in range(1, STEPS):
        if q >= 2:
            later(q - 1, lambda q=q: (arrived_from_y(q), stripe(q)))
        later(2 * q - 1, lambda q=q: compact(q))
    for q in range(STEPS):
        later(2 * q + 4, lambda q=q: choose(q))
    for q in range(STEPS - 1):
        later(2 * q + 6, lambda q=q: assemble(q))
    for layer in range(2):
        later(4 * layer + 10, lambda layer=layer: before_layer(layer))
        for half in range(2):
            later(
                4 * layer + 10 + 2 * half,
                lambda layer=layer, half=half: attend_rows(layer, 2 * half, 2, 1),
            )
        later(4 * layer + 12, lambda layer=layer: after_layer(layer))

    for slot in range(2 * STEPS + 3):
        for q in range(STEPS):
            hop = slot - 2 * q + 1
            if not 1 <= hop <= 4:
                continue
            for half in range(2):
                for up in (True, False):
                    if hop <= hops(up, half):
                        z_arrival(q, up, half, hop).wait_recv()
                        if hop < hops(up, half):
                            z_copy(q, up, half, hop + 1).start()
                        plane = mod(z - hop, NZ) if up else mod(z + hop, NZ)
                        share(z_ref(q, plane, half), q)
        for work in todo.get(slot, ()):
            work()

    before_layer(2)
    attend_rows(2, 0, REQ, 2)
    after_layer(2)
    before_layer(3)
    attend_rows(3, 0, REQ, 2, (0,))
    assemble(STEPS - 1)
    attend_rows(3, 0, REQ, 2, (1,))

    striped(STEPS - 2)
    striped(STEPS - 1)
    x_sent(STEPS - 2)
    x_sent(STEPS - 1)
    for q in range(STEPS):
        what = pools[q].at[pl.ds(0, NZ * cz)]
        pltpu.make_async_copy(what, what, csend.at[q]).wait()
        for up in (True, False):
            for half in range(2):
                for hop in range(1, hops(up, half) + 1):
                    z_copy(q, up, half, hop).wait_send()
    for i in range(1, NY):
        for j in range(2):
            scatter_copy(i, j).wait_send()
        for copy in own_scatter(i):
            copy.wait_send()
        for layer in range(LAYERS - 1):
            what = ssq.at[layer, y]
            pltpu.make_async_copy(what, what, qsend.at[layer, i]).wait()
    for layer in range(LAYERS):

        @pl.when(layer != y)
        def _():
            what = staged.at[layer]
            pltpu.make_async_copy(what, what, outsend.at[layer]).wait()

    what = out.at[:, pl.ds(0, 3 * WIDE)]
    pltpu.make_async_copy(what, what, outrecv).wait()
    what = out.at[:, pl.ds(0, WIDE)]
    pltpu.make_async_copy(what, what, outlocal).wait()


def fast_attend(cz, collective_id, store, own, hidden, gain, tab):
    vmem = pl.BlockSpec(memory_space=pltpu.VMEM)
    smem = pl.BlockSpec(memory_space=pltpu.SMEM)
    hbm = pl.BlockSpec(memory_space=pl.ANY)
    bf16 = jnp.bfloat16
    dma = pltpu.SemaphoreType.DMA
    return pl.pallas_call(
        functools.partial(fast_kernel, cz),
        out_shape=jax.ShapeDtypeStruct((REQ * QT, D), bf16),
        in_specs=[hbm, hbm, vmem, vmem, smem],
        out_specs=hbm,
        scratch_shapes=[
            pltpu.VMEM((STEPS, PASS_DEV, PT, ONE), bf16),
            pltpu.VMEM((2, PLANE, CX, PT, ONE), bf16),
            pltpu.VMEM((STEPS, REQ, NRET * PT, ONE), bf16),
            pltpu.VMEM((LAYERS, REQ * QT, PAIR), bf16),
            pltpu.VMEM((REQ, 2, 128, 4 * QT), bf16),
            pltpu.VMEM((LAYERS, REQ * QT, WIDE), bf16),
            pltpu.VMEM((LAYERS, 2, 128, 4 * QT), jnp.float32),
            pltpu.VMEM((8, 4 * QT), jnp.float32),
            pltpu.VMEM((LAYERS - 1, NY, 8, 4 * QT), jnp.float32),
            pltpu.VMEM((NY - 1, 2, PASS_DEV, PT, ONE), bf16),
            pltpu.VMEM((PASS_DEV, PT, ONE), bf16),
            pltpu.VMEM((2, 2 * PLANE, PT, ONE), bf16),
            dma((NY, 2, 2)),
            dma((NY, 2)),
            dma((STEPS,)),
            dma((NY, 2)),
            dma((LAYERS, 2)),
            dma((6,)),
            dma((STEPS,)),
            dma((STEPS,)),
            dma((STEPS,)),
            dma((STEPS,)),
            dma((STEPS, 2, 2, 4)),
            dma((STEPS, 2, 2, 4)),
            dma((STEPS,)),
            dma((STEPS,)),
            dma((LAYERS - 1, NY)),
            dma((LAYERS - 1,)),
            dma((LAYERS,)),
            dma(()),
            dma(()),
        ]
        + [pltpu.VMEM((PLANE * 2, PT, ONE), bf16)] * STEPS
        + [pltpu.VMEM((NC * NZ * CZS[-1], PT, ONE), bf16)] * STEPS
        + [pltpu.VMEM((PLANE * CX, PT, ONE), bf16)] * STEPS,
        compiler_params=pltpu.CompilerParams(
            collective_id=collective_id, has_side_effects=True, vmem_limit_bytes=60 * 1024 * 1024
        ),
        name="fast_attend_" + str(cz),
    )(store, own, hidden, gain, tab)


def general_kernel(
    store,
    own_in,
    hid,
    gain,
    sel,
    slots,
    out,
    pool,
    recv,
    send,
    rstage,
    stage,
    own,
    kv,
    state,
    rs,
    ssq,
    ysend,
    yrecv,
    osend,
    orecv,
    local,
    zsend,
    zrecv,
    xsend,
    xrecv,
    qsend,
    qrecv,
    outsend,
    outrecv,
    outlocal,
):
    cache, x, y, z, c = where_am_i()
    me = x * NC + c

    def plane_id(t):
        return (cache_at(t // NC, z, lax.rem(t, NC)), y)

    def z_id(dz):
        return (cache_at(x, mod(z + dz, NZ), c), y)

    def y_id(s):
        return (cache, s)

    def step_of(layer, s):
        return jnp.where(layer == s, 0, jnp.where(layer < s, layer + 1, layer))

    barrier = pltpu.get_barrier_semaphore()
    for i in range(1, PLANE):
        pl.semaphore_signal(
            barrier, inc=1, device_id=plane_id(lax.rem(me + i, PLANE)), device_id_type=MESH
        )
    for i in range(1, NY):
        pl.semaphore_signal(
            barrier, inc=1, device_id=y_id(lax.rem(y + i, NY)), device_id_type=MESH
        )
    for dz in (1, -1):
        pl.semaphore_signal(barrier, inc=1, device_id=z_id(dz), device_id_type=MESH)
    pl.semaphore_wait(barrier, PLANE + NY)

    def local_copies():
        made = []
        for part in range(2):
            cols = pl.ds(pl.multiple_of(part * 1024 + y * HALF, HALF), HALF)
            half = pl.ds(part * HALF, HALF)
            made.append(
                pltpu.make_async_copy(
                    store.at[:, :, cols], pool.at[0, z, :, :, half], local.at[part]
                )
            )
            made.append(
                pltpu.make_async_copy(
                    own_in.at[:, cols], own.at[y, :, half], local.at[2 + part]
                )
            )
        return made

    def scatter_copies(i):
        s = lax.rem(y + i, NY)
        made = []
        for part in range(2):
            cols = pl.ds(pl.multiple_of(part * 1024 + s * HALF, HALF), HALF)
            half = pl.ds(part * HALF, HALF)
            made.append(
                pltpu.make_async_remote_copy(
                    src_ref=store.at[:, :, cols],
                    dst_ref=pool.at[step_of(y, s), z, :, :, half],
                    send_sem=ysend.at[i, part],
                    recv_sem=yrecv.at[step_of(y, s), part],
                    device_id=y_id(s),
                    device_id_type=MESH,
                )
            )
            made.append(
                pltpu.make_async_remote_copy(
                    src_ref=own_in.at[:, cols],
                    dst_ref=own.at[y, :, half],
                    send_sem=osend.at[i, part],
                    recv_sem=orecv.at[y, part],
                    device_id=y_id(s),
                    device_id_type=MESH,
                )
            )
        return made

    for copy in local_copies():
        copy.start()
    for i in (1, 3, 2):
        for copy in scatter_copies(i):
            copy.start()

    def z_copy(k, up, half, hop):
        plane = mod(z - (hop - 1), NZ) if up else mod(z + (hop - 1), NZ)
        rows = pl.ds(half * 8, 8)
        where = pool.at[k, plane, rows]
        return pltpu.make_async_remote_copy(
            src_ref=where,
            dst_ref=where,
            send_sem=zsend.at[k, int(up), half, hop - 1],
            recv_sem=zrecv.at[k, int(up), half, hop - 1],
            device_id=z_id(1 if up else -1),
            device_id_type=MESH,
        )

    def z_arrival(k, up, half, hop):
        plane = mod(z - hop, NZ) if up else mod(z + hop, NZ)
        where = pool.at[k, plane, pl.ds(half * 8, 8)]
        return pltpu.make_async_remote_copy(
            src_ref=where,
            dst_ref=where,
            send_sem=zsend.at[k, int(up), half, hop - 1],
            recv_sem=zrecv.at[k, int(up), half, hop - 1],
            device_id=z_id(1 if up else -1),
            device_id_type=MESH,
        )

    def hops(up, half):
        return 4 if bool(up) == (half == 0) else 3

    def z_first(k):
        for half in range(2):
            for up in (True, False):
                z_copy(k, up, half, 1).start()

    def choose(k, plane):
        par = lax.rem(k, 2)
        stage[...] = pool[k, plane]

        def fill(t, _):
            for r in range(CAP):
                send[par, plane, t, r] = stage[sel[plane, t * CAP + r]]
            return 0

        lax.fori_loop(0, PLANE, fill, 0)
        recv[k, me, plane] = send[par, plane, me]

        def push(i, _):
            t = lax.rem(me + i, PLANE)
            pltpu.make_async_remote_copy(
                src_ref=send.at[par, plane, t],
                dst_ref=recv.at[k, me, plane],
                send_sem=xsend.at[k],
                recv_sem=xrecv.at[k],
                device_id=plane_id(t),
                device_id_type=MESH,
            ).start()
            return 0

        lax.fori_loop(1, PLANE, push, 0)

    def x_sent(k):
        what = send.at[lax.rem(k, 2), :, pl.ds(0, PLANE - 1)]
        pltpu.make_async_copy(what, what, xsend.at[k]).wait()

    def x_arrived(k):
        what = recv.at[k, pl.ds(0, PLANE - 1)]
        pltpu.make_async_copy(what, what, xrecv.at[k]).wait()

    def y_arrived(k):
        for part in range(2):
            what = pool.at[k, z, :, :, pl.ds(part * HALF, HALF)]
            pltpu.make_async_copy(what, what, yrecv.at[k, part]).wait()

    def attend(layer):
        k = step_of(layer, y)

        def lift(i, _):
            rstage[pl.ds(i * 16, 16)] = recv[k, i].reshape(16, PT, PAIR)
            return 0

        lax.fori_loop(0, PLANE, lift, 0)

        @pl.when(layer != y)
        def _():
            for part in range(2):
                what = own.at[layer, :, pl.ds(part * HALF, HALF)]
                pltpu.make_async_copy(what, what, orecv.at[layer, part]).wait()

        if layer > 0:
            what = ssq.at[layer - 1, pl.ds(0, NY - 1)]
            pltpu.make_async_copy(what, what, qrecv.at[layer - 1]).wait()
            total = ssq[layer - 1, 0] + ssq[layer - 1, 1] + ssq[layer - 1, 2] + ssq[layer - 1, 3]
            total = jnp.broadcast_to(total[0:1], (128, 256)).T
            rs[...] = lax.rsqrt(total * (1.0 / D) + 1e-05)

        row = lax.rem(lax.broadcasted_iota(jnp.int32, (4 * QT, KEYS), 0), QT)
        col = lax.broadcasted_iota(jnp.int32, (4 * QT, KEYS), 1)
        seen = (col < NRET * PT + 1 + row)

        def one(r, _):
            rows = pl.ds(pl.multiple_of(r * QT, QT), QT)
            for n in range(NRET):
                kv[n * PT : (n + 1) * PT] = rstage[slots[r * NRET + n]]
            kv[NRET * PT : NRET * PT + QT] = own[layer, rows]
            if layer == 0:
                before = hid[rows, pl.ds(pl.multiple_of(y * WIDE, WIDE), WIDE)]
            else:
                before = state[layer - 1, rows]
            wide = before.astype(jnp.float32)
            query = (wide * rs[rows, 0:1] * gain[layer : layer + 1, :]).astype(jnp.bfloat16)
            squares = jnp.zeros((QT, 128), jnp.float32)
            for j in range(2):
                heads = [4 * j + g for g in range(4)]
                qj = jnp.concatenate([query[:, h * 128 : (h + 1) * 128] for h in heads], axis=0)
                keys = kv[:, j * 128 : (j + 1) * 128]
                vals = kv[:, HALF + j * 128 : HALF + (j + 1) * 128]
                score = lax.dot_general(
                    qj, keys, (((1,), (1,)), ((), ())), preferred_element_type=jnp.float32
                )
                score = jnp.where(seen, score * (1.0 / 128**0.5), -jnp.inf)
                top = jnp.max(score, axis=-1, keepdims=True)
                expd = jnp.exp(score - top)
                total = jnp.sum(expd, axis=-1, keepdims=True)
                weight = (expd * (1.0 / total)).astype(jnp.bfloat16)
                mixed = jnp.dot(weight, vals, preferred_element_type=jnp.float32)
                for g, h in enumerate(heads):
                    new = wide[:, h * 128 : (h + 1) * 128] + mixed[g * QT : (g + 1) * QT]
                    new = new.astype(jnp.bfloat16)
                    state[layer, rows, h * 128 : (h + 1) * 128] = new
                    new = new.astype(jnp.float32)
                    squares = squares + new * new
            if layer < LAYERS - 1:
                squares = jnp.sum(squares, axis=-1, keepdims=True)
                rs[rows, :] = jnp.broadcast_to(squares, (QT, 128))
            cols = pl.ds(pl.multiple_of(y * WIDE, WIDE), WIDE)

            @pl.when(layer == y)
            def _():
                pltpu.make_async_copy(
                    state.at[layer, rows], out.at[rows, cols], outlocal
                ).start()

            @pl.when(layer != y)
            def _():
                pltpu.make_async_remote_copy(
                    src_ref=state.at[layer, rows],
                    dst_ref=out.at[rows, cols],
                    send_sem=outsend.at[layer],
                    recv_sem=outrecv,
                    device_id=y_id(layer),
                    device_id_type=MESH,
                ).start()

            return 0

        lax.fori_loop(0, REQ, one, 0)
        if layer < LAYERS - 1:
            ssq[layer, y] = rs[...].T[0:8]
            for i in range(1, NY):
                pltpu.make_async_remote_copy(
                    src_ref=ssq.at[layer, y],
                    dst_ref=ssq.at[layer, y],
                    send_sem=qsend.at[layer, i],
                    recv_sem=qrecv.at[layer],
                    device_id=y_id(lax.rem(y + i, NY)),
                    device_id_type=MESH,
                ).start()

    wide = hid[...].astype(jnp.float32)
    mean_sq = jnp.sum(wide * wide, axis=-1, keepdims=True) * (1.0 / D)
    rs[...] = jnp.broadcast_to(lax.rsqrt(mean_sq + 1e-05), (256, 128))
    kv[NRET * PT + QT :] = jnp.zeros((KEYS - NRET * PT - QT, PAIR), jnp.bfloat16)

    for copy in local_copies():
        copy.wait()
    z_first(0)

    def do_step(k):
        if k >= 2:
            x_sent(k - 2)
        choose(k, z)
        for hop in range(1, 5):
            for half in range(2):
                for up in (True, False):
                    if hop <= hops(up, half):
                        z_arrival(k, up, half, hop).wait_recv()
                        if hop < hops(up, half):
                            z_copy(k, up, half, hop + 1).start()
            if hop == 2 and k < LAYERS - 1:
                y_arrived(k + 1)
                z_first(k + 1)
            choose(k, mod(z - hop, NZ))
            if hop < 4:
                choose(k, mod(z + hop, NZ))
            if hop == 3 and k >= 2:
                if k == 2:
                    x_arrived(0)
                    x_arrived(1)
                    attend(0)
                else:
                    x_arrived(2)
                    attend(1)

    for k in range(LAYERS):
        do_step(k)
    x_arrived(3)
    attend(2)
    attend(3)

    x_sent(2)
    x_sent(3)
    for k in range(LAYERS):
        for up in (True, False):
            for half in range(2):
                for hop in range(1, hops(up, half) + 1):
                    z_copy(k, up, half, hop).wait_send()
    for i in range(1, NY):
        for copy in scatter_copies(i):
            copy.wait_send()
        for layer in range(LAYERS - 1):
            what = ssq.at[layer, y]
            pltpu.make_async_copy(what, what, qsend.at[layer, i]).wait()
    for layer in range(LAYERS):

        @pl.when(layer != y)
        def _():
            what = state.at[layer]
            pltpu.make_async_copy(what, what, outsend.at[layer]).wait()

    what = out.at[:, pl.ds(0, 3 * WIDE)]
    pltpu.make_async_copy(what, what, outrecv).wait()
    what = out.at[:, pl.ds(0, WIDE)]
    pltpu.make_async_copy(what, what, outlocal).wait()


def general_attend(store, own, hidden, gain, sel, slots):
    vmem = pl.BlockSpec(memory_space=pltpu.VMEM)
    smem = pl.BlockSpec(memory_space=pltpu.SMEM)
    hbm = pl.BlockSpec(memory_space=pl.ANY)
    bf16 = jnp.bfloat16
    dma = pltpu.SemaphoreType.DMA
    return pl.pallas_call(
        general_kernel,
        out_shape=jax.ShapeDtypeStruct((REQ * QT, D), bf16),
        in_specs=[hbm, hbm, vmem, vmem, smem, smem],
        out_specs=hbm,
        scratch_shapes=[
            pltpu.VMEM((LAYERS, NZ, PASS_DEV, PT, PAIR), bf16),
            pltpu.VMEM((LAYERS, PLANE, NZ, CAP, PT, PAIR), bf16),
            pltpu.VMEM((2, NZ, PLANE, CAP, PT, PAIR), bf16),
            pltpu.VMEM((PLANE * NZ * CAP, PT, PAIR), bf16),
            pltpu.VMEM((PASS_DEV, PT, PAIR), bf16),
            pltpu.VMEM((LAYERS, REQ * QT, PAIR), bf16),
            pltpu.VMEM((KEYS, PAIR), bf16),
            pltpu.VMEM((LAYERS, REQ * QT, WIDE), bf16),
            pltpu.VMEM((REQ * QT, 128), jnp.float32),
            pltpu.VMEM((LAYERS - 1, NY, 8, REQ * QT), jnp.float32),
            dma((NY, 2)),
            dma((LAYERS, 2)),
            dma((NY, 2)),
            dma((LAYERS, 2)),
            dma((4,)),
            dma((LAYERS, 2, 2, 4)),
            dma((LAYERS, 2, 2, 4)),
            dma((LAYERS,)),
            dma((LAYERS,)),
            dma((LAYERS - 1, NY)),
            dma((LAYERS - 1,)),
            dma((LAYERS,)),
            dma(()),
            dma(()),
        ],
        compiler_params=pltpu.CompilerParams(
            collective_id=1, has_side_effects=True, vmem_limit_bytes=60 * 1024 * 1024
        ),
        name="general_attend",
    )(store, own, hidden, gain, sel, slots)


def per_device(hidden, norm_gain, own_kv, passage_kv, retrieval, passage_slot):
    cache, x, y, z, c = where_am_i()
    ids = jnp.broadcast_to(jnp.tile(retrieval.reshape(-1), 4)[None, :], (8, 128))
    rows, gains, tab = greet(ids, passage_slot.reshape(8, 128), norm_gain)
    most_z, most_x = tab[34, 0], tab[35, 0]
    turn = jnp.arange(32, dtype=jnp.int32)

    def fast(cz, collective_id):
        def run(store, own, hidden, gains):
            return fast_attend(cz, collective_id, store, own, hidden, gains, tab)

        return run

    def general(store, own, hidden, gains):
        gain = lax.dynamic_slice(gains, (0, y * 8, 0), (NY, 8, 128)).reshape(NY, WIDE)
        near = lax.dynamic_slice(rows, (2 * z, 0), (2, 128)).reshape(NC, NX, 32)
        near = near.transpose(1, 0, 2).reshape(PLANE, 32)
        mine = x * NC + c
        owner = near // PASS_DEV
        inside = near % PASS_DEV
        source = (owner // (NZ * NC)) * NC + owner % NC
        plane = (owner // NC) % NZ
        earlier = (owner[:, None, :] == owner[:, :, None]) & (turn[None, :] < turn[:, None])
        rank = jnp.sum(earlier.astype(jnp.int32), axis=2)
        place = jnp.where(source == mine, plane * CAP + rank, -1)
        spots = jnp.arange(NZ * CAP, dtype=jnp.int32)
        sel = jnp.sum(
            jnp.where(place[:, None, :] == spots[None, :, None], inside[:, None, :], 0), axis=2
        )
        sel = sel.reshape(PLANE, NZ, CAP).transpose(1, 0, 2).reshape(NZ, PLANE * CAP)
        slot = (source * NZ + plane) * CAP + rank
        slots = lax.dynamic_slice(slot, (mine, 0), (1, 32)).reshape(32)
        return general_attend(store, own, hidden, gain, sel, slots)

    which = jnp.int32(0)
    for cz in CZS:
        which = which + (most_z > PLANE * cz).astype(jnp.int32)
    which = jnp.where(most_x > 2 * CX, len(CZS), which)
    branches = [fast(cz, 2 + i) for i, cz in enumerate(CZS)] + [general]
    done = lax.switch(which, branches, passage_kv[0], own_kv[0], hidden, gains)
    return done[None]


def solution(mesh):
    return jax.shard_map(
        per_device,
        mesh=mesh,
        in_specs=(
            P("cache", None),
            P("section", None),
            P("section", "cache", None),
            P("section", "cache", None, None),
            P("cache", None),
            P(),
        ),
        out_specs=P("section", "cache", None),
        check_vma=False,
    )
```

```python
import functools

import jax
import jax.numpy as jnp
from jax import lax
from jax.experimental import pallas as pl
from jax.experimental.pallas import tpu as pltpu
from jax.sharding import PartitionSpec as P

D = 4096
QT = 64
PT = 32
NRET = 8
NX, NZ, NC, NY = 4, 8, 2, 4
PLANE = NX * NC
PASS_DEV = 16
REQ = 4
LAYERS = 4
CAP = 2
HALF = 256
PAIR = 512
WIDE = 1024
KEYS = 384
MESH = pl.DeviceIdType.MESH
STEPS = 2 * LAYERS
ONE = 256
CZS = (11, 13)
CX = 8
OWN = 64
KV_ROWS = NRET * PT + OWN


def mod(a, n):
    return lax.rem(a + n, n)


def where_am_i():
    cache = lax.axis_index("cache")
    y = lax.axis_index("section")
    c = lax.rem(cache, NC)
    z = lax.rem(cache // NC, NZ)
    x = cache // (NC * NZ)
    return cache, x, y, z, c


def cache_at(x, z, c):
    return (x * NZ + z) * NC + c


def greet_kernel(
    ids_ref,
    slot_ref,
    gain_ref,
    rows_out,
    gain_out,
    tab_out,
    mine,
    near,
    tile,
    far,
    fields,
    psend,
    precv,
    zsend,
    zrecv,
    gsend,
    grecv,
):
    cache, x, y, z, c = where_am_i()
    me = c * NX + x
    f32, bf16, i32 = jnp.float32, jnp.bfloat16, jnp.int32

    def plane_id(i):
        t = lax.rem(me + i, PLANE)
        return (cache_at(lax.rem(t, NX), z, t // NX), y)

    def z_id(i):
        return (cache_at(x, lax.rem(z + i, NZ), c), y)

    def y_id(i):
        return (cache, lax.rem(y + i, NY))

    def lanes(shape):
        return lax.broadcasted_iota(i32, shape, len(shape) - 1)

    def subs(shape):
        return lax.broadcasted_iota(i32, shape, len(shape) - 2)

    def mm(a, b):
        return jnp.dot(a.astype(bf16), b.astype(bf16), preferred_element_type=f32)

    barrier = pltpu.get_barrier_semaphore()
    for count, peer in ((PLANE, plane_id), (NZ, z_id), (NY, y_id)):
        for i in range(1, count):
            pl.semaphore_signal(barrier, inc=1, device_id=peer(i), device_id_type=MESH)

    ids = ids_ref[0:1, :]
    hit = (jnp.broadcast_to(ids % 128, (128, 128)) == subs((128, 128))).astype(f32)
    high = mm((slot_ref[...] // 32).astype(f32), hit)
    low = mm((slot_ref[...] % 32).astype(f32), hit)
    pick = jnp.broadcast_to(ids // 128, (8, 128)) == subs((8, 128))
    found = jnp.sum(jnp.where(pick, high * 32.0 + low, 0.0), axis=0, keepdims=True)
    found = jnp.where(lanes((1, 128)) // 32 == lax.rem(me, 4), found, 0.0)
    mine[...] = jnp.broadcast_to(found, (8, 128)).astype(i32)
    for i in range(32):
        gain_out[y, i : i + 1, :] = gain_ref[:, i * 128 : (i + 1) * 128].astype(f32)

    pl.semaphore_wait(barrier, PLANE + NZ + NY - 3)
    first, second, third = [], [], []
    for i in range(1, PLANE):
        first.append(
            pltpu.make_async_remote_copy(
                src_ref=mine,
                dst_ref=near.at[me],
                send_sem=psend.at[i],
                recv_sem=precv.at[i],
                device_id=plane_id(i),
                device_id_type=MESH,
            )
        )
    for i in range(1, NY):
        second.append(
            pltpu.make_async_remote_copy(
                src_ref=gain_out.at[y],
                dst_ref=gain_out.at[y],
                send_sem=gsend.at[i],
                recv_sem=grecv.at[i],
                device_id=y_id(i),
                device_id_type=MESH,
            )
        )
    for copy in first + second:
        copy.start()
    near[me] = mine[...]
    for copy in first:
        copy.wait()
    row = subs((8, 128))
    tile[...] = jnp.where(row == 0, near[0] + near[1] + near[2] + near[3], 0) + jnp.where(
        row == 1, near[4] + near[5] + near[6] + near[7], 0
    )
    for i in range(1, NZ):
        third.append(
            pltpu.make_async_remote_copy(
                src_ref=tile,
                dst_ref=far.at[z],
                send_sem=zsend.at[i],
                recv_sem=zrecv.at[i],
                device_id=z_id(i),
                device_id_type=MESH,
            )
        )
    for copy in third:
        copy.start()
    far[z] = tile[...]
    for copy in third:
        copy.wait()
    for i in range(NZ):
        rows_out[2 * i : 2 * i + 2, :] = far[i, 0:2, :]

    rows = rows_out[...]
    owner = rows // PASS_DEV
    inside = rows % PASS_DEV
    plane = (owner // NC) % NZ
    o8 = (owner % NC) * NX + owner // (NZ * NC)
    number = o8 * PASS_DEV + inside

    wide = (128, 128)
    count = jnp.zeros((NZ, 128), f32)
    for i in range(2 * NZ):
        in_plane = jnp.broadcast_to(plane[i : i + 1], (NZ, 128)) == subs((NZ, 128))
        is_number = jnp.broadcast_to(number[i : i + 1], wide) == subs(wide)
        count = count + lax.dot_general(
            in_plane.astype(f32).astype(bf16),
            is_number.astype(f32).astype(bf16),
            (((1,), (1,)), ((), ())),
            preferred_element_type=f32,
        )
    need = (count > 0.5).astype(f32)
    before = mm(need, (subs(wide) < lanes(wide)).astype(f32))
    first_of = mm(before, (subs(wide) == lanes(wide) // PASS_DEV * PASS_DEV).astype(f32))
    for i in range(2 * NZ):
        in_plane = jnp.broadcast_to(plane[i : i + 1], (NZ, 128)) == subs((NZ, 128))
        is_number = jnp.broadcast_to(number[i : i + 1], wide) == subs(wide)
        found = mm(before, is_number.astype(f32)) * in_plane.astype(f32)
        fields[0, i : i + 1, :] = jnp.sum(found, axis=0, keepdims=True).astype(i32)
    place = fields[0]
    chip = (place % PLANE) % NX

    same = (subs(wide) // 32 == lanes(wide) // 32) & (subs(wide) < lanes(wide))
    rank = jnp.zeros((2 * NZ, 128), f32)
    for v in range(NX):
        here = (chip == v).astype(f32)
        rank = rank + here * mm(here, same.astype(f32))
    rank = rank.astype(i32)
    fields[1] = plane
    fields[2] = rank

    def one_max(value):
        return jnp.max(jnp.max(value, axis=1, keepdims=True), axis=0, keepdims=True)

    most_z = one_max(jnp.sum(need, axis=1, keepdims=True)).astype(i32)
    most_x = one_max(rank) + 1

    ours = (subs((NZ, 128)) == z).astype(f32)
    my_need = jnp.sum(need * ours, axis=0, keepdims=True) > 0.5
    my_rank = jnp.sum(before * ours, axis=0, keepdims=True).astype(i32)
    my_first = jnp.sum(first_of * ours, axis=0, keepdims=True).astype(i32)
    again = (my_rank - my_first) // PLANE
    lane = lanes((1, 128))
    tall = (PASS_DEV, 128)
    key = jnp.where(my_need & (lane // PASS_DEV == me), my_rank % PLANE * 2 + again, -1)
    hit = jnp.broadcast_to(key, tall) == subs(tall)
    ssel = jnp.sum(jnp.where(hit, lanes(tall) % PASS_DEV, 0), axis=1, keepdims=True)
    key = jnp.where(my_need & (my_rank % PLANE == me), my_rank // PLANE, -1)
    hit = jnp.broadcast_to(key, tall) == subs(tall)
    spot = jnp.broadcast_to(lane // PASS_DEV * 2 + again, tall)
    csel = jnp.sum(jnp.where(hit, spot, 0), axis=1, keepdims=True)
    tab_out[0:16, :] = jnp.where(
        lanes(tall) == 0, jnp.broadcast_to(csel, tall), jnp.broadcast_to(ssel, tall)
    )

    block = (subs(wide) // 32 == lanes(wide)).astype(f32)
    for half in range(2):
        at = pl.ds(2 * z + half, 1)
        g, p, k = fields[0, at, :], fields[1, at, :], fields[2, at, :]
        t = g % PLANE
        b = t % NX
        where = ((t // NX) * NZ + p) * CZS[-1] + jnp.minimum(g // PLANE, CZS[-1] - 1)
        where = where.astype(f32)
        key = jnp.where((b == x) & (k % NC == c), k // NC, -1)
        hit = jnp.broadcast_to(key, (CX, 128)) == subs((CX, 128))
        chosen = jnp.where(hit, jnp.broadcast_to(where, (CX, 128)), 0.0)
        tab_out[16 + 8 * half : 24 + 8 * half, :] = mm(chosen, block).astype(i32)
        slot = ((k % NC) * NX + b) * CX + jnp.minimum(k // NC, CX - 1)
        tab_out[32 + half : 33 + half, :] = slot
    tab_out[34:35, :] = jnp.broadcast_to(most_z, (1, 128))
    tab_out[35:36, :] = jnp.broadcast_to(most_x, (1, 128))
    tab_out[36:40, :] = jnp.zeros((4, 128), i32)
    for copy in second:
        copy.wait()


def greet(ids, slot, gain):
    vmem = pl.BlockSpec(memory_space=pltpu.VMEM)
    dma = pltpu.SemaphoreType.DMA
    return pl.pallas_call(
        greet_kernel,
        out_shape=(
            jax.ShapeDtypeStruct((2 * NZ, 128), jnp.int32),
            jax.ShapeDtypeStruct((NY, 32, 128), jnp.float32),
            jax.ShapeDtypeStruct((40, 128), jnp.int32),
        ),
        in_specs=[vmem, vmem, vmem],
        out_specs=(vmem, vmem, vmem),
        scratch_shapes=[
            pltpu.VMEM((8, 128), jnp.int32),
            pltpu.VMEM((PLANE, 8, 128), jnp.int32),
            pltpu.VMEM((8, 128), jnp.int32),
            pltpu.VMEM((NZ, 8, 128), jnp.int32),
            pltpu.VMEM((3, 2 * NZ, 128), jnp.int32),
            dma((PLANE,)),
            dma((PLANE,)),
            dma((NZ,)),
            dma((NZ,)),
            dma((NY,)),
            dma((NY,)),
        ],
        compiler_params=pltpu.CompilerParams(collective_id=0, has_side_effects=True),
        name="greet",
    )(ids, slot, gain)


def fast_kernel(
    cz, store, own_in, hid, gain, tab, out, ybuf, send, kvs, own, state, staged, gains, rs,
    ssq, box, ystage, sbox, packed, ysend, yrecv, osend, orecv, local, ssend, srecv, csend, crecv, zsend, zrecv, xsend, xrecv,
    qsend, qrecv, outsend, outrecv, outlocal, *many
):
    strips, pools, recvs = many[:STEPS], many[STEPS : 2 * STEPS], many[2 * STEPS :]
    cache, x, y, z, c = where_am_i()
    me = c * NX + x
    scale = 1.4426950408889634 / 128**0.5

    def plane_id(t):
        return (cache_at(lax.rem(t, NX), z, t // NX), y)

    def z_id(dz):
        return (cache_at(x, mod(z + dz, NZ), c), y)

    def y_id(s):
        return (cache, s)

    def step_of(i, s):
        return jnp.where(i == 2 * s, 0, jnp.where(i < 2 * s, i + 1, i))

    def part_of(q):
        return 2 * y if q == 0 else jnp.where(q - 1 < 2 * y, q - 1, q)

    barrier = pltpu.get_barrier_semaphore()
    for i in range(1, PLANE):
        pl.semaphore_signal(
            barrier, inc=1, device_id=plane_id(lax.rem(me + i, PLANE)), device_id_type=MESH
        )
    for i in range(1, NY):
        pl.semaphore_signal(
            barrier, inc=1, device_id=y_id(lax.rem(y + i, NY)), device_id_type=MESH
        )
    for dz in (1, -1):
        pl.semaphore_signal(barrier, inc=1, device_id=z_id(dz), device_id_type=MESH)
    pl.semaphore_wait(barrier, PLANE + NY)

    def local_copies():
        made = []
        for j in range(2):
            for part in range(2):
                cols = pl.ds(pl.multiple_of(part * 1024 + y * HALF + j * 128, 128), 128)
                made.append(
                    pltpu.make_async_copy(
                        store.at[:, :, cols],
                        ybuf.at[step_of(2 * y + j, y), :, :, pl.ds(part * 128, 128)],
                        local.at[2 * j + part],
                    )
                )
        for part in range(2):
            cols = pl.ds(pl.multiple_of(part * 1024 + y * HALF, HALF), HALF)
            made.append(
                pltpu.make_async_copy(
                    own_in.at[:, cols], own.at[y, :, pl.ds(part * HALF, HALF)], local.at[4 + part]
                )
            )
        return made

    def pack_copies(i, j):
        s = lax.rem(y + i, NY)
        made = []
        for part in range(2):
            cols = pl.ds(pl.multiple_of(part * 1024 + s * HALF + j * 128, 128), 128)
            made.append(
                pltpu.make_async_copy(
                    store.at[:, :, cols],
                    box.at[i - 1, j, :, :, pl.ds(part * 128, 128)],
                    packed.at[i, j, part],
                )
            )
        return made

    def scatter_copy(i, j):
        s = lax.rem(y + i, NY)
        q = step_of(2 * y + j, s)
        return pltpu.make_async_remote_copy(
            src_ref=box.at[i - 1, j],
            dst_ref=ybuf.at[q],
            send_sem=ysend.at[i, j],
            recv_sem=yrecv.at[q],
            device_id=y_id(s),
            device_id_type=MESH,
        )

    def own_scatter(i):
        s = lax.rem(y + i, NY)
        made = []
        for part in range(2):
            cols = pl.ds(pl.multiple_of(part * 1024 + s * HALF, HALF), HALF)
            made.append(
                pltpu.make_async_remote_copy(
                    src_ref=own_in.at[:, cols],
                    dst_ref=own.at[y, :, pl.ds(part * HALF, HALF)],
                    send_sem=osend.at[i, part],
                    recv_sem=orecv.at[y, part],
                    device_id=y_id(s),
                    device_id_type=MESH,
                )
            )
        return made

    def stripe(q):
        par = q % 2
        if q >= 2:
            striped(q - 2)
        ystage[...] = ybuf[q]

        def fill(i, _):
            sbox[par, i] = ystage[tab[i, 1]]
            return 0

        lax.fori_loop(0, 2 * PLANE, fill, 0)

        def push(i, _):
            t = lax.rem(me + i, PLANE)
            pltpu.make_async_remote_copy(
                src_ref=sbox.at[par, pl.ds(t * 2, 2)],
                dst_ref=strips[q].at[pl.ds(me * 2, 2)],
                send_sem=ssend.at[q],
                recv_sem=srecv.at[q],
                device_id=plane_id(t),
                device_id_type=MESH,
            ).start()
            return 0

        strips[q][pl.ds(me * 2, 2)] = sbox[par, pl.ds(me * 2, 2)]
        lax.fori_loop(1, PLANE, push, 0)

    def striped(q):
        what = strips[q].at[pl.ds(0, 2 * PLANE - 2)]
        pltpu.make_async_copy(what, what, ssend.at[q]).wait()

    def z_ref(q, plane, half):
        at = (c * NZ + plane) * CZS[-1]
        if half == 0:
            return pools[q].at[pl.ds(at, cz - cz // 2)]
        return pools[q].at[pl.ds(at + cz - cz // 2, cz // 2)]

    def z_copy(q, up, half, hop):
        where = z_ref(q, mod(z - (hop - 1), NZ) if up else mod(z + (hop - 1), NZ), half)
        return pltpu.make_async_remote_copy(
            src_ref=where,
            dst_ref=where,
            send_sem=zsend.at[q, int(up), half, hop - 1],
            recv_sem=zrecv.at[q, int(up), half, hop - 1],
            device_id=z_id(1 if up else -1),
            device_id_type=MESH,
        )

    def z_arrival(q, up, half, hop):
        where = z_ref(q, mod(z - hop, NZ) if up else mod(z + hop, NZ), half)
        return pltpu.make_async_remote_copy(
            src_ref=where,
            dst_ref=where,
            send_sem=zsend.at[q, int(up), half, hop - 1],
            recv_sem=zrecv.at[q, int(up), half, hop - 1],
            device_id=z_id(1 if up else -1),
            device_id_type=MESH,
        )

    def hops(up, half):
        return 4 if bool(up) == (half == 0) else 3

    def share(where, q):
        pltpu.make_async_remote_copy(
            src_ref=where,
            dst_ref=where,
            send_sem=csend.at[q],
            recv_sem=crecv.at[q],
            device_id=(cache_at(x, z, 1 - c), y),
            device_id_type=MESH,
        ).start()

    def compact(q):
        what = strips[q].at[pl.ds(0, 2 * PLANE - 2)]
        pltpu.make_async_copy(what, what, srecv.at[q]).wait()
        for i in range(cz):
            pools[q][(c * NZ + z) * CZS[-1] + i] = strips[q][tab[i, 0]]
        for half in range(2):
            for up in (True, False):
                z_copy(q, up, half, 1).start()
        share(pools[q].at[pl.ds((c * NZ + z) * CZS[-1], cz)], q)

    def choose(q):
        par = q % 2
        what = pools[q].at[pl.ds(0, NZ * cz)]
        pltpu.make_async_copy(what, what, crecv.at[q]).wait()
        if q >= 2:
            x_sent(q - 2)

        def fill(t, _):
            for i in range(CX):
                send[par, t, i] = pools[q][tab[16 + 8 * (t // 4) + i, lax.rem(t, 4)]]
            return 0

        lax.fori_loop(0, PLANE, fill, 0)
        recvs[q][pl.ds(me * CX, CX)] = send[par, me]

        def push(i, _):
            t = lax.rem(me + i, PLANE)
            pltpu.make_async_remote_copy(
                src_ref=send.at[par, t],
                dst_ref=recvs[q].at[pl.ds(me * CX, CX)],
                send_sem=xsend.at[q],
                recv_sem=xrecv.at[q],
                device_id=plane_id(t),
                device_id_type=MESH,
            ).start()
            return 0

        lax.fori_loop(1, PLANE, push, 0)

    def x_sent(q):
        what = send.at[q % 2, pl.ds(0, PLANE - 1)]
        pltpu.make_async_copy(what, what, xsend.at[q]).wait()

    def assemble(q):
        what = recvs[q].at[pl.ds(0, (PLANE - 1) * CX)]
        pltpu.make_async_copy(what, what, xrecv.at[q]).wait()
        part = part_of(q)

        def one(r, _):
            for n in range(NRET):
                at = tab[32 + me // 4, lax.rem(me, 4) * 32 + r * NRET + n]
                kvs[part, r, n * PT : (n + 1) * PT] = recvs[q][at]
            return 0

        lax.fori_loop(0, REQ, one, 0)

    def y_arrived(q):
        what = ybuf.at[q]
        pltpu.make_async_copy(what, what, yrecv.at[q]).wait()

    krow = lax.broadcasted_iota(jnp.int32, (OWN, 4 * QT), 0)
    qcol = lax.rem(lax.broadcasted_iota(jnp.int32, (OWN, 4 * QT), 1), QT)

    def before_layer(layer):
        @pl.when(layer != y)
        def _():
            for part in range(2):
                what = own.at[layer, :, pl.ds(part * HALF, HALF)]
                pltpu.make_async_copy(what, what, orecv.at[layer, part]).wait()

        if layer > 0:
            what = ssq.at[layer - 1, pl.ds(0, NY - 1)]
            pltpu.make_async_copy(what, what, qrecv.at[layer - 1]).wait()
            total = ssq[layer - 1, 0] + ssq[layer - 1, 1] + ssq[layer - 1, 2] + ssq[layer - 1, 3]
            total = total + pltpu.roll(total, QT, 1)
            total = total + pltpu.roll(total, 2 * QT, 1)
            rs[...] = lax.rsqrt(total * (1.0 / D) + 1e-05)

    def attend(layer, r, heads_of):
        rows = pl.ds(pl.multiple_of(r * QT, QT), QT)
        causal = krow <= qcol
        squares = jnp.zeros((1, 4 * QT), jnp.float32)
        for j in heads_of:
            part = 2 * layer + j
            wide = state[r, j].astype(jnp.float32)
            query = (wide * rs[pl.ds(r, 1), :] * gains[layer, j]).astype(jnp.bfloat16)
            far_keys = kvs[part, r, :, 0:128]
            far_vals = kvs[part, r, :, 128:256]
            near_keys = own[layer, rows, j * 128 : (j + 1) * 128]
            near_vals = own[layer, rows, HALF + j * 128 : HALF + (j + 1) * 128]
            far = jnp.dot(far_keys, query, preferred_element_type=jnp.float32)
            near = jnp.dot(near_keys, query, preferred_element_type=jnp.float32)
            near = jnp.where(causal, near, -jnp.inf)
            top = jnp.maximum(
                jnp.max(far, axis=0, keepdims=True), jnp.max(near, axis=0, keepdims=True)
            )
            far = jnp.exp2((far - top) * scale)
            near = jnp.exp2((near - top) * scale)
            total = jnp.sum(far, axis=0, keepdims=True) + jnp.sum(near, axis=0, keepdims=True)
            total = 1.0 / total
            far = (far * total).astype(jnp.bfloat16)
            near = (near * total).astype(jnp.bfloat16)
            first = (((0,), (0,)), ((), ()))
            mixed = lax.dot_general(far_vals, far, first, preferred_element_type=jnp.float32)
            mixed = mixed + lax.dot_general(
                near_vals, near, first, preferred_element_type=jnp.float32
            )
            new = (wide + mixed).astype(jnp.bfloat16)
            state[r, j] = new
            turned = new.T
            for g in range(4):
                h = 4 * j + g
                staged[layer, rows, h * 128 : (h + 1) * 128] = turned[g * QT : (g + 1) * QT]
            new = new.astype(jnp.float32)
            squares = squares + jnp.sum(new * new, axis=0, keepdims=True)
        if layer < LAYERS - 1:
            ssq[layer, y, pl.ds(r, 1), :] = squares
        width = PAIR * len(heads_of)
        cols = pl.ds(pl.multiple_of(y * WIDE + heads_of[0] * PAIR, PAIR), width)
        made = staged.at[layer, rows, pl.ds(heads_of[0] * PAIR, width)]

        @pl.when(layer == y)
        def _():
            pltpu.make_async_copy(made, out.at[rows, cols], outlocal).start()

        @pl.when(layer != y)
        def _():
            pltpu.make_async_remote_copy(
                src_ref=made,
                dst_ref=out.at[rows, cols],
                send_sem=outsend.at[layer],
                recv_sem=outrecv,
                device_id=y_id(layer),
                device_id_type=MESH,
            ).start()

    def after_layer(layer):
        for i in range(1, NY):
            pltpu.make_async_remote_copy(
                src_ref=ssq.at[layer, y],
                dst_ref=ssq.at[layer, y],
                send_sem=qsend.at[layer, i],
                recv_sem=qrecv.at[layer],
                device_id=y_id(lax.rem(y + i, NY)),
                device_id_type=MESH,
            ).start()

    def attend_rows(layer, first, count, together, heads_of=(0, 1)):
        def body(i, _):
            for u in range(together):
                attend(layer, first + i * together + u, heads_of)
            return 0

        lax.fori_loop(0, count // together, body, 0)

    own_copies = local_copies()
    for copy in own_copies[:2]:
        copy.start()
    packs = [(i, j, pack_copies(i, j)) for j in range(2) for i in (1, 3, 2)]
    for i, j, copies in packs[:3]:
        for copy in copies:
            copy.start()
    for copy in own_copies[2:]:
        copy.start()
    for i, j, copies in packs[3:]:
        for copy in copies:
            copy.start()
    own_copies[0].wait()
    own_copies[1].wait()
    stripe(0)
    for i, j, copies in packs:
        for copy in copies:
            copy.wait()

    def scatter(first, last):
        @pl.when((y >= first) & (y <= last))
        def _():
            for j in range(2):
                for i in (1, 3, 2):
                    scatter_copy(i, j).start()

    def scatter_own():
        for i in (1, 3, 2):
            for copy in own_scatter(i):
                copy.start()

    scatter(0, 1)
    compact(0)

    for layer in range(LAYERS - 1):
        ssq[layer, y] = jnp.zeros((8, 4 * QT), jnp.float32)
    mean_sq = jnp.zeros((REQ * QT, 1), jnp.float32)
    for i in range(8):
        wide = hid[:, i * 512 : (i + 1) * 512].astype(jnp.float32)
        mean_sq = mean_sq + jnp.sum(wide * wide, axis=-1, keepdims=True)
    mean_sq = jnp.broadcast_to(mean_sq * (1.0 / D), (REQ * QT, 128)).T
    mean_sq = lax.rsqrt(mean_sq + 1e-05)
    for r in range(REQ):
        part = mean_sq[0:1, r * QT : (r + 1) * QT]
        rs[r : r + 1, :] = jnp.concatenate([part] * 4, axis=1)
    rs[REQ:, :] = jnp.zeros((8 - REQ, 4 * QT), jnp.float32)
    for j in range(2):
        for r in range(REQ):
            heads = []
            for g in range(4):
                cols = pl.ds(pl.multiple_of(y * WIDE + (4 * j + g) * 128, 128), 128)
                heads.append(hid[r * QT : (r + 1) * QT, cols])
            state[r, j] = jnp.concatenate(heads, axis=0).T
        for layer in range(LAYERS):
            heads = []
            for g in range(4):
                at = gain[layer, pl.ds(y * 8 + 4 * j + g, 1), :]
                heads.append(jnp.broadcast_to(at, (QT, 128)))
            gains[layer, j] = jnp.concatenate(heads, axis=0).T

    def arrived_from_y(q):
        part = part_of(q)

        @pl.when(part != 2 * y + 1)
        def _():
            y_arrived(q)

    for copy in own_copies[2:]:
        copy.wait()
    arrived_from_y(1)
    stripe(1)
    todo = {}

    def later(slot, work):
        todo.setdefault(slot, []).append(work)

    later(0, lambda: scatter(2, 2))
    later(1, lambda: scatter(3, 3))
    later(3, scatter_own)

    for q in range(1, STEPS):
        if q >= 2:
            later(q - 1, lambda q=q: (arrived_from_y(q), stripe(q)))
        later(2 * q - 1, lambda q=q: compact(q))
    for q in range(STEPS):
        later(2 * q + 3, lambda q=q: choose(q))
    for q in range(STEPS - 1):
        later(2 * q + 6, lambda q=q: assemble(q))
    for layer in range(2):
        later(4 * layer + 10, lambda layer=layer: before_layer(layer))
        for half in range(2):
            later(
                4 * layer + 10 + 2 * half,
                lambda layer=layer, half=half: attend_rows(layer, 2 * half, 2, 1),
            )
        later(4 * layer + 12, lambda layer=layer: after_layer(layer))

    for slot in range(2 * STEPS + 3):
        for q in range(STEPS):
            hop = slot - 2 * q + 1
            if not 1 <= hop <= 4:
                continue
            for half in range(2):
                for up in (True, False):
                    if hop <= hops(up, half):
                        z_arrival(q, up, half, hop).wait_recv()
                        if hop < hops(up, half):
                            z_copy(q, up, half, hop + 1).start()
                        plane = mod(z - hop, NZ) if up else mod(z + hop, NZ)
                        share(z_ref(q, plane, half), q)
        for work in todo.get(slot, ()):
            work()

    before_layer(2)
    attend_rows(2, 0, REQ, 2)
    after_layer(2)
    before_layer(3)
    attend_rows(3, 0, REQ, 2, (0,))
    assemble(STEPS - 1)
    attend_rows(3, 0, REQ, 2, (1,))

    striped(STEPS - 2)
    striped(STEPS - 1)
    x_sent(STEPS - 2)
    x_sent(STEPS - 1)
    for q in range(STEPS):
        what = pools[q].at[pl.ds(0, NZ * cz)]
        pltpu.make_async_copy(what, what, csend.at[q]).wait()
        for up in (True, False):
            for half in range(2):
                for hop in range(1, hops(up, half) + 1):
                    z_copy(q, up, half, hop).wait_send()
    for i in range(1, NY):
        for j in range(2):
            scatter_copy(i, j).wait_send()
        for copy in own_scatter(i):
            copy.wait_send()
        for layer in range(LAYERS - 1):
            what = ssq.at[layer, y]
            pltpu.make_async_copy(what, what, qsend.at[layer, i]).wait()
    for layer in range(LAYERS):

        @pl.when(layer != y)
        def _():
            what = staged.at[layer]
            pltpu.make_async_copy(what, what, outsend.at[layer]).wait()

    what = out.at[:, pl.ds(0, 3 * WIDE)]
    pltpu.make_async_copy(what, what, outrecv).wait()
    what = out.at[:, pl.ds(0, WIDE)]
    pltpu.make_async_copy(what, what, outlocal).wait()


def fast_attend(cz, collective_id, store, own, hidden, gain, tab):
    vmem = pl.BlockSpec(memory_space=pltpu.VMEM)
    smem = pl.BlockSpec(memory_space=pltpu.SMEM)
    hbm = pl.BlockSpec(memory_space=pl.ANY)
    bf16 = jnp.bfloat16
    dma = pltpu.SemaphoreType.DMA
    return pl.pallas_call(
        functools.partial(fast_kernel, cz),
        out_shape=jax.ShapeDtypeStruct((REQ * QT, D), bf16),
        in_specs=[hbm, hbm, vmem, vmem, smem],
        out_specs=hbm,
        scratch_shapes=[
            pltpu.VMEM((STEPS, PASS_DEV, PT, ONE), bf16),
            pltpu.VMEM((2, PLANE, CX, PT, ONE), bf16),
            pltpu.VMEM((STEPS, REQ, NRET * PT, ONE), bf16),
            pltpu.VMEM((LAYERS, REQ * QT, PAIR), bf16),
            pltpu.VMEM((REQ, 2, 128, 4 * QT), bf16),
            pltpu.VMEM((LAYERS, REQ * QT, WIDE), bf16),
            pltpu.VMEM((LAYERS, 2, 128, 4 * QT), jnp.float32),
            pltpu.VMEM((8, 4 * QT), jnp.float32),
            pltpu.VMEM((LAYERS - 1, NY, 8, 4 * QT), jnp.float32),
            pltpu.VMEM((NY - 1, 2, PASS_DEV, PT, ONE), bf16),
            pltpu.VMEM((PASS_DEV, PT, ONE), bf16),
            pltpu.VMEM((2, 2 * PLANE, PT, ONE), bf16),
            dma((NY, 2, 2)),
            dma((NY, 2)),
            dma((STEPS,)),
            dma((NY, 2)),
            dma((LAYERS, 2)),
            dma((6,)),
            dma((STEPS,)),
            dma((STEPS,)),
            dma((STEPS,)),
            dma((STEPS,)),
            dma((STEPS, 2, 2, 4)),
            dma((STEPS, 2, 2, 4)),
            dma((STEPS,)),
            dma((STEPS,)),
            dma((LAYERS - 1, NY)),
            dma((LAYERS - 1,)),
            dma((LAYERS,)),
            dma(()),
            dma(()),
        ]
        + [pltpu.VMEM((PLANE * 2, PT, ONE), bf16)] * STEPS
        + [pltpu.VMEM((NC * NZ * CZS[-1], PT, ONE), bf16)] * STEPS
        + [pltpu.VMEM((PLANE * CX, PT, ONE), bf16)] * STEPS,
        compiler_params=pltpu.CompilerParams(
            collective_id=collective_id, has_side_effects=True, vmem_limit_bytes=60 * 1024 * 1024
        ),
        name="fast_attend_" + str(cz),
    )(store, own, hidden, gain, tab)


def general_kernel(
    store,
    own_in,
    hid,
    gain,
    sel,
    slots,
    out,
    pool,
    recv,
    send,
    rstage,
    stage,
    own,
    kv,
    state,
    rs,
    ssq,
    ysend,
    yrecv,
    osend,
    orecv,
    local,
    zsend,
    zrecv,
    xsend,
    xrecv,
    qsend,
    qrecv,
    outsend,
    outrecv,
    outlocal,
):
    cache, x, y, z, c = where_am_i()
    me = x * NC + c

    def plane_id(t):
        return (cache_at(t // NC, z, lax.rem(t, NC)), y)

    def z_id(dz):
        return (cache_at(x, mod(z + dz, NZ), c), y)

    def y_id(s):
        return (cache, s)

    def step_of(layer, s):
        return jnp.where(layer == s, 0, jnp.where(layer < s, layer + 1, layer))

    barrier = pltpu.get_barrier_semaphore()
    for i in range(1, PLANE):
        pl.semaphore_signal(
            barrier, inc=1, device_id=plane_id(lax.rem(me + i, PLANE)), device_id_type=MESH
        )
    for i in range(1, NY):
        pl.semaphore_signal(
            barrier, inc=1, device_id=y_id(lax.rem(y + i, NY)), device_id_type=MESH
        )
    for dz in (1, -1):
        pl.semaphore_signal(barrier, inc=1, device_id=z_id(dz), device_id_type=MESH)
    pl.semaphore_wait(barrier, PLANE + NY)

    def local_copies():
        made = []
        for part in range(2):
            cols = pl.ds(pl.multiple_of(part * 1024 + y * HALF, HALF), HALF)
            half = pl.ds(part * HALF, HALF)
            made.append(
                pltpu.make_async_copy(
                    store.at[:, :, cols], pool.at[0, z, :, :, half], local.at[part]
                )
            )
            made.append(
                pltpu.make_async_copy(
                    own_in.at[:, cols], own.at[y, :, half], local.at[2 + part]
                )
            )
        return made

    def scatter_copies(i):
        s = lax.rem(y + i, NY)
        made = []
        for part in range(2):
            cols = pl.ds(pl.multiple_of(part * 1024 + s * HALF, HALF), HALF)
            half = pl.ds(part * HALF, HALF)
            made.append(
                pltpu.make_async_remote_copy(
                    src_ref=store.at[:, :, cols],
                    dst_ref=pool.at[step_of(y, s), z, :, :, half],
                    send_sem=ysend.at[i, part],
                    recv_sem=yrecv.at[step_of(y, s), part],
                    device_id=y_id(s),
                    device_id_type=MESH,
                )
            )
            made.append(
                pltpu.make_async_remote_copy(
                    src_ref=own_in.at[:, cols],
                    dst_ref=own.at[y, :, half],
                    send_sem=osend.at[i, part],
                    recv_sem=orecv.at[y, part],
                    device_id=y_id(s),
                    device_id_type=MESH,
                )
            )
        return made

    for copy in local_copies():
        copy.start()
    for i in (1, 3, 2):
        for copy in scatter_copies(i):
            copy.start()

    def z_copy(k, up, half, hop):
        plane = mod(z - (hop - 1), NZ) if up else mod(z + (hop - 1), NZ)
        rows = pl.ds(half * 8, 8)
        where = pool.at[k, plane, rows]
        return pltpu.make_async_remote_copy(
            src_ref=where,
            dst_ref=where,
            send_sem=zsend.at[k, int(up), half, hop - 1],
            recv_sem=zrecv.at[k, int(up), half, hop - 1],
            device_id=z_id(1 if up else -1),
            device_id_type=MESH,
        )

    def z_arrival(k, up, half, hop):
        plane = mod(z - hop, NZ) if up else mod(z + hop, NZ)
        where = pool.at[k, plane, pl.ds(half * 8, 8)]
        return pltpu.make_async_remote_copy(
            src_ref=where,
            dst_ref=where,
            send_sem=zsend.at[k, int(up), half, hop - 1],
            recv_sem=zrecv.at[k, int(up), half, hop - 1],
            device_id=z_id(1 if up else -1),
            device_id_type=MESH,
        )

    def hops(up, half):
        return 4 if bool(up) == (half == 0) else 3

    def z_first(k):
        for half in range(2):
            for up in (True, False):
                z_copy(k, up, half, 1).start()

    def choose(k, plane):
        par = lax.rem(k, 2)
        stage[...] = pool[k, plane]

        def fill(t, _):
            for r in range(CAP):
                send[par, plane, t, r] = stage[sel[plane, t * CAP + r]]
            return 0

        lax.fori_loop(0, PLANE, fill, 0)
        recv[k, me, plane] = send[par, plane, me]

        def push(i, _):
            t = lax.rem(me + i, PLANE)
            pltpu.make_async_remote_copy(
                src_ref=send.at[par, plane, t],
                dst_ref=recv.at[k, me, plane],
                send_sem=xsend.at[k],
                recv_sem=xrecv.at[k],
                device_id=plane_id(t),
                device_id_type=MESH,
            ).start()
            return 0

        lax.fori_loop(1, PLANE, push, 0)

    def x_sent(k):
        what = send.at[lax.rem(k, 2), :, pl.ds(0, PLANE - 1)]
        pltpu.make_async_copy(what, what, xsend.at[k]).wait()

    def x_arrived(k):
        what = recv.at[k, pl.ds(0, PLANE - 1)]
        pltpu.make_async_copy(what, what, xrecv.at[k]).wait()

    def y_arrived(k):
        for part in range(2):
            what = pool.at[k, z, :, :, pl.ds(part * HALF, HALF)]
            pltpu.make_async_copy(what, what, yrecv.at[k, part]).wait()

    def attend(layer):
        k = step_of(layer, y)

        def lift(i, _):
            rstage[pl.ds(i * 16, 16)] = recv[k, i].reshape(16, PT, PAIR)
            return 0

        lax.fori_loop(0, PLANE, lift, 0)

        @pl.when(layer != y)
        def _():
            for part in range(2):
                what = own.at[layer, :, pl.ds(part * HALF, HALF)]
                pltpu.make_async_copy(what, what, orecv.at[layer, part]).wait()

        if layer > 0:
            what = ssq.at[layer - 1, pl.ds(0, NY - 1)]
            pltpu.make_async_copy(what, what, qrecv.at[layer - 1]).wait()
            total = ssq[layer - 1, 0] + ssq[layer - 1, 1] + ssq[layer - 1, 2] + ssq[layer - 1, 3]
            total = jnp.broadcast_to(total[0:1], (128, 256)).T
            rs[...] = lax.rsqrt(total * (1.0 / D) + 1e-05)

        row = lax.rem(lax.broadcasted_iota(jnp.int32, (4 * QT, KEYS), 0), QT)
        col = lax.broadcasted_iota(jnp.int32, (4 * QT, KEYS), 1)
        seen = (col < NRET * PT + 1 + row)

        def one(r, _):
            rows = pl.ds(pl.multiple_of(r * QT, QT), QT)
            for n in range(NRET):
                kv[n * PT : (n + 1) * PT] = rstage[slots[r * NRET + n]]
            kv[NRET * PT : NRET * PT + QT] = own[layer, rows]
            if layer == 0:
                before = hid[rows, pl.ds(pl.multiple_of(y * WIDE, WIDE), WIDE)]
            else:
                before = state[layer - 1, rows]
            wide = before.astype(jnp.float32)
            query = (wide * rs[rows, 0:1] * gain[layer : layer + 1, :]).astype(jnp.bfloat16)
            squares = jnp.zeros((QT, 128), jnp.float32)
            for j in range(2):
                heads = [4 * j + g for g in range(4)]
                qj = jnp.concatenate([query[:, h * 128 : (h + 1) * 128] for h in heads], axis=0)
                keys = kv[:, j * 128 : (j + 1) * 128]
                vals = kv[:, HALF + j * 128 : HALF + (j + 1) * 128]
                score = lax.dot_general(
                    qj, keys, (((1,), (1,)), ((), ())), preferred_element_type=jnp.float32
                )
                score = jnp.where(seen, score * (1.0 / 128**0.5), -jnp.inf)
                top = jnp.max(score, axis=-1, keepdims=True)
                expd = jnp.exp(score - top)
                total = jnp.sum(expd, axis=-1, keepdims=True)
                weight = (expd * (1.0 / total)).astype(jnp.bfloat16)
                mixed = jnp.dot(weight, vals, preferred_element_type=jnp.float32)
                for g, h in enumerate(heads):
                    new = wide[:, h * 128 : (h + 1) * 128] + mixed[g * QT : (g + 1) * QT]
                    new = new.astype(jnp.bfloat16)
                    state[layer, rows, h * 128 : (h + 1) * 128] = new
                    new = new.astype(jnp.float32)
                    squares = squares + new * new
            if layer < LAYERS - 1:
                squares = jnp.sum(squares, axis=-1, keepdims=True)
                rs[rows, :] = jnp.broadcast_to(squares, (QT, 128))
            cols = pl.ds(pl.multiple_of(y * WIDE, WIDE), WIDE)

            @pl.when(layer == y)
            def _():
                pltpu.make_async_copy(
                    state.at[layer, rows], out.at[rows, cols], outlocal
                ).start()

            @pl.when(layer != y)
            def _():
                pltpu.make_async_remote_copy(
                    src_ref=state.at[layer, rows],
                    dst_ref=out.at[rows, cols],
                    send_sem=outsend.at[layer],
                    recv_sem=outrecv,
                    device_id=y_id(layer),
                    device_id_type=MESH,
                ).start()

            return 0

        lax.fori_loop(0, REQ, one, 0)
        if layer < LAYERS - 1:
            ssq[layer, y] = rs[...].T[0:8]
            for i in range(1, NY):
                pltpu.make_async_remote_copy(
                    src_ref=ssq.at[layer, y],
                    dst_ref=ssq.at[layer, y],
                    send_sem=qsend.at[layer, i],
                    recv_sem=qrecv.at[layer],
                    device_id=y_id(lax.rem(y + i, NY)),
                    device_id_type=MESH,
                ).start()

    wide = hid[...].astype(jnp.float32)
    mean_sq = jnp.sum(wide * wide, axis=-1, keepdims=True) * (1.0 / D)
    rs[...] = jnp.broadcast_to(lax.rsqrt(mean_sq + 1e-05), (256, 128))
    kv[NRET * PT + QT :] = jnp.zeros((KEYS - NRET * PT - QT, PAIR), jnp.bfloat16)

    for copy in local_copies():
        copy.wait()
    z_first(0)

    def do_step(k):
        if k >= 2:
            x_sent(k - 2)
        choose(k, z)
        for hop in range(1, 5):
            for half in range(2):
                for up in (True, False):
                    if hop <= hops(up, half):
                        z_arrival(k, up, half, hop).wait_recv()
                        if hop < hops(up, half):
                            z_copy(k, up, half, hop + 1).start()
            if hop == 2 and k < LAYERS - 1:
                y_arrived(k + 1)
                z_first(k + 1)
            choose(k, mod(z - hop, NZ))
            if hop < 4:
                choose(k, mod(z + hop, NZ))
            if hop == 3 and k >= 2:
                if k == 2:
                    x_arrived(0)
                    x_arrived(1)
                    attend(0)
                else:
                    x_arrived(2)
                    attend(1)

    for k in range(LAYERS):
        do_step(k)
    x_arrived(3)
    attend(2)
    attend(3)

    x_sent(2)
    x_sent(3)
    for k in range(LAYERS):
        for up in (True, False):
            for half in range(2):
                for hop in range(1, hops(up, half) + 1):
                    z_copy(k, up, half, hop).wait_send()
    for i in range(1, NY):
        for copy in scatter_copies(i):
            copy.wait_send()
        for layer in range(LAYERS - 1):
            what = ssq.at[layer, y]
            pltpu.make_async_copy(what, what, qsend.at[layer, i]).wait()
    for layer in range(LAYERS):

        @pl.when(layer != y)
        def _():
            what = state.at[layer]
            pltpu.make_async_copy(what, what, outsend.at[layer]).wait()

    what = out.at[:, pl.ds(0, 3 * WIDE)]
    pltpu.make_async_copy(what, what, outrecv).wait()
    what = out.at[:, pl.ds(0, WIDE)]
    pltpu.make_async_copy(what, what, outlocal).wait()


def general_attend(store, own, hidden, gain, sel, slots):
    vmem = pl.BlockSpec(memory_space=pltpu.VMEM)
    smem = pl.BlockSpec(memory_space=pltpu.SMEM)
    hbm = pl.BlockSpec(memory_space=pl.ANY)
    bf16 = jnp.bfloat16
    dma = pltpu.SemaphoreType.DMA
    return pl.pallas_call(
        general_kernel,
        out_shape=jax.ShapeDtypeStruct((REQ * QT, D), bf16),
        in_specs=[hbm, hbm, vmem, vmem, smem, smem],
        out_specs=hbm,
        scratch_shapes=[
            pltpu.VMEM((LAYERS, NZ, PASS_DEV, PT, PAIR), bf16),
            pltpu.VMEM((LAYERS, PLANE, NZ, CAP, PT, PAIR), bf16),
            pltpu.VMEM((2, NZ, PLANE, CAP, PT, PAIR), bf16),
            pltpu.VMEM((PLANE * NZ * CAP, PT, PAIR), bf16),
            pltpu.VMEM((PASS_DEV, PT, PAIR), bf16),
            pltpu.VMEM((LAYERS, REQ * QT, PAIR), bf16),
            pltpu.VMEM((KEYS, PAIR), bf16),
            pltpu.VMEM((LAYERS, REQ * QT, WIDE), bf16),
            pltpu.VMEM((REQ * QT, 128), jnp.float32),
            pltpu.VMEM((LAYERS - 1, NY, 8, REQ * QT), jnp.float32),
            dma((NY, 2)),
            dma((LAYERS, 2)),
            dma((NY, 2)),
            dma((LAYERS, 2)),
            dma((4,)),
            dma((LAYERS, 2, 2, 4)),
            dma((LAYERS, 2, 2, 4)),
            dma((LAYERS,)),
            dma((LAYERS,)),
            dma((LAYERS - 1, NY)),
            dma((LAYERS - 1,)),
            dma((LAYERS,)),
            dma(()),
            dma(()),
        ],
        compiler_params=pltpu.CompilerParams(
            collective_id=1, has_side_effects=True, vmem_limit_bytes=60 * 1024 * 1024
        ),
        name="general_attend",
    )(store, own, hidden, gain, sel, slots)


def per_device(hidden, norm_gain, own_kv, passage_kv, retrieval, passage_slot):
    cache, x, y, z, c = where_am_i()
    ids = jnp.broadcast_to(jnp.tile(retrieval.reshape(-1), 4)[None, :], (8, 128))
    rows, gains, tab = greet(ids, passage_slot.reshape(8, 128), norm_gain)
    most_z, most_x = tab[34, 0], tab[35, 0]
    turn = jnp.arange(32, dtype=jnp.int32)

    def fast(cz, collective_id):
        def run(store, own, hidden, gains):
            return fast_attend(cz, collective_id, store, own, hidden, gains, tab)

        return run

    def general(store, own, hidden, gains):
        gain = lax.dynamic_slice(gains, (0, y * 8, 0), (NY, 8, 128)).reshape(NY, WIDE)
        near = lax.dynamic_slice(rows, (2 * z, 0), (2, 128)).reshape(NC, NX, 32)
        near = near.transpose(1, 0, 2).reshape(PLANE, 32)
        mine = x * NC + c
        owner = near // PASS_DEV
        inside = near % PASS_DEV
        source = (owner // (NZ * NC)) * NC + owner % NC
        plane = (owner // NC) % NZ
        earlier = (owner[:, None, :] == owner[:, :, None]) & (turn[None, :] < turn[:, None])
        rank = jnp.sum(earlier.astype(jnp.int32), axis=2)
        place = jnp.where(source == mine, plane * CAP + rank, -1)
        spots = jnp.arange(NZ * CAP, dtype=jnp.int32)
        sel = jnp.sum(
            jnp.where(place[:, None, :] == spots[None, :, None], inside[:, None, :], 0), axis=2
        )
        sel = sel.reshape(PLANE, NZ, CAP).transpose(1, 0, 2).reshape(NZ, PLANE * CAP)
        slot = (source * NZ + plane) * CAP + rank
        slots = lax.dynamic_slice(slot, (mine, 0), (1, 32)).reshape(32)
        return general_attend(store, own, hidden, gain, sel, slots)

    which = jnp.int32(0)
    for cz in CZS:
        which = which + (most_z > PLANE * cz).astype(jnp.int32)
    which = jnp.where(most_x > 2 * CX, len(CZS), which)
    branches = [fast(cz, 2 + i) for i, cz in enumerate(CZS)] + [general]
    done = lax.switch(which, branches, passage_kv[0], own_kv[0], hidden, gains)
    return done[None]


def solution(mesh):
    return jax.shard_map(
        per_device,
        mesh=mesh,
        in_specs=(
            P("cache", None),
            P("section", None),
            P("section", "cache", None),
            P("section", "cache", None, None),
            P("cache", None),
            P(),
        ),
        out_specs=P("section", "cache", None),
        check_vma=False,
    )
```

```python
import functools

import jax
import jax.numpy as jnp
from jax import lax
from jax.experimental import pallas as pl
from jax.experimental.pallas import tpu as pltpu
from jax.sharding import PartitionSpec as P

D = 4096
QT = 64
PT = 32
NRET = 8
NX, NZ, NC, NY = 4, 8, 2, 4
PLANE = NX * NC
PASS_DEV = 16
REQ = 4
LAYERS = 4
CAP = 2
HALF = 256
PAIR = 512
WIDE = 1024
KEYS = 384
MESH = pl.DeviceIdType.MESH
STEPS = 2 * LAYERS
ONE = 256
CZS = (11, 13)
CX = 8
OWN = 64
KV_ROWS = NRET * PT + OWN


def mod(a, n):
    return lax.rem(a + n, n)


def where_am_i():
    cache = lax.axis_index("cache")
    y = lax.axis_index("section")
    c = lax.rem(cache, NC)
    z = lax.rem(cache // NC, NZ)
    x = cache // (NC * NZ)
    return cache, x, y, z, c


def cache_at(x, z, c):
    return (x * NZ + z) * NC + c


def greet_kernel(
    ids_ref,
    slot_ref,
    gain_ref,
    rows_out,
    gain_out,
    tab_out,
    mine,
    near,
    tile,
    far,
    fields,
    psend,
    precv,
    zsend,
    zrecv,
    gsend,
    grecv,
):
    cache, x, y, z, c = where_am_i()
    me = c * NX + x
    f32, bf16, i32 = jnp.float32, jnp.bfloat16, jnp.int32

    def plane_id(i):
        t = lax.rem(me + i, PLANE)
        return (cache_at(lax.rem(t, NX), z, t // NX), y)

    def z_id(i):
        return (cache_at(x, lax.rem(z + i, NZ), c), y)

    def y_id(i):
        return (cache, lax.rem(y + i, NY))

    def lanes(shape):
        return lax.broadcasted_iota(i32, shape, len(shape) - 1)

    def subs(shape):
        return lax.broadcasted_iota(i32, shape, len(shape) - 2)

    def mm(a, b):
        return jnp.dot(a.astype(bf16), b.astype(bf16), preferred_element_type=f32)

    barrier = pltpu.get_barrier_semaphore()
    for count, peer in ((PLANE, plane_id), (NZ, z_id), (NY, y_id)):
        for i in range(1, count):
            pl.semaphore_signal(barrier, inc=1, device_id=peer(i), device_id_type=MESH)

    ids = ids_ref[0:1, :]
    hit = (jnp.broadcast_to(ids % 128, (128, 128)) == subs((128, 128))).astype(f32)
    high = mm((slot_ref[...] // 32).astype(f32), hit)
    low = mm((slot_ref[...] % 32).astype(f32), hit)
    pick = jnp.broadcast_to(ids // 128, (8, 128)) == subs((8, 128))
    found = jnp.sum(jnp.where(pick, high * 32.0 + low, 0.0), axis=0, keepdims=True)
    found = jnp.where(lanes((1, 128)) // 32 == lax.rem(me, 4), found, 0.0)
    mine[...] = jnp.broadcast_to(found, (8, 128)).astype(i32)
    for i in range(32):
        gain_out[y, i : i + 1, :] = gain_ref[:, i * 128 : (i + 1) * 128].astype(f32)

    pl.semaphore_wait(barrier, PLANE + NZ + NY - 3)
    first, second, third = [], [], []
    for i in range(1, PLANE):
        first.append(
            pltpu.make_async_remote_copy(
                src_ref=mine,
                dst_ref=near.at[me],
                send_sem=psend.at[i],
                recv_sem=precv.at[i],
                device_id=plane_id(i),
                device_id_type=MESH,
            )
        )
    for i in range(1, NY):
        second.append(
            pltpu.make_async_remote_copy(
                src_ref=gain_out.at[y],
                dst_ref=gain_out.at[y],
                send_sem=gsend.at[i],
                recv_sem=grecv.at[i],
                device_id=y_id(i),
                device_id_type=MESH,
            )
        )
    for copy in first + second:
        copy.start()
    near[me] = mine[...]
    for copy in first:
        copy.wait()
    row = subs((8, 128))
    tile[...] = jnp.where(row == 0, near[0] + near[1] + near[2] + near[3], 0) + jnp.where(
        row == 1, near[4] + near[5] + near[6] + near[7], 0
    )
    for i in range(1, NZ):
        third.append(
            pltpu.make_async_remote_copy(
                src_ref=tile,
                dst_ref=far.at[z],
                send_sem=zsend.at[i],
                recv_sem=zrecv.at[i],
                device_id=z_id(i),
                device_id_type=MESH,
            )
        )
    for copy in third:
        copy.start()
    far[z] = tile[...]
    for copy in third:
        copy.wait()
    for i in range(NZ):
        rows_out[2 * i : 2 * i + 2, :] = far[i, 0:2, :]

    rows = rows_out[...]
    owner = rows // PASS_DEV
    inside = rows % PASS_DEV
    plane = (owner // NC) % NZ
    o8 = (owner % NC) * NX + owner // (NZ * NC)
    number = o8 * PASS_DEV + inside

    wide = (128, 128)
    count = jnp.zeros((NZ, 128), f32)
    for i in range(2 * NZ):
        in_plane = jnp.broadcast_to(plane[i : i + 1], (NZ, 128)) == subs((NZ, 128))
        is_number = jnp.broadcast_to(number[i : i + 1], wide) == subs(wide)
        count = count + lax.dot_general(
            in_plane.astype(f32).astype(bf16),
            is_number.astype(f32).astype(bf16),
            (((1,), (1,)), ((), ())),
            preferred_element_type=f32,
        )
    need = (count > 0.5).astype(f32)
    before = mm(need, (subs(wide) < lanes(wide)).astype(f32))
    first_of = mm(before, (subs(wide) == lanes(wide) // PASS_DEV * PASS_DEV).astype(f32))
    for i in range(2 * NZ):
        in_plane = jnp.broadcast_to(plane[i : i + 1], (NZ, 128)) == subs((NZ, 128))
        is_number = jnp.broadcast_to(number[i : i + 1], wide) == subs(wide)
        found = mm(before, is_number.astype(f32)) * in_plane.astype(f32)
        fields[0, i : i + 1, :] = jnp.sum(found, axis=0, keepdims=True).astype(i32)
    place = fields[0]
    chip = (place % PLANE) % NX

    same = (subs(wide) // 32 == lanes(wide) // 32) & (subs(wide) < lanes(wide))
    rank = jnp.zeros((2 * NZ, 128), f32)
    for v in range(NX):
        here = (chip == v).astype(f32)
        rank = rank + here * mm(here, same.astype(f32))
    rank = rank.astype(i32)
    fields[1] = plane
    fields[2] = rank

    def one_max(value):
        return jnp.max(jnp.max(value, axis=1, keepdims=True), axis=0, keepdims=True)

    most_z = one_max(jnp.sum(need, axis=1, keepdims=True)).astype(i32)
    most_x = one_max(rank) + 1

    ours = (subs((NZ, 128)) == z).astype(f32)
    my_need = jnp.sum(need * ours, axis=0, keepdims=True) > 0.5
    my_rank = jnp.sum(before * ours, axis=0, keepdims=True).astype(i32)
    my_first = jnp.sum(first_of * ours, axis=0, keepdims=True).astype(i32)
    again = (my_rank - my_first) // PLANE
    lane = lanes((1, 128))
    tall = (PASS_DEV, 128)
    key = jnp.where(my_need & (lane // PASS_DEV == me), my_rank % PLANE * 2 + again, -1)
    hit = jnp.broadcast_to(key, tall) == subs(tall)
    ssel = jnp.sum(jnp.where(hit, lanes(tall) % PASS_DEV, 0), axis=1, keepdims=True)
    key = jnp.where(my_need & (my_rank % PLANE == me), my_rank // PLANE, -1)
    hit = jnp.broadcast_to(key, tall) == subs(tall)
    spot = jnp.broadcast_to(lane // PASS_DEV * 2 + again, tall)
    csel = jnp.sum(jnp.where(hit, spot, 0), axis=1, keepdims=True)
    tab_out[0:16, :] = jnp.where(
        lanes(tall) == 0, jnp.broadcast_to(csel, tall), jnp.broadcast_to(ssel, tall)
    )

    block = (subs(wide) // 32 == lanes(wide)).astype(f32)
    for half in range(2):
        at = pl.ds(2 * z + half, 1)
        g, p, k = fields[0, at, :], fields[1, at, :], fields[2, at, :]
        t = g % PLANE
        b = t % NX
        where = ((t // NX) * NZ + p) * CZS[-1] + jnp.minimum(g // PLANE, CZS[-1] - 1)
        where = where.astype(f32)
        key = jnp.where((b == x) & (k % NC == c), k // NC, -1)
        hit = jnp.broadcast_to(key, (CX, 128)) == subs((CX, 128))
        chosen = jnp.where(hit, jnp.broadcast_to(where, (CX, 128)), 0.0)
        tab_out[16 + 8 * half : 24 + 8 * half, :] = mm(chosen, block).astype(i32)
        slot = ((k % NC) * NX + b) * CX + jnp.minimum(k // NC, CX - 1)
        tab_out[32 + half : 33 + half, :] = slot
    tab_out[34:35, :] = jnp.broadcast_to(most_z, (1, 128))
    tab_out[35:36, :] = jnp.broadcast_to(most_x, (1, 128))
    tab_out[36:40, :] = jnp.zeros((4, 128), i32)
    for copy in second:
        copy.wait()


def greet(ids, slot, gain):
    vmem = pl.BlockSpec(memory_space=pltpu.VMEM)
    dma = pltpu.SemaphoreType.DMA
    return pl.pallas_call(
        greet_kernel,
        out_shape=(
            jax.ShapeDtypeStruct((2 * NZ, 128), jnp.int32),
            jax.ShapeDtypeStruct((NY, 32, 128), jnp.float32),
            jax.ShapeDtypeStruct((40, 128), jnp.int32),
        ),
        in_specs=[vmem, vmem, vmem],
        out_specs=(vmem, vmem, vmem),
        scratch_shapes=[
            pltpu.VMEM((8, 128), jnp.int32),
            pltpu.VMEM((PLANE, 8, 128), jnp.int32),
            pltpu.VMEM((8, 128), jnp.int32),
            pltpu.VMEM((NZ, 8, 128), jnp.int32),
            pltpu.VMEM((3, 2 * NZ, 128), jnp.int32),
            dma((PLANE,)),
            dma((PLANE,)),
            dma((NZ,)),
            dma((NZ,)),
            dma((NY,)),
            dma((NY,)),
        ],
        compiler_params=pltpu.CompilerParams(collective_id=0, has_side_effects=True),
        name="greet",
    )(ids, slot, gain)


def fast_kernel(
    cz, store, own_in, hid, gain, tab, out, ybuf, send, kvs, own, state, staged, gains, rs,
    ssq, box, ystage, sbox, packed, ysend, yrecv, osend, orecv, local, ssend, srecv, csend, crecv, zsend, zrecv, xsend, xrecv,
    qsend, qrecv, outsend, outrecv, outlocal, *many
):
    strips, pools, recvs = many[:STEPS], many[STEPS : 2 * STEPS], many[2 * STEPS :]
    cache, x, y, z, c = where_am_i()
    me = c * NX + x
    scale = 1.4426950408889634 / 128**0.5

    def plane_id(t):
        return (cache_at(lax.rem(t, NX), z, t // NX), y)

    def z_id(dz):
        return (cache_at(x, mod(z + dz, NZ), c), y)

    def y_id(s):
        return (cache, s)

    def step_of(i, s):
        return jnp.where(i == 2 * s, 0, jnp.where(i < 2 * s, i + 1, i))

    def part_of(q):
        return 2 * y if q == 0 else jnp.where(q - 1 < 2 * y, q - 1, q)

    barrier = pltpu.get_barrier_semaphore()
    for i in range(1, PLANE):
        pl.semaphore_signal(
            barrier, inc=1, device_id=plane_id(lax.rem(me + i, PLANE)), device_id_type=MESH
        )
    for i in range(1, NY):
        pl.semaphore_signal(
            barrier, inc=1, device_id=y_id(lax.rem(y + i, NY)), device_id_type=MESH
        )
    for dz in (1, -1):
        pl.semaphore_signal(barrier, inc=1, device_id=z_id(dz), device_id_type=MESH)
    pl.semaphore_wait(barrier, PLANE + NY)

    def local_copies():
        made = []
        for j in range(2):
            for part in range(2):
                cols = pl.ds(pl.multiple_of(part * 1024 + y * HALF + j * 128, 128), 128)
                made.append(
                    pltpu.make_async_copy(
                        store.at[:, :, cols],
                        ybuf.at[step_of(2 * y + j, y), :, :, pl.ds(part * 128, 128)],
                        local.at[2 * j + part],
                    )
                )
        for part in range(2):
            cols = pl.ds(pl.multiple_of(part * 1024 + y * HALF, HALF), HALF)
            made.append(
                pltpu.make_async_copy(
                    own_in.at[:, cols], own.at[y, :, pl.ds(part * HALF, HALF)], local.at[4 + part]
                )
            )
        return made

    def pack_copies(i, j):
        s = lax.rem(y + i, NY)
        made = []
        for part in range(2):
            cols = pl.ds(pl.multiple_of(part * 1024 + s * HALF + j * 128, 128), 128)
            made.append(
                pltpu.make_async_copy(
                    store.at[:, :, cols],
                    box.at[i - 1, j, :, :, pl.ds(part * 128, 128)],
                    packed.at[i, j, part],
                )
            )
        return made

    def scatter_copy(i, j):
        s = lax.rem(y + i, NY)
        q = step_of(2 * y + j, s)
        return pltpu.make_async_remote_copy(
            src_ref=box.at[i - 1, j],
            dst_ref=ybuf.at[q],
            send_sem=ysend.at[i, j],
            recv_sem=yrecv.at[q],
            device_id=y_id(s),
            device_id_type=MESH,
        )

    def own_scatter(i):
        s = lax.rem(y + i, NY)
        made = []
        for part in range(2):
            cols = pl.ds(pl.multiple_of(part * 1024 + s * HALF, HALF), HALF)
            made.append(
                pltpu.make_async_remote_copy(
                    src_ref=own_in.at[:, cols],
                    dst_ref=own.at[y, :, pl.ds(part * HALF, HALF)],
                    send_sem=osend.at[i, part],
                    recv_sem=orecv.at[y, part],
                    device_id=y_id(s),
                    device_id_type=MESH,
                )
            )
        return made

    def stripe(q):
        par = q % 2
        if q >= 2:
            striped(q - 2)
        ystage[...] = ybuf[q]

        def fill(i, _):
            sbox[par, i] = ystage[tab[i, 1]]
            return 0

        lax.fori_loop(0, 2 * PLANE, fill, 0)

        def push(i, _):
            t = lax.rem(me + i, PLANE)
            pltpu.make_async_remote_copy(
                src_ref=sbox.at[par, pl.ds(t * 2, 2)],
                dst_ref=strips[q].at[pl.ds(me * 2, 2)],
                send_sem=ssend.at[q],
                recv_sem=srecv.at[q],
                device_id=plane_id(t),
                device_id_type=MESH,
            ).start()
            return 0

        strips[q][pl.ds(me * 2, 2)] = sbox[par, pl.ds(me * 2, 2)]
        lax.fori_loop(1, PLANE, push, 0)

    def striped(q):
        what = strips[q].at[pl.ds(0, 2 * PLANE - 2)]
        pltpu.make_async_copy(what, what, ssend.at[q]).wait()

    def z_ref(q, plane, half):
        at = (c * NZ + plane) * CZS[-1]
        if half == 0:
            return pools[q].at[pl.ds(at, cz - cz // 2)]
        return pools[q].at[pl.ds(at + cz - cz // 2, cz // 2)]

    def z_copy(q, up, half, hop):
        where = z_ref(q, mod(z - (hop - 1), NZ) if up else mod(z + (hop - 1), NZ), half)
        return pltpu.make_async_remote_copy(
            src_ref=where,
            dst_ref=where,
            send_sem=zsend.at[q, int(up), half, hop - 1],
            recv_sem=zrecv.at[q, int(up), half, hop - 1],
            device_id=z_id(1 if up else -1),
            device_id_type=MESH,
        )

    def z_arrival(q, up, half, hop):
        where = z_ref(q, mod(z - hop, NZ) if up else mod(z + hop, NZ), half)
        return pltpu.make_async_remote_copy(
            src_ref=where,
            dst_ref=where,
            send_sem=zsend.at[q, int(up), half, hop - 1],
            recv_sem=zrecv.at[q, int(up), half, hop - 1],
            device_id=z_id(1 if up else -1),
            device_id_type=MESH,
        )

    def hops(up, half):
        return 4 if bool(up) == (half == 0) else 3

    def share(where, q):
        pltpu.make_async_remote_copy(
            src_ref=where,
            dst_ref=where,
            send_sem=csend.at[q],
            recv_sem=crecv.at[q],
            device_id=(cache_at(x, z, 1 - c), y),
            device_id_type=MESH,
        ).start()

    def compact(q):
        what = strips[q].at[pl.ds(0, 2 * PLANE - 2)]
        pltpu.make_async_copy(what, what, srecv.at[q]).wait()
        for i in range(cz):
            pools[q][(c * NZ + z) * CZS[-1] + i] = strips[q][tab[i, 0]]
        for half in range(2):
            for up in (True, False):
                z_copy(q, up, half, 1).start()
        share(pools[q].at[pl.ds((c * NZ + z) * CZS[-1], cz)], q)

    def choose(q):
        par = q % 2
        what = pools[q].at[pl.ds(0, NZ * cz)]
        pltpu.make_async_copy(what, what, crecv.at[q]).wait()
        if q >= 2:
            x_sent(q - 2)

        def fill(t, _):
            for i in range(CX):
                send[par, t, i] = pools[q][tab[16 + 8 * (t // 4) + i, lax.rem(t, 4)]]
            return 0

        lax.fori_loop(0, PLANE, fill, 0)
        recvs[q][pl.ds(me * CX, CX)] = send[par, me]

        def push(i, _):
            t = lax.rem(me + i, PLANE)
            pltpu.make_async_remote_copy(
                src_ref=send.at[par, t],
                dst_ref=recvs[q].at[pl.ds(me * CX, CX)],
                send_sem=xsend.at[q],
                recv_sem=xrecv.at[q],
                device_id=plane_id(t),
                device_id_type=MESH,
            ).start()
            return 0

        lax.fori_loop(1, PLANE, push, 0)

    def x_sent(q):
        what = send.at[q % 2, pl.ds(0, PLANE - 1)]
        pltpu.make_async_copy(what, what, xsend.at[q]).wait()

    def assemble(q):
        what = recvs[q].at[pl.ds(0, (PLANE - 1) * CX)]
        pltpu.make_async_copy(what, what, xrecv.at[q]).wait()
        part = part_of(q)

        def one(r, _):
            for n in range(NRET):
                at = tab[32 + me // 4, lax.rem(me, 4) * 32 + r * NRET + n]
                kvs[part, r, n * PT : (n + 1) * PT] = recvs[q][at]
            return 0

        lax.fori_loop(0, REQ, one, 0)

    def y_arrived(q):
        what = ybuf.at[q]
        pltpu.make_async_copy(what, what, yrecv.at[q]).wait()

    krow = lax.broadcasted_iota(jnp.int32, (OWN, 4 * QT), 0)
    qcol = lax.rem(lax.broadcasted_iota(jnp.int32, (OWN, 4 * QT), 1), QT)

    def before_layer(layer):
        @pl.when(layer != y)
        def _():
            for part in range(2):
                what = own.at[layer, :, pl.ds(part * HALF, HALF)]
                pltpu.make_async_copy(what, what, orecv.at[layer, part]).wait()

        if layer > 0:
            what = ssq.at[layer - 1, pl.ds(0, NY - 1)]
            pltpu.make_async_copy(what, what, qrecv.at[layer - 1]).wait()
            total = ssq[layer - 1, 0] + ssq[layer - 1, 1] + ssq[layer - 1, 2] + ssq[layer - 1, 3]
            total = total + pltpu.roll(total, QT, 1)
            total = total + pltpu.roll(total, 2 * QT, 1)
            rs[...] = lax.rsqrt(total * (1.0 / D) + 1e-05)

    def attend(layer, r, heads_of):
        rows = pl.ds(pl.multiple_of(r * QT, QT), QT)
        causal = krow <= qcol
        squares = jnp.zeros((1, 4 * QT), jnp.float32)
        for j in heads_of:
            part = 2 * layer + j
            wide = state[r, j].astype(jnp.float32)
            query = (wide * rs[pl.ds(r, 1), :] * gains[layer, j]).astype(jnp.bfloat16)
            far_keys = kvs[part, r, :, 0:128]
            far_vals = kvs[part, r, :, 128:256]
            near_keys = own[layer, rows, j * 128 : (j + 1) * 128]
            near_vals = own[layer, rows, HALF + j * 128 : HALF + (j + 1) * 128]
            far = jnp.dot(far_keys, query, preferred_element_type=jnp.float32)
            near = jnp.dot(near_keys, query, preferred_element_type=jnp.float32)
            near = jnp.where(causal, near, -jnp.inf)
            top = jnp.maximum(
                jnp.max(far, axis=0, keepdims=True), jnp.max(near, axis=0, keepdims=True)
            )
            far = jnp.exp2((far - top) * scale)
            near = jnp.exp2((near - top) * scale)
            total = jnp.sum(far, axis=0, keepdims=True) + jnp.sum(near, axis=0, keepdims=True)
            total = 1.0 / total
            far = (far * total).astype(jnp.bfloat16)
            near = (near * total).astype(jnp.bfloat16)
            first = (((0,), (0,)), ((), ()))
            mixed = lax.dot_general(far_vals, far, first, preferred_element_type=jnp.float32)
            mixed = mixed + lax.dot_general(
                near_vals, near, first, preferred_element_type=jnp.float32
            )
            new = (wide + mixed).astype(jnp.bfloat16)
            state[r, j] = new
            turned = new.T
            for g in range(4):
                h = 4 * j + g
                staged[layer, rows, h * 128 : (h + 1) * 128] = turned[g * QT : (g + 1) * QT]
            new = new.astype(jnp.float32)
            squares = squares + jnp.sum(new * new, axis=0, keepdims=True)
        if layer < LAYERS - 1:
            ssq[layer, y, pl.ds(r, 1), :] = squares
        width = PAIR * len(heads_of)
        cols = pl.ds(pl.multiple_of(y * WIDE + heads_of[0] * PAIR, PAIR), width)
        made = staged.at[layer, rows, pl.ds(heads_of[0] * PAIR, width)]

        @pl.when(layer == y)
        def _():
            pltpu.make_async_copy(made, out.at[rows, cols], outlocal).start()

        @pl.when(layer != y)
        def _():
            pltpu.make_async_remote_copy(
                src_ref=made,
                dst_ref=out.at[rows, cols],
                send_sem=outsend.at[layer],
                recv_sem=outrecv,
                device_id=y_id(layer),
                device_id_type=MESH,
            ).start()

    def after_layer(layer):
        for i in range(1, NY):
            pltpu.make_async_remote_copy(
                src_ref=ssq.at[layer, y],
                dst_ref=ssq.at[layer, y],
                send_sem=qsend.at[layer, i],
                recv_sem=qrecv.at[layer],
                device_id=y_id(lax.rem(y + i, NY)),
                device_id_type=MESH,
            ).start()

    def attend_rows(layer, first, count, together, heads_of=(0, 1)):
        def body(i, _):
            for u in range(together):
                attend(layer, first + i * together + u, heads_of)
            return 0

        lax.fori_loop(0, count // together, body, 0)

    own_copies = local_copies()
    for copy in own_copies[:2]:
        copy.start()
    packs = [(i, j, pack_copies(i, j)) for j in range(2) for i in (1, 3, 2)]
    for i, j, copies in packs[:3]:
        for copy in copies:
            copy.start()
    for copy in own_copies[2:]:
        copy.start()
    for i, j, copies in packs[3:]:
        for copy in copies:
            copy.start()
    own_copies[0].wait()
    own_copies[1].wait()
    stripe(0)
    for i, j, copies in packs:
        for copy in copies:
            copy.wait()

    def scatter(first, last):
        @pl.when((y >= first) & (y <= last))
        def _():
            for j in range(2):
                for i in (1, 3, 2):
                    scatter_copy(i, j).start()

    def scatter_own():
        for i in (1, 3, 2):
            for copy in own_scatter(i):
                copy.start()

    scatter(0, 1)
    compact(0)

    for layer in range(LAYERS - 1):
        ssq[layer, y] = jnp.zeros((8, 4 * QT), jnp.float32)
    mean_sq = jnp.zeros((REQ * QT, 1), jnp.float32)
    for i in range(8):
        wide = hid[:, i * 512 : (i + 1) * 512].astype(jnp.float32)
        mean_sq = mean_sq + jnp.sum(wide * wide, axis=-1, keepdims=True)
    mean_sq = jnp.broadcast_to(mean_sq * (1.0 / D), (REQ * QT, 128)).T
    mean_sq = lax.rsqrt(mean_sq + 1e-05)
    for r in range(REQ):
        part = mean_sq[0:1, r * QT : (r + 1) * QT]
        rs[r : r + 1, :] = jnp.concatenate([part] * 4, axis=1)
    rs[REQ:, :] = jnp.zeros((8 - REQ, 4 * QT), jnp.float32)
    for j in range(2):
        for r in range(REQ):
            heads = []
            for g in range(4):
                cols = pl.ds(pl.multiple_of(y * WIDE + (4 * j + g) * 128, 128), 128)
                heads.append(hid[r * QT : (r + 1) * QT, cols])
            state[r, j] = jnp.concatenate(heads, axis=0).T
        for layer in range(LAYERS):
            heads = []
            for g in range(4):
                at = gain[layer, pl.ds(y * 8 + 4 * j + g, 1), :]
                heads.append(jnp.broadcast_to(at, (QT, 128)))
            gains[layer, j] = jnp.concatenate(heads, axis=0).T

    def arrived_from_y(q):
        part = part_of(q)

        @pl.when(part != 2 * y + 1)
        def _():
            y_arrived(q)

    for copy in own_copies[2:]:
        copy.wait()
    arrived_from_y(1)
    stripe(1)
    todo = {}

    def later(slot, work):
        todo.setdefault(slot, []).append(work)

    later(0, lambda: scatter(2, 2))
    later(1, lambda: scatter(3, 3))
    later(3, scatter_own)

    for q in range(1, STEPS):
        if q >= 2:
            later(q - 1, lambda q=q: (arrived_from_y(q), stripe(q)))
        later(2 * q - 2, lambda q=q: compact(q))
    for q in range(STEPS):
        later(2 * q + 3, lambda q=q: choose(q))
    for q in range(STEPS - 1):
        later(2 * q + 6, lambda q=q: assemble(q))
    for layer in range(2):
        later(4 * layer + 10, lambda layer=layer: before_layer(layer))
        for half in range(2):
            later(
                4 * layer + 10 + 2 * half,
                lambda layer=layer, half=half: attend_rows(layer, 2 * half, 2, 1),
            )
        later(4 * layer + 12, lambda layer=layer: after_layer(layer))

    for slot in range(2 * STEPS + 3):
        for q in range(STEPS):
            hop = slot - 2 * q + 1
            if not 1 <= hop <= 4:
                continue
            for half in range(2):
                for up in (True, False):
                    if hop <= hops(up, half):
                        z_arrival(q, up, half, hop).wait_recv()
                        if hop < hops(up, half):
                            z_copy(q, up, half, hop + 1).start()
                        plane = mod(z - hop, NZ) if up else mod(z + hop, NZ)
                        share(z_ref(q, plane, half), q)
        for work in todo.get(slot, ()):
            work()

    before_layer(2)
    attend_rows(2, 0, REQ, 2)
    after_layer(2)
    before_layer(3)
    attend_rows(3, 0, REQ, 2, (0,))
    assemble(STEPS - 1)
    attend_rows(3, 0, REQ, 2, (1,))

    striped(STEPS - 2)
    striped(STEPS - 1)
    x_sent(STEPS - 2)
    x_sent(STEPS - 1)
    for q in range(STEPS):
        what = pools[q].at[pl.ds(0, NZ * cz)]
        pltpu.make_async_copy(what, what, csend.at[q]).wait()
        for up in (True, False):
            for half in range(2):
                for hop in range(1, hops(up, half) + 1):
                    z_copy(q, up, half, hop).wait_send()
    for i in range(1, NY):
        for j in range(2):
            scatter_copy(i, j).wait_send()
        for copy in own_scatter(i):
            copy.wait_send()
        for layer in range(LAYERS - 1):
            what = ssq.at[layer, y]
            pltpu.make_async_copy(what, what, qsend.at[layer, i]).wait()
    for layer in range(LAYERS):

        @pl.when(layer != y)
        def _():
            what = staged.at[layer]
            pltpu.make_async_copy(what, what, outsend.at[layer]).wait()

    what = out.at[:, pl.ds(0, 3 * WIDE)]
    pltpu.make_async_copy(what, what, outrecv).wait()
    what = out.at[:, pl.ds(0, WIDE)]
    pltpu.make_async_copy(what, what, outlocal).wait()


def fast_attend(cz, collective_id, store, own, hidden, gain, tab):
    vmem = pl.BlockSpec(memory_space=pltpu.VMEM)
    smem = pl.BlockSpec(memory_space=pltpu.SMEM)
    hbm = pl.BlockSpec(memory_space=pl.ANY)
    bf16 = jnp.bfloat16
    dma = pltpu.SemaphoreType.DMA
    return pl.pallas_call(
        functools.partial(fast_kernel, cz),
        out_shape=jax.ShapeDtypeStruct((REQ * QT, D), bf16),
        in_specs=[hbm, hbm, vmem, vmem, smem],
        out_specs=hbm,
        scratch_shapes=[
            pltpu.VMEM((STEPS, PASS_DEV, PT, ONE), bf16),
            pltpu.VMEM((2, PLANE, CX, PT, ONE), bf16),
            pltpu.VMEM((STEPS, REQ, NRET * PT, ONE), bf16),
            pltpu.VMEM((LAYERS, REQ * QT, PAIR), bf16),
            pltpu.VMEM((REQ, 2, 128, 4 * QT), bf16),
            pltpu.VMEM((LAYERS, REQ * QT, WIDE), bf16),
            pltpu.VMEM((LAYERS, 2, 128, 4 * QT), jnp.float32),
            pltpu.VMEM((8, 4 * QT), jnp.float32),
            pltpu.VMEM((LAYERS - 1, NY, 8, 4 * QT), jnp.float32),
            pltpu.VMEM((NY - 1, 2, PASS_DEV, PT, ONE), bf16),
            pltpu.VMEM((PASS_DEV, PT, ONE), bf16),
            pltpu.VMEM((2, 2 * PLANE, PT, ONE), bf16),
            dma((NY, 2, 2)),
            dma((NY, 2)),
            dma((STEPS,)),
            dma((NY, 2)),
            dma((LAYERS, 2)),
            dma((6,)),
            dma((STEPS,)),
            dma((STEPS,)),
            dma((STEPS,)),
            dma((STEPS,)),
            dma((STEPS, 2, 2, 4)),
            dma((STEPS, 2, 2, 4)),
            dma((STEPS,)),
            dma((STEPS,)),
            dma((LAYERS - 1, NY)),
            dma((LAYERS - 1,)),
            dma((LAYERS,)),
            dma(()),
            dma(()),
        ]
        + [pltpu.VMEM((PLANE * 2, PT, ONE), bf16)] * STEPS
        + [pltpu.VMEM((NC * NZ * CZS[-1], PT, ONE), bf16)] * STEPS
        + [pltpu.VMEM((PLANE * CX, PT, ONE), bf16)] * STEPS,
        compiler_params=pltpu.CompilerParams(
            collective_id=collective_id, has_side_effects=True, vmem_limit_bytes=60 * 1024 * 1024
        ),
        name="fast_attend_" + str(cz),
    )(store, own, hidden, gain, tab)


def general_kernel(
    store,
    own_in,
    hid,
    gain,
    sel,
    slots,
    out,
    pool,
    recv,
    send,
    rstage,
    stage,
    own,
    kv,
    state,
    rs,
    ssq,
    ysend,
    yrecv,
    osend,
    orecv,
    local,
    zsend,
    zrecv,
    xsend,
    xrecv,
    qsend,
    qrecv,
    outsend,
    outrecv,
    outlocal,
):
    cache, x, y, z, c = where_am_i()
    me = x * NC + c

    def plane_id(t):
        return (cache_at(t // NC, z, lax.rem(t, NC)), y)

    def z_id(dz):
        return (cache_at(x, mod(z + dz, NZ), c), y)

    def y_id(s):
        return (cache, s)

    def step_of(layer, s):
        return jnp.where(layer == s, 0, jnp.where(layer < s, layer + 1, layer))

    barrier = pltpu.get_barrier_semaphore()
    for i in range(1, PLANE):
        pl.semaphore_signal(
            barrier, inc=1, device_id=plane_id(lax.rem(me + i, PLANE)), device_id_type=MESH
        )
    for i in range(1, NY):
        pl.semaphore_signal(
            barrier, inc=1, device_id=y_id(lax.rem(y + i, NY)), device_id_type=MESH
        )
    for dz in (1, -1):
        pl.semaphore_signal(barrier, inc=1, device_id=z_id(dz), device_id_type=MESH)
    pl.semaphore_wait(barrier, PLANE + NY)

    def local_copies():
        made = []
        for part in range(2):
            cols = pl.ds(pl.multiple_of(part * 1024 + y * HALF, HALF), HALF)
            half = pl.ds(part * HALF, HALF)
            made.append(
                pltpu.make_async_copy(
                    store.at[:, :, cols], pool.at[0, z, :, :, half], local.at[part]
                )
            )
            made.append(
                pltpu.make_async_copy(
                    own_in.at[:, cols], own.at[y, :, half], local.at[2 + part]
                )
            )
        return made

    def scatter_copies(i):
        s = lax.rem(y + i, NY)
        made = []
        for part in range(2):
            cols = pl.ds(pl.multiple_of(part * 1024 + s * HALF, HALF), HALF)
            half = pl.ds(part * HALF, HALF)
            made.append(
                pltpu.make_async_remote_copy(
                    src_ref=store.at[:, :, cols],
                    dst_ref=pool.at[step_of(y, s), z, :, :, half],
                    send_sem=ysend.at[i, part],
                    recv_sem=yrecv.at[step_of(y, s), part],
                    device_id=y_id(s),
                    device_id_type=MESH,
                )
            )
            made.append(
                pltpu.make_async_remote_copy(
                    src_ref=own_in.at[:, cols],
                    dst_ref=own.at[y, :, half],
                    send_sem=osend.at[i, part],
                    recv_sem=orecv.at[y, part],
                    device_id=y_id(s),
                    device_id_type=MESH,
                )
            )
        return made

    for copy in local_copies():
        copy.start()
    for i in (1, 3, 2):
        for copy in scatter_copies(i):
            copy.start()

    def z_copy(k, up, half, hop):
        plane = mod(z - (hop - 1), NZ) if up else mod(z + (hop - 1), NZ)
        rows = pl.ds(half * 8, 8)
        where = pool.at[k, plane, rows]
        return pltpu.make_async_remote_copy(
            src_ref=where,
            dst_ref=where,
            send_sem=zsend.at[k, int(up), half, hop - 1],
            recv_sem=zrecv.at[k, int(up), half, hop - 1],
            device_id=z_id(1 if up else -1),
            device_id_type=MESH,
        )

    def z_arrival(k, up, half, hop):
        plane = mod(z - hop, NZ) if up else mod(z + hop, NZ)
        where = pool.at[k, plane, pl.ds(half * 8, 8)]
        return pltpu.make_async_remote_copy(
            src_ref=where,
            dst_ref=where,
            send_sem=zsend.at[k, int(up), half, hop - 1],
            recv_sem=zrecv.at[k, int(up), half, hop - 1],
            device_id=z_id(1 if up else -1),
            device_id_type=MESH,
        )

    def hops(up, half):
        return 4 if bool(up) == (half == 0) else 3

    def z_first(k):
        for half in range(2):
            for up in (True, False):
                z_copy(k, up, half, 1).start()

    def choose(k, plane):
        par = lax.rem(k, 2)
        stage[...] = pool[k, plane]

        def fill(t, _):
            for r in range(CAP):
                send[par, plane, t, r] = stage[sel[plane, t * CAP + r]]
            return 0

        lax.fori_loop(0, PLANE, fill, 0)
        recv[k, me, plane] = send[par, plane, me]

        def push(i, _):
            t = lax.rem(me + i, PLANE)
            pltpu.make_async_remote_copy(
                src_ref=send.at[par, plane, t],
                dst_ref=recv.at[k, me, plane],
                send_sem=xsend.at[k],
                recv_sem=xrecv.at[k],
                device_id=plane_id(t),
                device_id_type=MESH,
            ).start()
            return 0

        lax.fori_loop(1, PLANE, push, 0)

    def x_sent(k):
        what = send.at[lax.rem(k, 2), :, pl.ds(0, PLANE - 1)]
        pltpu.make_async_copy(what, what, xsend.at[k]).wait()

    def x_arrived(k):
        what = recv.at[k, pl.ds(0, PLANE - 1)]
        pltpu.make_async_copy(what, what, xrecv.at[k]).wait()

    def y_arrived(k):
        for part in range(2):
            what = pool.at[k, z, :, :, pl.ds(part * HALF, HALF)]
            pltpu.make_async_copy(what, what, yrecv.at[k, part]).wait()

    def attend(layer):
        k = step_of(layer, y)

        def lift(i, _):
            rstage[pl.ds(i * 16, 16)] = recv[k, i].reshape(16, PT, PAIR)
            return 0

        lax.fori_loop(0, PLANE, lift, 0)

        @pl.when(layer != y)
        def _():
            for part in range(2):
                what = own.at[layer, :, pl.ds(part * HALF, HALF)]
                pltpu.make_async_copy(what, what, orecv.at[layer, part]).wait()

        if layer > 0:
            what = ssq.at[layer - 1, pl.ds(0, NY - 1)]
            pltpu.make_async_copy(what, what, qrecv.at[layer - 1]).wait()
            total = ssq[layer - 1, 0] + ssq[layer - 1, 1] + ssq[layer - 1, 2] + ssq[layer - 1, 3]
            total = jnp.broadcast_to(total[0:1], (128, 256)).T
            rs[...] = lax.rsqrt(total * (1.0 / D) + 1e-05)

        row = lax.rem(lax.broadcasted_iota(jnp.int32, (4 * QT, KEYS), 0), QT)
        col = lax.broadcasted_iota(jnp.int32, (4 * QT, KEYS), 1)
        seen = (col < NRET * PT + 1 + row)

        def one(r, _):
            rows = pl.ds(pl.multiple_of(r * QT, QT), QT)
            for n in range(NRET):
                kv[n * PT : (n + 1) * PT] = rstage[slots[r * NRET + n]]
            kv[NRET * PT : NRET * PT + QT] = own[layer, rows]
            if layer == 0:
                before = hid[rows, pl.ds(pl.multiple_of(y * WIDE, WIDE), WIDE)]
            else:
                before = state[layer - 1, rows]
            wide = before.astype(jnp.float32)
            query = (wide * rs[rows, 0:1] * gain[layer : layer + 1, :]).astype(jnp.bfloat16)
            squares = jnp.zeros((QT, 128), jnp.float32)
            for j in range(2):
                heads = [4 * j + g for g in range(4)]
                qj = jnp.concatenate([query[:, h * 128 : (h + 1) * 128] for h in heads], axis=0)
                keys = kv[:, j * 128 : (j + 1) * 128]
                vals = kv[:, HALF + j * 128 : HALF + (j + 1) * 128]
                score = lax.dot_general(
                    qj, keys, (((1,), (1,)), ((), ())), preferred_element_type=jnp.float32
                )
                score = jnp.where(seen, score * (1.0 / 128**0.5), -jnp.inf)
                top = jnp.max(score, axis=-1, keepdims=True)
                expd = jnp.exp(score - top)
                total = jnp.sum(expd, axis=-1, keepdims=True)
                weight = (expd * (1.0 / total)).astype(jnp.bfloat16)
                mixed = jnp.dot(weight, vals, preferred_element_type=jnp.float32)
                for g, h in enumerate(heads):
                    new = wide[:, h * 128 : (h + 1) * 128] + mixed[g * QT : (g + 1) * QT]
                    new = new.astype(jnp.bfloat16)
                    state[layer, rows, h * 128 : (h + 1) * 128] = new
                    new = new.astype(jnp.float32)
                    squares = squares + new * new
            if layer < LAYERS - 1:
                squares = jnp.sum(squares, axis=-1, keepdims=True)
                rs[rows, :] = jnp.broadcast_to(squares, (QT, 128))
            cols = pl.ds(pl.multiple_of(y * WIDE, WIDE), WIDE)

            @pl.when(layer == y)
            def _():
                pltpu.make_async_copy(
                    state.at[layer, rows], out.at[rows, cols], outlocal
                ).start()

            @pl.when(layer != y)
            def _():
                pltpu.make_async_remote_copy(
                    src_ref=state.at[layer, rows],
                    dst_ref=out.at[rows, cols],
                    send_sem=outsend.at[layer],
                    recv_sem=outrecv,
                    device_id=y_id(layer),
                    device_id_type=MESH,
                ).start()

            return 0

        lax.fori_loop(0, REQ, one, 0)
        if layer < LAYERS - 1:
            ssq[layer, y] = rs[...].T[0:8]
            for i in range(1, NY):
                pltpu.make_async_remote_copy(
                    src_ref=ssq.at[layer, y],
                    dst_ref=ssq.at[layer, y],
                    send_sem=qsend.at[layer, i],
                    recv_sem=qrecv.at[layer],
                    device_id=y_id(lax.rem(y + i, NY)),
                    device_id_type=MESH,
                ).start()

    wide = hid[...].astype(jnp.float32)
    mean_sq = jnp.sum(wide * wide, axis=-1, keepdims=True) * (1.0 / D)
    rs[...] = jnp.broadcast_to(lax.rsqrt(mean_sq + 1e-05), (256, 128))
    kv[NRET * PT + QT :] = jnp.zeros((KEYS - NRET * PT - QT, PAIR), jnp.bfloat16)

    for copy in local_copies():
        copy.wait()
    z_first(0)

    def do_step(k):
        if k >= 2:
            x_sent(k - 2)
        choose(k, z)
        for hop in range(1, 5):
            for half in range(2):
                for up in (True, False):
                    if hop <= hops(up, half):
                        z_arrival(k, up, half, hop).wait_recv()
                        if hop < hops(up, half):
                            z_copy(k, up, half, hop + 1).start()
            if hop == 2 and k < LAYERS - 1:
                y_arrived(k + 1)
                z_first(k + 1)
            choose(k, mod(z - hop, NZ))
            if hop < 4:
                choose(k, mod(z + hop, NZ))
            if hop == 3 and k >= 2:
                if k == 2:
                    x_arrived(0)
                    x_arrived(1)
                    attend(0)
                else:
                    x_arrived(2)
                    attend(1)

    for k in range(LAYERS):
        do_step(k)
    x_arrived(3)
    attend(2)
    attend(3)

    x_sent(2)
    x_sent(3)
    for k in range(LAYERS):
        for up in (True, False):
            for half in range(2):
                for hop in range(1, hops(up, half) + 1):
                    z_copy(k, up, half, hop).wait_send()
    for i in range(1, NY):
        for copy in scatter_copies(i):
            copy.wait_send()
        for layer in range(LAYERS - 1):
            what = ssq.at[layer, y]
            pltpu.make_async_copy(what, what, qsend.at[layer, i]).wait()
    for layer in range(LAYERS):

        @pl.when(layer != y)
        def _():
            what = state.at[layer]
            pltpu.make_async_copy(what, what, outsend.at[layer]).wait()

    what = out.at[:, pl.ds(0, 3 * WIDE)]
    pltpu.make_async_copy(what, what, outrecv).wait()
    what = out.at[:, pl.ds(0, WIDE)]
    pltpu.make_async_copy(what, what, outlocal).wait()


def general_attend(store, own, hidden, gain, sel, slots):
    vmem = pl.BlockSpec(memory_space=pltpu.VMEM)
    smem = pl.BlockSpec(memory_space=pltpu.SMEM)
    hbm = pl.BlockSpec(memory_space=pl.ANY)
    bf16 = jnp.bfloat16
    dma = pltpu.SemaphoreType.DMA
    return pl.pallas_call(
        general_kernel,
        out_shape=jax.ShapeDtypeStruct((REQ * QT, D), bf16),
        in_specs=[hbm, hbm, vmem, vmem, smem, smem],
        out_specs=hbm,
        scratch_shapes=[
            pltpu.VMEM((LAYERS, NZ, PASS_DEV, PT, PAIR), bf16),
            pltpu.VMEM((LAYERS, PLANE, NZ, CAP, PT, PAIR), bf16),
            pltpu.VMEM((2, NZ, PLANE, CAP, PT, PAIR), bf16),
            pltpu.VMEM((PLANE * NZ * CAP, PT, PAIR), bf16),
            pltpu.VMEM((PASS_DEV, PT, PAIR), bf16),
            pltpu.VMEM((LAYERS, REQ * QT, PAIR), bf16),
            pltpu.VMEM((KEYS, PAIR), bf16),
            pltpu.VMEM((LAYERS, REQ * QT, WIDE), bf16),
            pltpu.VMEM((REQ * QT, 128), jnp.float32),
            pltpu.VMEM((LAYERS - 1, NY, 8, REQ * QT), jnp.float32),
            dma((NY, 2)),
            dma((LAYERS, 2)),
            dma((NY, 2)),
            dma((LAYERS, 2)),
            dma((4,)),
            dma((LAYERS, 2, 2, 4)),
            dma((LAYERS, 2, 2, 4)),
            dma((LAYERS,)),
            dma((LAYERS,)),
            dma((LAYERS - 1, NY)),
            dma((LAYERS - 1,)),
            dma((LAYERS,)),
            dma(()),
            dma(()),
        ],
        compiler_params=pltpu.CompilerParams(
            collective_id=1, has_side_effects=True, vmem_limit_bytes=60 * 1024 * 1024
        ),
        name="general_attend",
    )(store, own, hidden, gain, sel, slots)


def per_device(hidden, norm_gain, own_kv, passage_kv, retrieval, passage_slot):
    cache, x, y, z, c = where_am_i()
    ids = jnp.broadcast_to(jnp.tile(retrieval.reshape(-1), 4)[None, :], (8, 128))
    rows, gains, tab = greet(ids, passage_slot.reshape(8, 128), norm_gain)
    most_z, most_x = tab[34, 0], tab[35, 0]
    turn = jnp.arange(32, dtype=jnp.int32)

    def fast(cz, collective_id):
        def run(store, own, hidden, gains):
            return fast_attend(cz, collective_id, store, own, hidden, gains, tab)

        return run

    def general(store, own, hidden, gains):
        gain = lax.dynamic_slice(gains, (0, y * 8, 0), (NY, 8, 128)).reshape(NY, WIDE)
        near = lax.dynamic_slice(rows, (2 * z, 0), (2, 128)).reshape(NC, NX, 32)
        near = near.transpose(1, 0, 2).reshape(PLANE, 32)
        mine = x * NC + c
        owner = near // PASS_DEV
        inside = near % PASS_DEV
        source = (owner // (NZ * NC)) * NC + owner % NC
        plane = (owner // NC) % NZ
        earlier = (owner[:, None, :] == owner[:, :, None]) & (turn[None, :] < turn[:, None])
        rank = jnp.sum(earlier.astype(jnp.int32), axis=2)
        place = jnp.where(source == mine, plane * CAP + rank, -1)
        spots = jnp.arange(NZ * CAP, dtype=jnp.int32)
        sel = jnp.sum(
            jnp.where(place[:, None, :] == spots[None, :, None], inside[:, None, :], 0), axis=2
        )
        sel = sel.reshape(PLANE, NZ, CAP).transpose(1, 0, 2).reshape(NZ, PLANE * CAP)
        slot = (source * NZ + plane) * CAP + rank
        slots = lax.dynamic_slice(slot, (mine, 0), (1, 32)).reshape(32)
        return general_attend(store, own, hidden, gain, sel, slots)

    which = jnp.int32(0)
    for cz in CZS:
        which = which + (most_z > PLANE * cz).astype(jnp.int32)
    which = jnp.where(most_x > 2 * CX, len(CZS), which)
    branches = [fast(cz, 2 + i) for i, cz in enumerate(CZS)] + [general]
    done = lax.switch(which, branches, passage_kv[0], own_kv[0], hidden, gains)
    return done[None]


def solution(mesh):
    return jax.shard_map(
        per_device,
        mesh=mesh,
        in_specs=(
            P("cache", None),
            P("section", None),
            P("section", "cache", None),
            P("section", "cache", None, None),
            P("cache", None),
            P(),
        ),
        out_specs=P("section", "cache", None),
        check_vma=False,
    )
```
